32 devices in a mesh: dp: 4 (over z), ctx: 4 (over y, x), tensor: 2 (over core).
Axes of the slice: x: 2, y: 2, z: 4, core: 2. Of those that a mesh axis runs over, the one named last changes fastest.
Arguments:
- tokens: bfloat16 [12288, 1152], P(('dp', 'ctx')), may hold values from -6 to 6
- out_cotangent: bfloat16 [12288, 1152], P(('dp', 'ctx')), may hold values from -6 to 6
- lengths: int32 [4, 4], P('dp'), may hold values from 1 to 2688, as said below
- norm_gains: float32 [1152, 4], P(('dp', 'ctx')), may hold values from 0.5 to 1.5
- gain_first: float32 [1152, 4], P(('dp', 'ctx')), may hold values from -112 to 112
- gain_second: float32 [1152, 4], P(('dp', 'ctx')), may hold values from 1474.56 to 5775.36
- head_gains: float32 [256, 2], P(('dp', 'ctx')), may hold values from 0.5 to 1.5
- head_first: float32 [256, 2], P(('dp', 'ctx')), may hold values from -224 to 224
- head_second: float32 [256, 2], P(('dp', 'ctx')), may hold values from 5898.24 to 23101.44
- query_weight: float32 [1152, 1024], P(('dp', 'ctx'), 'tensor'), may hold values from -0.1875 to 0.1875
- query_first: float32 [1152, 1024], P(('dp', 'ctx'), 'tensor'), may hold values from -112 to 112
- query_second: float32 [1152, 1024], P(('dp', 'ctx'), 'tensor'), may hold values from 1474.56 to 5775.36
- keyval_weight: float32 [1152, 512], P(('dp', 'ctx')), may hold values from -0.1875 to 0.1875
- keyval_first: float32 [1152, 512], P(('dp', 'ctx')), may hold values from -224 to 224
- keyval_second: float32 [1152, 512], P(('dp', 'ctx')), may hold values from 5898.24 to 23101.44
- output_weight: float32 [1152, 1024], P(('dp', 'ctx'), 'tensor'), may hold values from -0.1875 to 0.1875
- output_first: float32 [1152, 1024], P(('dp', 'ctx'), 'tensor'), may hold values from -112 to 112
- output_second: float32 [1152, 1024], P(('dp', 'ctx'), 'tensor'), may hold values from 1351.68 to 5406.72
- gate_up: float32 [1152, 2, 6912], P(('dp', 'ctx'), None, 'tensor'), may hold values from -0.1875 to 0.1875
- gate_first: float32 [1152, 2, 6912], P(('dp', 'ctx'), None, 'tensor'), may hold values from -32 to 32
- gate_second: float32 [1152, 2, 6912], P(('dp', 'ctx'), None, 'tensor'), may hold values from 114.2784 to 454.656
- down_weight: float32 [1152, 6912], P(('dp', 'ctx'), 'tensor'), may hold values from -0.078125 to 0.078125
- down_first: float32 [1152, 6912], P(('dp', 'ctx'), 'tensor'), may hold values from -64 to 64
- down_second: float32 [1152, 6912], P(('dp', 'ctx'), 'tensor'), may hold values from 646.3488 to 2580.48
Outputs:
- result: bfloat16 [12288, 1152], P(('dp', 'ctx'))
- input_grad: float32 [12288, 1152], P(('dp', 'ctx'))
- gains_new: float32 [1152, 4], P(('dp', 'ctx'))
- gain_first_new: float32 [1152, 4], P(('dp', 'ctx'))
- gain_second_new: float32 [1152, 4], P(('dp', 'ctx'))
- heads_new: float32 [256, 2], P(('dp', 'ctx'))
- head_first_new: float32 [256, 2], P(('dp', 'ctx'))
- head_second_new: float32 [256, 2], P(('dp', 'ctx'))
- query_new: float32 [1152, 1024], P(('dp', 'ctx'), 'tensor')
- query_first_new: float32 [1152, 1024], P(('dp', 'ctx'), 'tensor')
- query_second_new: float32 [1152, 1024], P(('dp', 'ctx'), 'tensor')
- keyval_new: float32 [1152, 512], P(('dp', 'ctx'))
- keyval_first_new: float32 [1152, 512], P(('dp', 'ctx'))
- keyval_second_new: float32 [1152, 512], P(('dp', 'ctx'))
- output_new: float32 [1152, 1024], P(('dp', 'ctx'), 'tensor')
- output_first_new: float32 [1152, 1024], P(('dp', 'ctx'), 'tensor')
- output_second_new: float32 [1152, 1024], P(('dp', 'ctx'), 'tensor')
- gate_new: float32 [1152, 2, 6912], P(('dp', 'ctx'), None, 'tensor')
- gate_first_new: float32 [1152, 2, 6912], P(('dp', 'ctx'), None, 'tensor')
- gate_second_new: float32 [1152, 2, 6912], P(('dp', 'ctx'), None, 'tensor')
- down_new: float32 [1152, 6912], P(('dp', 'ctx'), 'tensor')
- down_first_new: float32 [1152, 6912], P(('dp', 'ctx'), 'tensor')
- down_second_new: float32 [1152, 6912], P(('dp', 'ctx'), 'tensor')
The draws below stay inside these ranges and needn't reach their ends.
Inputs may be any that keep to these rules, and one draw needn't show every extreme that they name: `lengths`: each row sums to 3072; exactly one entry of each row is 2688, the others sum to 384.
All inputs are finite; a program needn't handle non-finite values.
Results may differ from the reference program's by a relative error of at most 0.019.
The reference program's roundings to bfloat16 on the way count: a program that leaves them out, or rounds other values in their place, can miss the bound.
Values may be sent and summed in bfloat16 or wider, within the bound.
A program may use at most 256 MiB of HBM per device.

```python
import math
import jax
import jax.numpy as jnp
from jax import lax

D = 1152
HQ = 4
HD = 256
FF = 6912
WIN = 512
TOK_DEV = 768
SEQS = 4
STEP = 10
TOK_GROUP = 3072
LONGEST = 2688
TOKENS = 12288
N_DP = 4


def draw_lengths(key, part):
    key = jax.random.fold_in(key, 17)
    subkeys = jax.random.split(key, 3)
    short_total = TOK_DEV // 2
    first_short = jax.random.randint(subkeys[0], (N_DP,), 1, short_total - 1)
    second_short = jax.random.randint(subkeys[1], (N_DP,), 1, short_total - first_short)
    third_short = short_total - first_short - second_short
    shorts = jnp.stack([first_short, second_short, third_short], axis=1).astype(jnp.int32)
    long_slot = jax.random.randint(subkeys[2], (N_DP,), 0, SEQS)
    columns = []
    for column in range(SEQS):
        short_index = jnp.clip(column - (column > long_slot).astype(jnp.int32), 0, SEQS - 2)
        short_value = jnp.take_along_axis(shorts, short_index[:, None], axis=1)[:, 0]
        columns.append(jnp.where(long_slot == column, LONGEST, short_value))
    return jnp.stack(columns, axis=1).astype(jnp.int32)


def shard_levels(rng, extent, cuts, low, top_value):
    factor_of = 1.0
    for dim, blocks in cuts:
        steps = jax.random.uniform(jax.random.fold_in(jax.random.fold_in(rng, 6), dim), (blocks,), jnp.float32, low / len(cuts), top_value / len(cuts))
        factor_of = factor_of * jnp.repeat(jnp.exp(steps), extent[dim] // blocks).reshape((-1,) + (1,) * (len(extent) - 1 - dim))
    return factor_of


def normal_values(key, shape, width, limit, shards=(), held_as=jnp.bfloat16):
    entries = width * jax.random.normal(key, shape, jnp.float32)
    if shards:
        entries = entries * shard_levels(key, shape, shards, -0.22, 0.18)
    return jnp.clip(entries, -limit, limit).astype(held_as)


def setup_inputs(seed: int = 0) -> dict:
    keys = jax.random.split(jax.random.key(seed), 25)
    tokens = normal_values(keys[0], (TOKENS, D), 1.0, 6.0, ((0, 16),))
    out_cotangent = normal_values(keys[1], (TOKENS, D), 1.0, 6.0, ((0, 16),))
    lengths = draw_lengths(jax.random.fold_in(keys[24], 71), 0)
    norm_gains = jnp.clip(1.0 + 0.1 * jax.random.normal(keys[3], (D, 4), jnp.float32), 0.5, 1.5)
    gain_first = normal_values(keys[4], (D, 4), (0.17 * TOKENS ** 0.5), 112.0, ((0, 16),), jnp.float32)
    gain_second = jnp.clip(jnp.exp(math.log(5775.36) - 1.3652409 * jax.random.uniform(keys[5], (D, 4), jnp.float32) ** shard_levels(keys[5], (D, 4), ((0, 16),), -0.2, 0.2)), 1474.56, 5775.36)
    head_gains = jnp.clip(1.0 + 0.1 * jax.random.normal(keys[6], (HD, 2), jnp.float32), 0.5, 1.5)
    head_first = normal_values(keys[7], (HD, 2), (0.17 * (HQ * TOKENS) ** 0.5), 224.0, ((0, 16),), jnp.float32)
    head_second = jnp.clip(jnp.exp(math.log(23101.44) - 1.3652409 * jax.random.uniform(keys[8], (HD, 2), jnp.float32) ** shard_levels(keys[8], (HD, 2), ((0, 16),), -0.2, 0.2)), 5898.24, 23101.44)
    query_weight = normal_values(keys[9], (D, HQ * HD), D ** -0.5, 0.1875, ((0, 16), (1, 2)), jnp.float32)
    query_first = normal_values(keys[10], (D, HQ * HD), (0.17 * TOKENS ** 0.5), 112.0, ((0, 16), (1, 2)), jnp.float32)
    query_second = jnp.clip(jnp.exp(math.log(5775.36) - 1.3652409 * jax.random.uniform(keys[11], (D, HQ * HD), jnp.float32) ** shard_levels(keys[11], (D, HQ * HD), ((0, 16), (1, 2)), -0.2, 0.2)), 1474.56, 5775.36)
    keyval_weight = normal_values(keys[12], (D, 2 * HD), D ** -0.5, 0.1875, ((0, 16),), jnp.float32)
    keyval_first = normal_values(keys[13], (D, 2 * HD), (0.17 * (HQ * TOKENS) ** 0.5), 224.0, ((0, 16),), jnp.float32)
    keyval_second = jnp.clip(jnp.exp(math.log(23101.44) - 1.3652409 * jax.random.uniform(keys[14], (D, 2 * HD), jnp.float32) ** shard_levels(keys[14], (D, 2 * HD), ((0, 16),), -0.2, 0.2)), 5898.24, 23101.44)
    output_weight = normal_values(keys[15], (D, HQ * HD), (HQ * HD) ** -0.5, 0.1875, ((0, 16), (1, 2)), jnp.float32)
    output_first = normal_values(keys[16], (D, HQ * HD), (0.16 * TOKENS ** 0.5), 112.0, ((0, 16), (1, 2)), jnp.float32)
    output_second = jnp.clip(jnp.exp(math.log(5406.72) - 1.3862944 * jax.random.uniform(keys[17], (D, HQ * HD), jnp.float32) ** shard_levels(keys[17], (D, HQ * HD), ((0, 16), (1, 2)), -0.2, 0.2)), 1351.68, 5406.72)
    gate_up = normal_values(keys[18], (D, 2, FF), D ** -0.5, 0.1875, ((0, 16), (2, 2)), jnp.float32)
    gate_first = normal_values(keys[19], (D, 2, FF), (0.047 * TOKENS ** 0.5), 32.0, ((0, 16), (2, 2)), jnp.float32)
    gate_second = jnp.clip(jnp.exp(math.log(454.656) - 1.3809036 * jax.random.uniform(keys[20], (D, 2, FF), jnp.float32) ** shard_levels(keys[20], (D, 2, FF), ((0, 16), (2, 2)), -0.2, 0.2)), 114.2784, 454.656)
    down_weight = normal_values(keys[21], (D, FF), FF ** -0.5, 0.078125, ((0, 16), (1, 2)), jnp.float32)
    down_first = normal_values(keys[22], (D, FF), (0.111 * TOKENS ** 0.5), 64.0, ((0, 16), (1, 2)), jnp.float32)
    down_second = jnp.clip(jnp.exp(math.log(2580.48) - 1.3843914 * jax.random.uniform(keys[23], (D, FF), jnp.float32) ** shard_levels(keys[23], (D, FF), ((0, 16), (1, 2)), -0.2, 0.2)), 646.3488, 2580.48)
    return dict(tokens=tokens, out_cotangent=out_cotangent, lengths=lengths, norm_gains=norm_gains, gain_first=gain_first, gain_second=gain_second, head_gains=head_gains, head_first=head_first, head_second=head_second, query_weight=query_weight, query_first=query_first, query_second=query_second, keyval_weight=keyval_weight, keyval_first=keyval_first, keyval_second=keyval_second, output_weight=output_weight, output_first=output_first, output_second=output_second, gate_up=gate_up, gate_first=gate_first, gate_second=gate_second, down_weight=down_weight, down_first=down_first, down_second=down_second)


@jax.custom_vjp
def low(v):
    return lax.optimization_barrier(v.astype(jnp.bfloat16)).astype(jnp.float32)

@jax.custom_vjp
def low_back(v):
    return v

def low_keep(v):
    return (low(v), None)

def low_pass(kept, grad):
    return (grad,)

def back_keep(v):
    return (v, None)

def back_low(kept, grad):
    return (low(grad),)
low.defvjp(low_keep, low_pass)
low_back.defvjp(back_keep, back_low)
highest = lax.Precision.HIGHEST
norm_eps = 1e-06
beta_one = 0.9
beta_two = 0.95
adam_eps = 1e-08
decay_rate = 0.1
rope_base = 10000.0

def token_layout(lengths, places):
    stop_at = jnp.cumsum(lengths).astype(jnp.int32)
    start_at = (stop_at - lengths).astype(jnp.int32)
    segment = lax.optimization_barrier(jnp.sum((places[:, None] >= stop_at[None, :]).astype(jnp.int32), axis=1)).astype(jnp.int32)
    owned_by = segment[:, None] == jnp.arange(lengths.shape[0], dtype=jnp.int32)[None, :]
    seg_begin = lax.optimization_barrier(jnp.sum(jnp.where(owned_by, start_at[None, :], 0), axis=1)).astype(jnp.int32)
    return (segment, (places - seg_begin).astype(jnp.int32))

def rope_tables(position):
    half_dim = HD // 2
    exponent = jnp.arange(half_dim, dtype=jnp.float32) * (2.0 / HD)
    inverse = jnp.power(jnp.float32(rope_base), -exponent)
    angles = position.astype(jnp.float32)[:, None] * inverse[None, :]
    return (jnp.cos(angles), jnp.sin(angles))

def rotate(values, cosine_table, sine_table):
    half_dim = values.shape[-1] // 2
    lower_part = values[..., :half_dim]
    upper_part = values[..., half_dim:]
    return jnp.concatenate([lower_part * cosine_table - upper_part * sine_table, upper_part * cosine_table + lower_part * sine_table], axis=-1)

def rms_norm(values, gain_row):
    scale = lax.rsqrt(lax.optimization_barrier(jnp.mean(values * values, axis=-1, keepdims=True)) + norm_eps)
    return values * scale * gain_row

def group_block(block_in, lengths, params):
    gains_low, heads_low, query_low, keyval_low, output_low, gate_low, down_low = params
    token_count = block_in.shape[0]
    places = jnp.arange(token_count, dtype=jnp.int32)
    segment, position = token_layout(lengths, places)
    cosine_table, sine_table = rope_tables(position)
    allowed = (segment[:, None] == segment[None, :]) & (places[None, :] <= places[:, None]) & (places[:, None] - places[None, :] < WIN)
    score_scale = HD ** (-0.5)
    normed_one = low(rms_norm(block_in, gains_low[:, 0]))
    query_lin = low_back(jnp.dot(normed_one, query_low, precision=highest)).reshape(token_count, HQ, HD)
    keyval_lin = low_back(jnp.dot(normed_one, keyval_low, precision=highest))
    query_normed = rms_norm(query_lin, heads_low[:, 0])
    key_normed = rms_norm(keyval_lin[:, :HD], heads_low[:, 1])
    query_rot = low(rotate(query_normed, cosine_table[:, None, :], sine_table[:, None, :]))
    key_rot = low(rotate(key_normed, cosine_table, sine_table))
    value_low = low(keyval_lin[:, HD:])
    scores = low_back(jnp.einsum('qhd,kd->hqk', query_rot, key_rot, precision=highest) * score_scale)
    prob_values = jax.nn.softmax(jnp.where(allowed[None], scores, -1e+30), axis=-1)
    attended = low(low_back(jnp.einsum('hqk,kd->qhd', low(prob_values), value_low, precision=highest))).reshape(token_count, HQ * HD)
    branch_raw = low_back(jnp.dot(attended, output_low.T, precision=highest))
    middle = block_in + rms_norm(branch_raw, gains_low[:, 1])
    normed_two = low(rms_norm(middle, gains_low[:, 2]))
    gate_lin = low_back(jnp.einsum('td,dcf->tcf', normed_two, gate_low, precision=highest))
    hidden = low(jax.nn.gelu(gate_lin[:, 0], approximate=True) * gate_lin[:, 1])
    mlp_raw = low_back(jnp.dot(hidden, down_low.T, precision=highest))
    return middle + rms_norm(mlp_raw, gains_low[:, 3])

def adam_step(weight_value, gradient, first_moment, second_moment, step_rate, decay_factor):
    first_moment = beta_one * first_moment + (1.0 - beta_one) * gradient
    second_moment = beta_two * second_moment + (1.0 - beta_two) * gradient * gradient
    first_hat = first_moment / (1.0 - beta_one ** STEP)
    second_hat = second_moment / (1.0 - beta_two ** STEP)
    update = first_hat / (jnp.sqrt(second_hat) + adam_eps)
    return (weight_value - step_rate * (update + decay_factor * weight_value), first_moment, second_moment)

def reference(tokens, out_cotangent, lengths, norm_gains, gain_first, gain_second, head_gains, head_first, head_second, query_weight, query_first, query_second, keyval_weight, keyval_first, keyval_second, output_weight, output_first, output_second, gate_up, gate_first, gate_second, down_weight, down_first, down_second):
    masters = (norm_gains, head_gains, query_weight, keyval_weight, output_weight, gate_up, down_weight)

    def forward(inputs, params):
        lowered = tuple((low(weight_value) for weight_value in params))
        grouped = inputs.reshape(N_DP, TOK_GROUP, D)

        def scan_step(scan_carry, pieces):
            return (scan_carry, group_block(pieces[0], pieces[1], lowered))
        _, outputs = lax.scan(jax.checkpoint(scan_step), jnp.zeros((), jnp.float32), (grouped, lengths))
        return outputs.reshape(TOKENS, D)
    block_out, pullback = jax.vjp(forward, tokens.astype(jnp.float32), masters)
    input_grad, weight_grads = pullback(out_cotangent.astype(jnp.float32))
    gains_grad, heads_grad, query_grad, keyval_grad, output_grad, gate_grad, down_grad = weight_grads
    gains_new, gain_first_new, gain_second_new = adam_step(norm_gains, gains_grad, gain_first, gain_second, 0.5, 0.0)
    heads_new, head_first_new, head_second_new = adam_step(head_gains, heads_grad, head_first, head_second, 0.5, 0.0)
    query_new, query_first_new, query_second_new = adam_step(query_weight, query_grad, query_first, query_second, D ** (-0.5), decay_rate)
    keyval_new, keyval_first_new, keyval_second_new = adam_step(keyval_weight, keyval_grad, keyval_first, keyval_second, D ** (-0.5), decay_rate)
    output_new, output_first_new, output_second_new = adam_step(output_weight, output_grad, output_first, output_second, (HQ * HD) ** (-0.5), decay_rate)
    gate_new, gate_first_new, gate_second_new = adam_step(gate_up, gate_grad, gate_first, gate_second, D ** (-0.5), decay_rate)
    down_new, down_first_new, down_second_new = adam_step(down_weight, down_grad, down_first, down_second, FF ** (-0.5), decay_rate)
    return (block_out.astype(jnp.bfloat16), input_grad, gains_new, gain_first_new, gain_second_new, heads_new, head_first_new, head_second_new, query_new, query_first_new, query_second_new, keyval_new, keyval_first_new, keyval_second_new, output_new, output_first_new, output_second_new, gate_new, gate_first_new, gate_second_new, down_new, down_first_new, down_second_new)
```

```python
import functools

import jax
import jax.numpy as jnp
import numpy as np
from jax import lax
from jax.experimental import pallas as pl
from jax.experimental.pallas import tpu as pltpu
from jax.sharding import PartitionSpec as P

D = 1152
HQ = 4
HD = 256
FF = 6912
WIN = 512
STEP = 10


norm_eps = 1e-06
beta_one = 0.9
beta_two = 0.95
adam_eps = 1e-08
decay_rate = 0.1
rope_base = 10000.0
GELU_SCALE = float(np.sqrt(2.0 / np.pi))
MESH = pl.DeviceIdType.MESH


def from_behind(block, axis, distance):
    devices = range(lax.axis_size(axis))
    route = [(i - distance, i) for i in devices if i - distance in devices]
    return lax.ppermute(block, axis, route)


def from_partner(block, axis, bits):
    return lax.ppermute(block, axis, [(i ^ bits, i) for i in range(lax.axis_size(axis))])


def along_line(tiles, axis):
    n = lax.axis_size(axis)
    if n > 4:
        return lax.all_to_all(tiles, axis, split_axis=0, concat_axis=0, tiled=True)
    place = lax.axis_index(axis)
    arrived = [lax.dynamic_index_in_dim(tiles, place, 0, keepdims=False)]
    for shift in range(1, n):
        tile = lax.dynamic_index_in_dim(tiles, lax.rem(place + shift, n), 0, keepdims=False)
        arrived.append(lax.ppermute(tile, axis, [(i, (i + shift) % n) for i in range(n)]))
    return jnp.stack(arrived)


def core_ordered(own, other):
    first = lax.axis_index("tensor") == 0
    return jnp.concatenate([jnp.where(first, own, other), jnp.where(first, other, own)], axis=0)


def half_of(array, dim):
    size = array.shape[dim] // 2
    return lax.dynamic_slice_in_dim(array, lax.axis_index("tensor") * size, size, axis=dim)


def half_not_of(array, dim):
    size = array.shape[dim] // 2
    return lax.dynamic_slice_in_dim(array, (1 - lax.axis_index("tensor")) * size, size, axis=dim)


def token_layout(lengths, places):
    stop_at = jnp.cumsum(lengths)
    start_at = stop_at - lengths
    segment = jnp.sum((places[:, None] >= stop_at[None, :]).astype(jnp.int32), axis=1)
    owned_by = segment[:, None] == jnp.arange(lengths.shape[0], dtype=jnp.int32)[None, :]
    seg_begin = jnp.sum(jnp.where(owned_by, start_at[None, :], 0), axis=1)
    return (segment, places - seg_begin)


def rope_tables(position):
    half_dim = HD // 2
    exponent = jnp.arange(half_dim, dtype=jnp.float32) * (2.0 / HD)
    inverse = jnp.power(jnp.float32(rope_base), -exponent)
    angles = position.astype(jnp.float32)[:, None] * inverse[None, :]
    return (jnp.cos(angles), jnp.sin(angles))


def rotate(values, cosine_table, sine_table):
    half_dim = values.shape[-1] // 2
    lower_part = values[..., :half_dim]
    upper_part = values[..., half_dim:]
    return jnp.concatenate(
        [
            lower_part * cosine_table - upper_part * sine_table,
            upper_part * cosine_table + lower_part * sine_table,
        ],
        axis=-1,
    )


def rms_norm(values, gain_row):
    scale = lax.rsqrt(jnp.mean(values * values, axis=-1, keepdims=True) + norm_eps)
    return values * scale * gain_row


def contract_rows(left_side, right_side):
    return lax.dot_general(
        left_side, right_side, (((0,), (0,)), ((), ())), preferred_element_type=jnp.float32
    )


def contract_columns(left_side, right_side):
    return lax.dot_general(
        left_side, right_side, (((1,), (1,)), ((), ())), preferred_element_type=jnp.float32
    )


def adam_step(weight_value, gradient, first_moment, second_moment, step_rate, decay_factor):
    first_moment = beta_one * first_moment + (1.0 - beta_one) * gradient
    second_moment = beta_two * second_moment + (1.0 - beta_two) * gradient * gradient
    first_hat = first_moment / (1.0 - beta_one**STEP)
    second_hat = second_moment / (1.0 - beta_two**STEP)
    update = first_hat / (jnp.sqrt(second_hat) + adam_eps)
    return (
        weight_value - step_rate * (update + decay_factor * weight_value),
        first_moment,
        second_moment,
    )


def places():
    return lax.axis_index("dp"), lax.axis_index("ctx"), lax.axis_index("tensor")


def plane_partners():
    dp, ctx, core = places()
    beside = ctx + 1 - 2 * lax.rem(ctx, 2)
    across = lax.rem(ctx + 2, 4)
    return (dp, beside, core), (dp, across, core), (dp, 3 - ctx, core), (dp, ctx, 1 - core)


def enter(n_dp, line):
    dp, ctx, core = places()
    barrier = pltpu.get_barrier_semaphore()

    def greet(device):
        pl.semaphore_signal(barrier, inc=1, device_id=device, device_id_type=MESH)

    for device in plane_partners():
        greet(device)
    if line:
        pl.when(dp < n_dp - 1)(lambda: greet((dp + 1, ctx, core)))
        pl.when(dp > 0)(lambda: greet((dp - 1, ctx, core)))
    ends = jnp.minimum(dp, 1) + jnp.minimum(n_dp - 1 - dp, 1) if line else 0
    pl.semaphore_wait(barrier, 4 + ends)


def in_columns(count, body):
    whole = count // 256

    def one(i, carry):
        body(pl.multiple_of(i * 256, 256), 256)
        return carry

    lax.fori_loop(0, whole, one, 0)
    if count % 256:
        body(whole * 256, count % 256)


def in_rows(count, body, start):
    size = 64

    def one(i, carry):
        return body(pl.multiple_of(i * size, size), size, carry)

    return lax.fori_loop(0, count // size, one, start)


def turned(values, cosine, sine):
    half_dim = values.shape[-1] // 2
    lower, upper = values[:, :half_dim], values[:, half_dim:]
    return jnp.concatenate([lower * cosine - upper * sine, upper * cosine + lower * sine], axis=1)


def scale_of(values):
    return lax.rsqrt(jnp.mean(values * values, axis=1, keepdims=True) + norm_eps)


def attend_kernel(
    n_dp,
    owned_heads,
    tokens,
    cosine,
    sine,
    lowest,
    attn_pack,
    mlp_pack,
    mlp_full,
    attn_full,
    gain_rows,
    head_rows,
    normed_out,
    lin,
    query_out,
    keyval_out,
    attended,
    log_total,
    branch_out,
    middle_out,
    normed_two,
    slots,
    wide_slots,
    keyval,
    partial,
    core_send,
    core_take,
    own_sem,
    mlp_plane_send,
    mlp_plane_recv,
    mlp_line_send,
    mlp_line_recv,
    attn_line_send,
    attn_line_recv,
    attn_plane_send,
    attn_plane_recv,
    keyval_send,
    keyval_recv,
):
    dp, ctx, core = places()
    x_dev, y_dev, far_dev, core_dev = plane_partners()
    plane = ((dp, ctx, core), x_dev, y_dev, far_dev)
    f32, bf16 = jnp.float32, jnp.bfloat16
    row_count, width = tokens.shape
    half = row_count // 2
    owned = attn_pack.shape[0]
    behind = keyval.shape[1] - row_count
    next_dev = (dp, ctx + 1, core)
    enter(n_dp, True)

    def remote(source, target, send, recv, device):
        return pltpu.make_async_remote_copy(
            src_ref=source, dst_ref=target, send_sem=send, recv_sem=recv, device_id=device,
            device_id_type=MESH,
        )

    def line_block(way, step, k):
        origin = dp - step if way == 0 else dp + step
        return origin * 4 + plane[k][1]

    def can_take(way, step):
        return dp >= step if way == 0 else dp <= n_dp - 1 - step

    def can_give(way):
        return dp < n_dp - 1 if way == 0 else dp > 0

    def line_dev(way):
        return (dp + 1, ctx, core) if way == 0 else (dp - 1, ctx, core)

    def mlp_hop(way, step, k):
        block = mlp_full.at[line_block(way, step, k)]
        index = (way * n_dp + step) * 4 + k
        return remote(block, block, mlp_line_send.at[index], mlp_line_recv.at[index], line_dev(way))

    def mlp_came(way, step, k):
        block = mlp_full.at[line_block(way, step, k)]
        index = (way * n_dp + step - 1) * 4 + k
        return remote(block, block, mlp_line_send.at[index], mlp_line_recv.at[index], line_dev(way))

    def attn_hop(way, step):
        block = slots.at[line_block(way, step, 0)]
        index = way * n_dp + step
        return remote(block, block, attn_line_send.at[index], attn_line_recv.at[index], line_dev(way))

    def attn_came(way, step):
        block = slots.at[line_block(way, step, 0)]
        index = way * n_dp + step - 1
        return remote(block, block, attn_line_send.at[index], attn_line_recv.at[index], line_dev(way))

    def each(step, act, give):
        for way in range(2):
            if give:
                fits = can_give(way) & can_take(way, step) if step else can_give(way)
            else:
                fits = can_take(way, step)
            pl.when(fits)(functools.partial(act, way))

    def attn_plane(way, step, side, came=False):
        from_k = {1: 0, 2: 0, 3: 1 if step % 2 == 0 else 2}[side]
        device = {1: x_dev, 2: y_dev, 3: y_dev if step % 2 == 0 else x_dev}[side]
        block = slots.at[line_block(way, step, side if came else from_k)]
        index = (way * n_dp + step) * 4 + side
        return remote(block, block, attn_plane_send.at[index], attn_plane_recv.at[index], device)

    own_attn = pltpu.make_async_copy(attn_pack, slots.at[dp * 4 + ctx], own_sem.at[0])
    own_mlp = pltpu.make_async_copy(mlp_pack.at[ctx], mlp_full.at[dp * 4 + ctx], own_sem.at[1])
    own_attn.start()
    own_mlp.start()
    own_attn.wait()
    each(0, lambda way: attn_hop(way, 0).start(), True)
    for side in (1, 2):
        attn_plane(0, 0, side).start()
    own_mlp.wait()
    each(0, lambda way: mlp_hop(way, 0, 0).start(), True)

    def mlp_plane(k, came=False):
        return remote(
            mlp_pack.at[plane[k][1]],
            mlp_full.at[dp * 4 + (plane[k][1] if came else ctx)],
            mlp_plane_send.at[k],
            mlp_plane_recv.at[k],
            plane[k],
        )

    for k in (1, 2, 3):
        mlp_plane(k).start()

    def came(way, step):
        attn_came(way, step).wait_recv()

    def hand_on(way, step):
        for side in (1, 2):
            attn_plane(way, step, side).start()

    for step in range(1, n_dp):
        each(step, lambda way: came(way, step), False)
        each(step, lambda way: attn_hop(way, step).start(), True)
        each(step, lambda way: hand_on(way, step), False)
    order = [(0, 0)] + [(way, step) for step in range(1, n_dp) for way in range(2)]

    def relay(way, step):
        for side in (1, 2):
            attn_plane(way, step, side, True).wait_recv()
        attn_plane(way, step, 3).start()

    def relayed(way, step):
        attn_plane(way, step, 3, True).wait_recv()

    def where_held(way, step, act):
        if step:
            pl.when(can_take(way, step))(lambda: act(way, step))
        else:
            act(way, step)

    for way, step in order:
        where_held(way, step, relay)

    def mlp_first(k):
        mlp_plane(k, True).wait_recv()
        each(0, lambda way: mlp_hop(way, 0, k).start(), True)

    def mlp_next(step, k):
        each(step, lambda way: mlp_came(way, step, k).wait_recv(), False)
        if step < n_dp - 1:
            each(step, lambda way: mlp_hop(way, step, k).start(), True)

    events = [functools.partial(mlp_first, k) for k in (1, 2, 3)] + [
        functools.partial(mlp_next, step, k) for step in range(1, n_dp) for k in range(4)
    ]
    events.reverse()

    def move(count):
        for _ in range(min(count, len(events))):
            events.pop()()

    move(2)
    for way, step in order:
        where_held(way, step, relayed)
    move(2)

    for block in range(n_dp * 4):
        wide_slots[block * owned : (block + 1) * owned, :] = slots[block].astype(f32)

    def narrow(first, size, carry):
        at = pl.ds(first, size)
        attn_full[at] = wide_slots[at].astype(bf16)
        return carry

    in_rows(width, narrow, 0)
    pick = lax.broadcasted_iota(jnp.int32, (8, 128), 0) == lax.broadcasted_iota(
        jnp.int32, (8, 128), 1
    )
    small = contract_columns(pick.astype(f32).astype(bf16), attn_full[:, 1280:1408])
    gain_rows[...] = small
    row_of = lax.broadcasted_iota(jnp.int32, (width, HD), 0)
    head_of = lax.broadcasted_iota(jnp.int32, (width, HD), 1)
    shift = owned_heads.bit_length() - 1
    chosen = row_of == (head_of >> shift) * owned + (head_of & (owned_heads - 1))
    heads = jnp.dot(
        small.astype(bf16), chosen.astype(f32).astype(bf16), preferred_element_type=f32
    )
    head_rows[...] = heads

    def normalize(first, size, carry):
        at = pl.ds(first, size)
        values = tokens[at].astype(f32)
        normed_out[at] = (values * scale_of(values) * gain_rows[0:1]).astype(bf16)
        return carry

    in_rows(row_count, normalize, 0)

    def project(start, size):
        lin[:, pl.ds(start, size)] = jnp.dot(
            normed_out[...], attn_full[:, pl.ds(start, size)], preferred_element_type=f32
        )

    in_columns(3 * HD, project)
    move(1)

    def turn_keyval(first, size, carry):
        at = pl.ds(first, size)
        values = lin[at, 2 * HD : 3 * HD]
        keys = turned(values * scale_of(values) * head_rows[5:6], cosine[at], sine[at])
        mine = jnp.where(core == 0, keys, values).astype(bf16)
        keyval[core, pl.ds(pl.multiple_of(first + behind, 64), size)] = mine
        return carry

    in_rows(row_count, turn_keyval, 0)
    own_rows, last_rows = pl.ds(behind, row_count), pl.ds(row_count, behind)
    past_rows = pl.ds(0, behind)

    def to_core(came=False):
        block = keyval.at[1 - core if came else core, own_rows]
        return remote(block, block, keyval_send.at[0], keyval_recv.at[0], core_dev)

    def past_to_core(came=False):
        block = keyval.at[1 - core if came else core, past_rows]
        return remote(block, block, keyval_send.at[2], keyval_recv.at[2], core_dev)

    to_next = remote(
        keyval.at[core, last_rows],
        keyval.at[core, past_rows],
        keyval_send.at[1],
        keyval_recv.at[1],
        next_dev,
    )
    pl.when(ctx < 3)(to_next.start)
    to_core().start()

    def turn_query(first, size, carry):
        at = pl.ds(first, size)
        for head in range(2):
            values = lin[at, head * HD : (head + 1) * HD]
            normal = values * scale_of(values) * head_rows[4:5]
            query_out[head, at] = turned(normal, cosine[at], sine[at]).astype(bf16)
        return carry

    in_rows(row_count, turn_query, 0)

    @pl.when(ctx > 0)
    def _():
        to_next.wait_recv()
        past_to_core().start()
        past_to_core(True).wait_recv()

    @pl.when(ctx == 0)
    def _():
        keyval[:, 0:behind] = jnp.zeros((2, behind, HD), bf16)

    to_core(True).wait_recv()
    move(2)

    block_rows = 256
    reach = block_rows + behind

    def attend(first, head):
        at = pl.ds(first, block_rows)
        near = pl.ds(first, reach)
        scores = contract_columns(query_out[head, at], keyval[0, near]) * HD ** (-0.5)
        key_at = first + lax.broadcasted_iota(jnp.int32, (block_rows, reach), 1)
        query_at = first + behind + lax.broadcasted_iota(jnp.int32, (block_rows, reach), 0)
        scores = jnp.where((key_at >= lowest[at]) & (key_at <= query_at), scores, -1e30)
        row_max = jnp.max(scores, axis=1, keepdims=True)
        values = jnp.exp(scores - row_max)
        row_total = jnp.sum(values, axis=1, keepdims=True)
        probs = (values / row_total).astype(bf16)
        log_total[head, at] = row_max + jnp.log(row_total)
        out = jnp.dot(probs, keyval[1, near], preferred_element_type=f32)
        attended[at, head * HD : (head + 1) * HD] = out.astype(bf16)

    for block in range(row_count // block_rows):
        for head in range(2):
            attend(block * block_rows, head)
        move(1)

    def outward(start, size):
        partial[:, pl.ds(start, size)] = contract_columns(
            attended[...], attn_full[pl.ds(start, size), 3 * HD : 5 * HD]
        )

    in_columns(width, outward)

    def give_half(first, size, carry):
        at = pl.ds(pl.multiple_of((1 - core) * half + first, 64), size)
        core_send[pl.ds(first, size)] = partial[at].astype(bf16)
        return carry

    in_rows(half, give_half, 0)
    exchange = remote(core_send, core_take, keyval_send.at[3], keyval_recv.at[3], core_dev)
    exchange.start()
    exchange.wait_recv()

    def finish(first, size, carry):
        at = pl.ds(first, size)
        whole_at = pl.ds(pl.multiple_of(core * half + first, 64), size)
        branch = partial[whole_at] + core_take[at].astype(f32)
        branch_out[at] = branch
        middle = tokens[whole_at].astype(f32) + branch * scale_of(branch) * gain_rows[1:2]
        middle_out[at] = middle
        normed_two[at] = (middle * scale_of(middle) * gain_rows[2:3]).astype(bf16)
        return carry

    in_rows(half, finish, 0)
    keyval_out[...] = keyval[...]
    move(len(events))

    exchange.wait_send()
    to_core().wait_send()
    pl.when(ctx < 3)(to_next.wait_send)
    pl.when(ctx > 0)(past_to_core().wait_send)
    for k in (1, 2, 3):
        mlp_plane(k).wait_send()
    for step in range(n_dp - 1):
        each(step, lambda way: attn_hop(way, step).wait_send(), True)
        for k in range(4):
            each(step, lambda way: mlp_hop(way, step, k).wait_send(), True)

    def left(way, step):
        for side in (1, 2, 3):
            attn_plane(way, step, side).wait_send()

    for way, step in order:
        where_held(way, step, left)


def attend_call(n_dp, owned_heads, behind, tokens, cosine, sine, lowest, attn_pack, mlp_pack):
    row_count, width = tokens.shape
    half = row_count // 2
    owned, attn_cols = attn_pack.shape
    blocks = n_dp * 4
    f32, bf16 = jnp.float32, jnp.bfloat16
    vmem = pl.BlockSpec(memory_space=pltpu.VMEM)
    anywhere = pl.BlockSpec(memory_space=pl.ANY)

    def array(dtype, *shape):
        return jax.ShapeDtypeStruct(shape, dtype)

    dma = pltpu.SemaphoreType.DMA
    return pl.pallas_call(
        functools.partial(attend_kernel, n_dp, owned_heads),
        out_shape=(
            array(bf16, blocks, owned, mlp_pack.shape[2]),
            array(bf16, width, attn_cols),
            array(f32, 8, width),
            array(f32, 8, HD),
            array(bf16, row_count, width),
            array(f32, row_count, 3 * HD),
            array(bf16, 2, row_count, HD),
            array(bf16, 2, behind + row_count, HD),
            array(bf16, row_count, 2 * HD),
            array(f32, 2, row_count, 1),
            array(f32, half, width),
            array(f32, half, width),
            array(bf16, half, width),
        ),
        in_specs=[vmem] * 4 + [anywhere] * 2,
        out_specs=(anywhere,) + (vmem,) * 12,
        scratch_shapes=[
            pltpu.VMEM((blocks, owned, attn_cols), bf16),
            pltpu.VMEM((width, attn_cols), f32),
            pltpu.VMEM((2, behind + row_count, HD), bf16),
            pltpu.VMEM((row_count, width), f32),
            pltpu.VMEM((half, width), bf16),
            pltpu.VMEM((half, width), bf16),
            dma((2,)),
            dma((4,)),
            dma((4,)),
            dma((8 * n_dp,)),
            dma((8 * n_dp,)),
            dma((2 * n_dp,)),
            dma((2 * n_dp,)),
            dma((8 * n_dp,)),
            dma((8 * n_dp,)),
            dma((4,)),
            dma((4,)),
        ],
        compiler_params=pltpu.CompilerParams(
            collective_id=1, has_side_effects=True, vmem_limit_bytes=60 * 2**20
        ),
        cost_estimate=pl.CostEstimate(
            flops=4 * 10**9, bytes_accessed=30 * 2**20, transcendentals=2 * 10**6
        ),
        name="attend",
    )(tokens, cosine, sine, lowest, attn_pack, mlp_pack)


def mlp_kernel(
    normed,
    middle,
    cotangent,
    gain,
    weights,
    result,
    back_sum,
    gain_sum,
    rows_out,
    grads_out,
    hidden_out,
    gate_out,
    rows,
    grads,
    hidden,
    pair,
    total,
    waiting,
    core_send,
    core_take,
    plane_send,
    plane_take,
    send_sem,
    recv_sem,
    out_sem,
):
    half = normed.shape[0]
    h = half // 2
    width = normed.shape[1]
    hid = hidden.shape[2]
    step_rows = 2 * half
    part_a, part_b = pl.ds(0, h), pl.ds(h, h)
    x_dev, y_dev, _, core_dev = plane_partners()
    f32, bf16 = jnp.float32, jnp.bfloat16

    enter(1, False)

    def remote(source, target, index, device):
        return pltpu.make_async_remote_copy(
            src_ref=source,
            dst_ref=target,
            send_sem=send_sem.at[index],
            recv_sem=recv_sem.at[index],
            device_id=device,
            device_id_type=MESH,
        )

    def gather_copies(buffer, base):
        def piece(step, side):
            return buffer.at[step, 0, side]

        return [
            remote(piece(0, part_a), piece(1, part_a), base, x_dev),
            remote(piece(0, part_b), piece(1, part_b), base + 1, y_dev),
            remote(piece(0, part_b), piece(2, part_b), base + 2, x_dev),
            remote(piece(0, part_a), piece(2, part_a), base + 3, y_dev),
            remote(piece(1, part_a), piece(3, part_a), base + 4, y_dev),
            remote(piece(1, part_b), piece(3, part_b), base + 5, x_dev),
        ] + [
            remote(buffer.at[step, 0], buffer.at[step, 1], base + 6 + step, core_dev)
            for step in range(4)
        ]

    def scatter_copies(base):
        return [
            remote(plane_send.at[0, part_a], plane_take.at[0, part_a], base, y_dev),
            remote(plane_send.at[0, part_b], plane_take.at[0, part_b], base + 1, x_dev),
            remote(plane_send.at[1, part_a], plane_take.at[1, part_a], base + 2, y_dev),
            remote(plane_send.at[1, part_b], plane_take.at[1, part_b], base + 3, x_dev),
            remote(plane_send.at[2, part_a], plane_take.at[2, part_a], base + 4, x_dev),
            remote(plane_send.at[2, part_b], plane_take.at[2, part_b], base + 5, y_dev),
        ] + [
            remote(core_send.at[step % 2], core_take.at[step], base + 6 + step, core_dev)
            for step in range(4)
        ]

    def out_copy(buffer, target, step, index):
        return pltpu.make_async_copy(
            buffer.at[step],
            target.at[step],
            out_sem.at[index * 4 + step],
        )

    def gather_step(copies, step):
        if step == 0:
            for copy in copies[:4]:
                copy.start()
        elif step == 1:
            copies[0].wait_recv()
            copies[1].wait_recv()
            copies[4].start()
            copies[5].start()
        else:
            copies[2 * step - 2].wait_recv()
            copies[2 * step - 1].wait_recv()
        copies[6 + step].start()
        copies[6 + step].wait_recv()

    def scatter_step(copies, step, left, first):
        kept = (total, waiting, back_sum, back_sum)[step]
        slot = core_send.at[step % 2]
        if step >= 2:
            copies[6 + step - 2].wait_send()

        def body(start, size):
            product = contract_columns(
                left[step], weights[pl.ds(start, size), first : first + left.shape[2]]
            )
            kept[:, pl.ds(start, size)] = product[:half]
            slot[:, pl.ds(start, size)] = product[half:].astype(bf16)

        in_columns(width, body)
        copies[6 + step].start()
        copies[6 + step].wait_recv()
        summed = kept[...] + core_take[step].astype(f32)
        if step < 2:
            kept[...] = summed
        else:
            plane_send[step - 2] = summed.astype(bf16)
            copies[2 * step - 4].start()
            copies[2 * step - 3].start()

    def scatter_end(copies):
        copies[2].wait_recv()
        copies[3].wait_recv()
        plane_send[2] = (waiting[...] + plane_take[1].astype(f32)).astype(bf16)
        copies[4].start()
        copies[5].start()

    def scatter_total(at):
        return total[at] + plane_take[0, at].astype(f32) + plane_take[2, at].astype(f32)

    def scatter_wait(copies):
        for index in (0, 1, 4, 5):
            copies[index].wait_recv()

    def sent(copies):
        for copy in copies:
            copy.wait_send()

    rows[0, 0] = normed[...]
    gather = gather_copies(rows, 0)
    scatter = scatter_copies(10)
    for step in range(4):
        gather_step(gather, step)
        out_copy(rows, rows_out, step, 0).start()

        def activate(j, carry):
            at = pl.multiple_of(j * 256, 256)
            lin = jnp.dot(
                rows[step].reshape(step_rows, width),
                weights[:, pl.ds(at, 256)],
                preferred_element_type=f32,
            )
            gate, up = lin[:, :128], lin[:, 128:]
            square = gate * gate
            curve = jnp.tanh(GELU_SCALE * gate * (1.0 + 0.044715 * square))
            gelu = 0.5 * gate * (1.0 + curve)
            slope = 0.5 * (1.0 + curve) + 0.5 * GELU_SCALE * gate * (1.0 - curve * curve) * (
                1.0 + 3 * 0.044715 * square
            )
            at_half = pl.multiple_of(j * 128, 128)
            hidden[step, :, pl.ds(at_half, 128)] = (gelu * up).astype(bf16)
            pair[step, :, pl.ds(at, 128)] = (slope * up).astype(bf16)
            pair[step, :, pl.ds(pl.multiple_of(at + 128, 128), 128)] = gelu.astype(bf16)
            return carry

        lax.fori_loop(0, hid // 128, activate, 0)
        out_copy(hidden, hidden_out, step, 1).start()
        scatter_step(scatter, step, hidden, 2 * hid)
    scatter_end(scatter)
    sent(gather)
    scatter_wait(scatter)
    sent(scatter[:6] + scatter[8:])

    def norm_rows(first, size, gain_total):
        at = pl.ds(first, size)
        raw = scatter_total(at)
        scale = lax.rsqrt(jnp.mean(raw * raw, axis=1, keepdims=True) + norm_eps)
        normal = raw * scale
        result[at] = (middle[at] + normal * gain[...]).astype(bf16)
        cotangents = cotangent[at].astype(f32)
        scaled = cotangents * gain[...]
        inner = jnp.mean(raw * scaled, axis=1, keepdims=True)
        back = scale * scaled - raw * (scale * scale * scale * inner)
        grads[0, 0, at] = back.astype(bf16)
        return gain_total + jnp.sum(cotangents * normal, axis=0, keepdims=True)

    gain_sum[...] = in_rows(half, norm_rows, jnp.zeros((1, width), f32))

    gather = gather_copies(grads, 20)
    scatter = scatter_copies(30)
    for step in range(4):
        gather_step(gather, step)
        out_copy(grads, grads_out, step, 2).start()

        def unfold(start, size):
            hidden_grad = jnp.dot(
                grads[step].reshape(step_rows, width),
                weights[:, pl.ds(pl.multiple_of(2 * hid + start, 128), size)],
                preferred_element_type=f32,
            )
            for tile in range(size // 128):
                piece = hidden_grad[:, tile * 128 : (tile + 1) * 128]
                for side in range(2):
                    at = pl.ds(pl.multiple_of(2 * start + (2 * tile + side) * 128, 128), 128)
                    pair[step, :, at] = (pair[step, :, at].astype(f32) * piece).astype(bf16)

        in_columns(hid, unfold)
        out_copy(pair, gate_out, step, 3).start()
        scatter_step(scatter, step, pair, 0)
    scatter_end(scatter)
    sent(gather)
    scatter_wait(scatter)

    def finish_rows(first, size, carry):
        at = pl.ds(first, size)
        back_sum[at] = scatter_total(at)
        return carry

    in_rows(half, finish_rows, 0)
    sent(scatter[:6] + scatter[8:])
    for step in range(4):
        for index, (buffer, target) in enumerate(
            ((rows, rows_out), (hidden, hidden_out), (grads, grads_out), (pair, gate_out))
        ):
            out_copy(buffer, target, step, index).wait()


def mlp_call(normed, middle, cotangent, gain, weights):
    half, width = normed.shape
    hid = weights.shape[1] // 3
    count = 8 * half
    f32, bf16 = jnp.float32, jnp.bfloat16
    vmem = pl.BlockSpec(memory_space=pltpu.VMEM)
    anywhere = pl.BlockSpec(memory_space=pl.ANY)
    outs = pl.pallas_call(
        mlp_kernel,
        out_shape=(
            jax.ShapeDtypeStruct((half, width), bf16),
            jax.ShapeDtypeStruct((half, width), f32),
            jax.ShapeDtypeStruct((1, width), f32),
            jax.ShapeDtypeStruct((4, 2, half, width), bf16),
            jax.ShapeDtypeStruct((4, 2, half, width), bf16),
            jax.ShapeDtypeStruct((4, 2 * half, hid), bf16),
            jax.ShapeDtypeStruct((4, 2 * half, 2 * hid), bf16),
        ),
        in_specs=[vmem] * 5,
        out_specs=(vmem, vmem, vmem, anywhere, anywhere, anywhere, anywhere),
        scratch_shapes=[
            pltpu.VMEM((4, 2, half, width), bf16),
            pltpu.VMEM((4, 2, half, width), bf16),
            pltpu.VMEM((4, 2 * half, hid), bf16),
            pltpu.VMEM((4, 2 * half, 2 * hid), bf16),
            pltpu.VMEM((half, width), f32),
            pltpu.VMEM((half, width), f32),
            pltpu.VMEM((2, half, width), bf16),
            pltpu.VMEM((4, half, width), bf16),
            pltpu.VMEM((3, half, width), bf16),
            pltpu.VMEM((3, half, width), bf16),
            pltpu.SemaphoreType.DMA((40,)),
            pltpu.SemaphoreType.DMA((40,)),
            pltpu.SemaphoreType.DMA((16,)),
        ],
        compiler_params=pltpu.CompilerParams(
            collective_id=0, has_side_effects=True, vmem_limit_bytes=62 * 2**20
        ),
        cost_estimate=pl.CostEstimate(
            flops=2 * count * width * hid * 6, bytes_accessed=60 * 2**20, transcendentals=count * hid
        ),
        name="feed_forward",
    )(normed, middle, cotangent, gain, weights)
    return outs[:3] + tuple(array.reshape(count, array.shape[-1]) for array in outs[3:])


def on_device(
    tokens,
    out_cotangent,
    lengths,
    norm_gains,
    gain_first,
    gain_second,
    head_gains,
    head_first,
    head_second,
    query_weight,
    query_first,
    query_second,
    keyval_weight,
    keyval_first,
    keyval_second,
    output_weight,
    output_first,
    output_second,
    gate_up,
    gate_first,
    gate_second,
    down_weight,
    down_first,
    down_second,
):
    bf16, f32 = jnp.bfloat16, jnp.float32
    row_count = tokens.shape[0]
    owned = query_weight.shape[0]
    owned_heads = head_gains.shape[0]
    n_dp, n_ctx = lax.axis_size("dp"), lax.axis_size("ctx")
    half_ff = gate_up.shape[2]
    wide = -(-half_ff // (n_ctx * 128)) * 128
    behind = WIN
    ctx_place = lax.axis_index("ctx")
    core_first = lax.axis_index("tensor") == 0
    score_scale = HD ** (-0.5)

    head_columns = jnp.pad(head_gains, ((0, owned - owned_heads), (0, 0)))
    small = jnp.concatenate([norm_gains, head_columns], axis=1).astype(bf16)
    attn_pack = jnp.concatenate(
        [
            query_weight.astype(bf16),
            half_of(keyval_weight, 1).astype(bf16),
            output_weight.astype(bf16),
            jnp.pad(small, ((0, 0), (0, 122))),
        ],
        axis=1,
    )
    cols = query_weight.shape[1]

    def in_parts(array):
        padded = jnp.pad(array.astype(bf16), ((0, 0), (0, n_ctx * wide - half_ff)))
        return padded.reshape(owned, n_ctx, wide // 128, 128)

    gate_parts = jnp.stack([in_parts(gate_up[:, side]) for side in range(2)], axis=3)
    mlp_pack = jnp.concatenate(
        [
            gate_parts.reshape(owned, n_ctx, 2 * wide),
            in_parts(down_weight).reshape(owned, n_ctx, wide),
        ],
        axis=2,
    )
    mlp_pack = jnp.moveaxis(mlp_pack, 1, 0)

    start_row = ctx_place * row_count
    row_index = jnp.arange(row_count, dtype=jnp.int32)
    query_position = token_layout(lengths[0], start_row + row_index)[1]
    query_cosine, query_sine = rope_tables(query_position)
    lowest = jnp.maximum(row_index - query_position + behind, row_index + 1)[:, None]
    (
        mlp_full,
        attn_full,
        gain_rows,
        head_rows,
        normed_one,
        lin,
        query_rot,
        keyval_all,
        attended_low,
        log_total,
        branch_raw,
        middle,
        normed_two_half,
    ) = attend_call(
        n_dp, owned_heads, behind, tokens, query_cosine, query_sine, lowest, attn_pack, mlp_pack
    )
    key_count = behind + row_count
    head_count = cols // HD
    full_query = attn_full[:, :cols]
    half_keyval = attn_full[:, cols : cols + HD]
    full_output = attn_full[:, cols + HD : 2 * cols + HD]
    query_norm_back = jax.vjp(
        rms_norm, lin[:, :cols].reshape(row_count, head_count, HD), head_rows[4]
    )[1]
    key_norm_back = jax.vjp(rms_norm, lin[:, cols:], head_rows[5])[1]
    key_all, value_all = keyval_all[0], keyval_all[1]
    post_one_back = jax.vjp(rms_norm, branch_raw, gain_rows[1])[1]
    norm_two_back = jax.vjp(rms_norm, middle, gain_rows[2])[1]
    inputs_half = half_of(tokens, 0).astype(f32)
    key_index = jnp.arange(key_count, dtype=jnp.int32)[None, :]
    allowed = (key_index >= lowest) & (key_index <= row_index[:, None] + behind)

    def core_summed(partial):
        arrived = from_partner(half_not_of(partial, 0).astype(bf16), "tensor", 1)
        return half_of(partial, 0) + arrived.astype(f32)

    cotangent_half = half_of(out_cotangent, 0)
    (
        result_half,
        normed_two_grad,
        gain_three_part,
        normed_two,
        mlp_raw_low,
        hidden_low,
        gate_grad,
    ) = mlp_call(
        normed_two_half,
        middle,
        cotangent_half,
        gain_rows[3:4],
        mlp_full.reshape(n_dp * n_ctx * owned, 3 * wide),
    )
    gain_three_grad = gain_three_part[0]
    cotangent_half = cotangent_half.astype(f32)
    result = core_ordered(result_half, from_partner(result_half, "tensor", 1))
    def exchanged(tiles):
        return lax.all_to_all(tiles, ("dp", "ctx"), split_axis=0, concat_axis=0, tiled=True)

    def to_owners(term):
        arrived = exchanged(term.astype(bf16).reshape(n_dp * n_ctx, owned, term.shape[1]))
        return arrived.reshape(n_dp, n_ctx, owned, term.shape[1]).astype(f32).sum(axis=0)

    def from_parts(tiles):
        return jnp.moveaxis(tiles, 0, 1).reshape(owned, n_ctx * wide)[:, :half_ff]

    down_reduced = from_parts(to_owners(contract_rows(mlp_raw_low, hidden_low)))
    gate_arrived = to_owners(contract_rows(normed_two, gate_grad))
    gate_arrived = gate_arrived.reshape(n_ctx, owned, wide // 128, 2, 128)
    gate_reduced = jnp.stack(
        [from_parts(gate_arrived[:, :, :, side].reshape(n_ctx, owned, wide)) for side in range(2)],
        axis=1,
    )

    middle_part, gain_two_grad = norm_two_back(normed_two_grad)
    middle_grad = cotangent_half + middle_part
    branch_pre_grad, gain_one_grad = post_one_back(middle_grad)
    branch_half = branch_pre_grad.astype(bf16)
    branch_low = core_ordered(branch_half, from_partner(branch_half, "tensor", 1))
    output_w_grad = contract_rows(branch_low, attended_low)
    attended_grad = (
        jnp.dot(branch_low, full_output, preferred_element_type=f32)
        .astype(bf16)
        .reshape(row_count, head_count, HD)
    )
    scores_again = (
        jnp.einsum("hqd,kd->hqk", query_rot, key_all, preferred_element_type=f32) * score_scale
    )
    prob_again = jnp.exp(jnp.where(allowed[None], scores_again, -1e30) - log_total)
    probs_grad = jnp.einsum("qhd,kd->hqk", attended_grad, value_all, preferred_element_type=f32)
    value_grad_all = jnp.einsum(
        "hqk,qhd->kd", prob_again.astype(bf16), attended_grad, preferred_element_type=f32
    )
    row_delta = jnp.sum(prob_again * probs_grad, axis=-1, keepdims=True)
    score_grad = (prob_again * (probs_grad - row_delta)).astype(bf16)
    query_rot_grad = (
        jnp.einsum("hqk,kd->qhd", score_grad, key_all, preferred_element_type=f32) * score_scale
    )
    key_grad_all = (
        jnp.einsum("hqk,hqd->kd", score_grad, query_rot, preferred_element_type=f32) * score_scale
    )
    grad_mine = jnp.where(core_first, key_grad_all, value_grad_all)
    grad_other = jnp.where(core_first, value_grad_all, key_grad_all)
    grad_mine = grad_mine + from_partner(grad_other.astype(bf16), "tensor", 1).astype(f32)
    returned = from_behind(grad_mine[:behind].astype(bf16), "ctx", -1).astype(f32)
    own_grad = grad_mine[behind:].at[row_count - behind :].add(returned)
    query_normed_grad = rotate(query_rot_grad, query_cosine[:, None, :], -query_sine[:, None, :])
    query_pre_grad, head_zero_part = query_norm_back(query_normed_grad)
    query_lin_grad = query_pre_grad.reshape(row_count, head_count * HD).astype(bf16)
    key_pre_grad, head_one_part = key_norm_back(rotate(own_grad, query_cosine, -query_sine))
    keyval_lin_grad = jnp.where(core_first, key_pre_grad, own_grad).astype(bf16)
    head_one_part = jnp.where(core_first, head_one_part, 0.0)
    normed_one_grad = core_summed(
        contract_columns(query_lin_grad, full_query) + contract_columns(keyval_lin_grad, half_keyval)
    )
    query_w_grad = contract_rows(normed_one, query_lin_grad)
    keyval_w_grad = contract_rows(normed_one, keyval_lin_grad)
    norm_one_back = jax.vjp(rms_norm, inputs_half, gain_rows[0])[1]
    input_part, gain_zero_grad = norm_one_back(normed_one_grad)
    input_half = middle_grad + input_part
    input_grad = core_ordered(input_half, from_partner(input_half, "tensor", 1))

    gains_part = jnp.stack([gain_zero_grad, gain_one_grad, gain_two_grad, gain_three_grad], axis=1)
    heads_part = jnp.stack([head_zero_part, head_one_part], axis=1)
    heads_part = jnp.pad(
        heads_part.reshape(-1, owned_heads, 2), ((0, 0), (0, owned - owned_heads), (0, 0))
    ).reshape(-1, 2)
    small_part = jnp.concatenate([gains_part, heads_part], axis=1)
    small_grad = small_part + from_partner(small_part, "tensor", 1)
    attn_grad = jnp.concatenate(
        [query_w_grad, keyval_w_grad, output_w_grad, jnp.pad(small_grad, ((0, 0), (0, 122)))], axis=1
    ).astype(bf16)
    attn_grad = jnp.moveaxis(attn_grad.reshape(n_dp, n_ctx, owned, -1), 1, 0)
    attn_arrived = along_line(attn_grad, "ctx").astype(f32).sum(axis=0).astype(bf16)
    attn_sum = along_line(attn_arrived, "dp").astype(f32).sum(axis=0)
    query_reduced = attn_sum[:, :cols]
    keyval_half = attn_sum[:, cols : cols + HD]
    output_reduced = attn_sum[:, cols + HD : 2 * cols + HD]
    keyval_not = from_partner(keyval_half, "tensor", 1)
    keyval_reduced = jnp.concatenate(
        [
            jnp.where(core_first, keyval_half, keyval_not),
            jnp.where(core_first, keyval_not, keyval_half),
        ],
        axis=1,
    )
    gains_reduced = attn_sum[:, 2 * cols + HD : 2 * cols + HD + 4]
    heads_reduced = attn_sum[:owned_heads, 2 * cols + HD + 4 : 2 * cols + HD + 6]

    gains_new, gain_first_new, gain_second_new = adam_step(
        norm_gains, gains_reduced, gain_first, gain_second, 0.5, 0.0
    )
    heads_new, head_first_new, head_second_new = adam_step(
        head_gains, heads_reduced, head_first, head_second, 0.5, 0.0
    )
    query_new, query_first_new, query_second_new = adam_step(
        query_weight, query_reduced, query_first, query_second, D ** (-0.5), decay_rate
    )
    keyval_new, keyval_first_new, keyval_second_new = adam_step(
        keyval_weight, keyval_reduced, keyval_first, keyval_second, D ** (-0.5), decay_rate
    )
    output_new, output_first_new, output_second_new = adam_step(
        output_weight, output_reduced, output_first, output_second, (HQ * HD) ** (-0.5), decay_rate
    )
    gate_new, gate_first_new, gate_second_new = adam_step(
        gate_up, gate_reduced, gate_first, gate_second, D ** (-0.5), decay_rate
    )
    down_new, down_first_new, down_second_new = adam_step(
        down_weight, down_reduced, down_first, down_second, FF ** (-0.5), decay_rate
    )
    return (
        result,
        input_grad,
        gains_new,
        gain_first_new,
        gain_second_new,
        heads_new,
        head_first_new,
        head_second_new,
        query_new,
        query_first_new,
        query_second_new,
        keyval_new,
        keyval_first_new,
        keyval_second_new,
        output_new,
        output_first_new,
        output_second_new,
        gate_new,
        gate_first_new,
        gate_second_new,
        down_new,
        down_first_new,
        down_second_new,
    )


def solution(mesh):
    placed = (
        P(("dp", "ctx"), None),
        P(("dp", "ctx"), None),
        P("dp", None),
        P(("dp", "ctx"), None),
        P(("dp", "ctx"), None),
        P(("dp", "ctx"), None),
        P(("dp", "ctx"), None),
        P(("dp", "ctx"), None),
        P(("dp", "ctx"), None),
        P(("dp", "ctx"), "tensor"),
        P(("dp", "ctx"), "tensor"),
        P(("dp", "ctx"), "tensor"),
        P(("dp", "ctx"), None),
        P(("dp", "ctx"), None),
        P(("dp", "ctx"), None),
        P(("dp", "ctx"), "tensor"),
        P(("dp", "ctx"), "tensor"),
        P(("dp", "ctx"), "tensor"),
        P(("dp", "ctx"), None, "tensor"),
        P(("dp", "ctx"), None, "tensor"),
        P(("dp", "ctx"), None, "tensor"),
        P(("dp", "ctx"), "tensor"),
        P(("dp", "ctx"), "tensor"),
        P(("dp", "ctx"), "tensor"),
    )
    return jax.shard_map(
        on_device,
        mesh=mesh,
        in_specs=placed,
        out_specs=(
            P(("dp", "ctx"), None),
            P(("dp", "ctx"), None),
            P(("dp", "ctx"), None),
            P(("dp", "ctx"), None),
            P(("dp", "ctx"), None),
            P(("dp", "ctx"), None),
            P(("dp", "ctx"), None),
            P(("dp", "ctx"), None),
            P(("dp", "ctx"), "tensor"),
            P(("dp", "ctx"), "tensor"),
            P(("dp", "ctx"), "tensor"),
            P(("dp", "ctx"), None),
            P(("dp", "ctx"), None),
            P(("dp", "ctx"), None),
            P(("dp", "ctx"), "tensor"),
            P(("dp", "ctx"), "tensor"),
            P(("dp", "ctx"), "tensor"),
            P(("dp", "ctx"), None, "tensor"),
            P(("dp", "ctx"), None, "tensor"),
            P(("dp", "ctx"), None, "tensor"),
            P(("dp", "ctx"), "tensor"),
            P(("dp", "ctx"), "tensor"),
            P(("dp", "ctx"), "tensor"),
        ),
        check_vma=False,
    )
```

```python
import functools

import jax
import jax.numpy as jnp
import numpy as np
from jax import lax
from jax.experimental import pallas as pl
from jax.experimental.pallas import tpu as pltpu
from jax.sharding import PartitionSpec as P

D = 1152
HQ = 4
HD = 256
FF = 6912
WIN = 512
STEP = 10


norm_eps = 1e-06
beta_one = 0.9
beta_two = 0.95
adam_eps = 1e-08
decay_rate = 0.1
rope_base = 10000.0
GELU_SCALE = float(np.sqrt(2.0 / np.pi))
MESH = pl.DeviceIdType.MESH


def from_partner(block, axis, bits):
    return lax.ppermute(block, axis, [(i ^ bits, i) for i in range(lax.axis_size(axis))])


def core_ordered(own, other):
    first = lax.axis_index("tensor") == 0
    return jnp.concatenate([jnp.where(first, own, other), jnp.where(first, other, own)], axis=0)


def half_of(array, dim):
    size = array.shape[dim] // 2
    return lax.dynamic_slice_in_dim(array, lax.axis_index("tensor") * size, size, axis=dim)


def token_layout(lengths, places):
    stop_at = jnp.cumsum(lengths)
    start_at = stop_at - lengths
    segment = jnp.sum((places[:, None] >= stop_at[None, :]).astype(jnp.int32), axis=1)
    owned_by = segment[:, None] == jnp.arange(lengths.shape[0], dtype=jnp.int32)[None, :]
    seg_begin = jnp.sum(jnp.where(owned_by, start_at[None, :], 0), axis=1)
    return (segment, places - seg_begin)


def rope_tables(position):
    half_dim = HD // 2
    exponent = jnp.arange(half_dim, dtype=jnp.float32) * (2.0 / HD)
    inverse = jnp.power(jnp.float32(rope_base), -exponent)
    angles = position.astype(jnp.float32)[:, None] * inverse[None, :]
    return (jnp.cos(angles), jnp.sin(angles))


def contract_rows(left_side, right_side):
    return lax.dot_general(
        left_side, right_side, (((0,), (0,)), ((), ())), preferred_element_type=jnp.float32
    )


def contract_columns(left_side, right_side):
    return lax.dot_general(
        left_side, right_side, (((1,), (1,)), ((), ())), preferred_element_type=jnp.float32
    )


def adam_step(weight_value, gradient, first_moment, second_moment, step_rate, decay_factor):
    first_moment = beta_one * first_moment + (1.0 - beta_one) * gradient
    second_moment = beta_two * second_moment + (1.0 - beta_two) * gradient * gradient
    first_hat = first_moment / (1.0 - beta_one**STEP)
    second_hat = second_moment / (1.0 - beta_two**STEP)
    update = first_hat / (jnp.sqrt(second_hat) + adam_eps)
    return (
        weight_value - step_rate * (update + decay_factor * weight_value),
        first_moment,
        second_moment,
    )


def places():
    return lax.axis_index("dp"), lax.axis_index("ctx"), lax.axis_index("tensor")


def plane_partners():
    dp, ctx, core = places()
    beside = ctx + 1 - 2 * lax.rem(ctx, 2)
    across = lax.rem(ctx + 2, 4)
    return (dp, beside, core), (dp, across, core), (dp, 3 - ctx, core), (dp, ctx, 1 - core)


def enter(n_dp, line):
    dp, ctx, core = places()
    barrier = pltpu.get_barrier_semaphore()

    def greet(device):
        pl.semaphore_signal(barrier, inc=1, device_id=device, device_id_type=MESH)

    for device in plane_partners():
        greet(device)
    if line:
        pl.when(dp < n_dp - 1)(lambda: greet((dp + 1, ctx, core)))
        pl.when(dp > 0)(lambda: greet((dp - 1, ctx, core)))
    ends = jnp.minimum(dp, 1) + jnp.minimum(n_dp - 1 - dp, 1) if line else 0
    pl.semaphore_wait(barrier, 4 + ends)


def in_columns(count, body):
    whole = count // 256

    def one(i, carry):
        body(pl.multiple_of(i * 256, 256), 256)
        return carry

    lax.fori_loop(0, whole, one, 0)
    if count % 256:
        body(whole * 256, count % 256)


def in_rows(count, body, start):
    size = 64

    def one(i, carry):
        return body(pl.multiple_of(i * size, size), size, carry)

    return lax.fori_loop(0, count // size, one, start)


def gather_copies(remote, buffer, base):
    x_dev, y_dev, _, core_dev = plane_partners()
    h = buffer.shape[2] // 2
    part_a, part_b = pl.ds(0, h), pl.ds(h, h)

    def piece(step, side):
        return buffer.at[step, 0, side]

    return [
        remote(piece(0, part_a), piece(1, part_a), base, x_dev),
        remote(piece(0, part_b), piece(1, part_b), base + 1, y_dev),
        remote(piece(0, part_b), piece(2, part_b), base + 2, x_dev),
        remote(piece(0, part_a), piece(2, part_a), base + 3, y_dev),
        remote(piece(1, part_a), piece(3, part_a), base + 4, y_dev),
        remote(piece(1, part_b), piece(3, part_b), base + 5, x_dev),
    ] + [
        remote(buffer.at[step, 0], buffer.at[step, 1], base + 6 + step, core_dev)
        for step in range(4)
    ]


def gather_step(copies, step):
    if step == 0:
        for copy in copies[:4]:
            copy.start()
    elif step == 1:
        copies[0].wait_recv()
        copies[1].wait_recv()
        copies[4].start()
        copies[5].start()
    else:
        copies[2 * step - 2].wait_recv()
        copies[2 * step - 1].wait_recv()
    copies[6 + step].start()
    copies[6 + step].wait_recv()


def turned(values, cosine, sine):
    half_dim = values.shape[-1] // 2
    lower, upper = values[:, :half_dim], values[:, half_dim:]
    return jnp.concatenate([lower * cosine - upper * sine, upper * cosine + lower * sine], axis=1)


def scale_of(values):
    return lax.rsqrt(jnp.mean(values * values, axis=1, keepdims=True) + norm_eps)


def attend_kernel(
    n_dp,
    owned_heads,
    tokens,
    cosine,
    sine,
    lowest,
    attn_pack,
    mlp_pack,
    mlp_full,
    attn_full,
    gain_rows,
    head_rows,
    normed_out,
    lin,
    query_out,
    keyval_out,
    attended,
    log_total,
    branch_out,
    middle_out,
    rows_out,
    slots,
    wide_slots,
    keyval,
    partial,
    core_send,
    core_take,
    own_sem,
    mlp_plane_send,
    mlp_plane_recv,
    mlp_line_send,
    mlp_line_recv,
    attn_line_send,
    attn_line_recv,
    attn_plane_send,
    attn_plane_recv,
    keyval_send,
    keyval_recv,
    rows,
    rows_send,
    rows_recv,
    rows_sem,
):
    dp, ctx, core = places()
    x_dev, y_dev, far_dev, core_dev = plane_partners()
    plane = ((dp, ctx, core), x_dev, y_dev, far_dev)
    f32, bf16 = jnp.float32, jnp.bfloat16
    row_count, width = tokens.shape
    half = row_count // 2
    owned = attn_pack.shape[0]
    behind = keyval.shape[1] - row_count
    next_dev = (dp, ctx + 1, core)
    enter(n_dp, True)

    def remote(source, target, send, recv, device):
        return pltpu.make_async_remote_copy(
            src_ref=source, dst_ref=target, send_sem=send, recv_sem=recv, device_id=device,
            device_id_type=MESH,
        )

    def line_block(way, step, k):
        origin = dp - step if way == 0 else dp + step
        return origin * 4 + plane[k][1]

    def can_take(way, step):
        return dp >= step if way == 0 else dp <= n_dp - 1 - step

    def can_give(way):
        return dp < n_dp - 1 if way == 0 else dp > 0

    def line_dev(way):
        return (dp + 1, ctx, core) if way == 0 else (dp - 1, ctx, core)

    def mlp_hop(way, step, k):
        block = mlp_full.at[line_block(way, step, k)]
        index = (way * n_dp + step) * 4 + k
        return remote(block, block, mlp_line_send.at[index], mlp_line_recv.at[index], line_dev(way))

    def mlp_came(way, step, k):
        block = mlp_full.at[line_block(way, step, k)]
        index = (way * n_dp + step - 1) * 4 + k
        return remote(block, block, mlp_line_send.at[index], mlp_line_recv.at[index], line_dev(way))

    def attn_hop(way, step):
        block = slots.at[line_block(way, step, 0)]
        index = way * n_dp + step
        return remote(block, block, attn_line_send.at[index], attn_line_recv.at[index], line_dev(way))

    def attn_came(way, step):
        block = slots.at[line_block(way, step, 0)]
        index = way * n_dp + step - 1
        return remote(block, block, attn_line_send.at[index], attn_line_recv.at[index], line_dev(way))

    def each(step, act, give):
        for way in range(2):
            if give:
                fits = can_give(way) & can_take(way, step) if step else can_give(way)
            else:
                fits = can_take(way, step)
            pl.when(fits)(functools.partial(act, way))

    def attn_plane(way, step, side, came=False):
        from_k = {1: 0, 2: 0, 3: 1 if step % 2 == 0 else 2}[side]
        device = {1: x_dev, 2: y_dev, 3: y_dev if step % 2 == 0 else x_dev}[side]
        block = slots.at[line_block(way, step, side if came else from_k)]
        index = (way * n_dp + step) * 4 + side
        return remote(block, block, attn_plane_send.at[index], attn_plane_recv.at[index], device)

    own_attn = pltpu.make_async_copy(attn_pack, slots.at[dp * 4 + ctx], own_sem.at[0])
    own_mlp = pltpu.make_async_copy(mlp_pack.at[ctx], mlp_full.at[dp * 4 + ctx], own_sem.at[1])
    own_attn.start()
    own_mlp.start()
    own_attn.wait()
    each(0, lambda way: attn_hop(way, 0).start(), True)
    for side in (1, 2):
        attn_plane(0, 0, side).start()
    own_mlp.wait()
    each(0, lambda way: mlp_hop(way, 0, 0).start(), True)

    def mlp_plane(k, came=False):
        return remote(
            mlp_pack.at[plane[k][1]],
            mlp_full.at[dp * 4 + (plane[k][1] if came else ctx)],
            mlp_plane_send.at[k],
            mlp_plane_recv.at[k],
            plane[k],
        )

    for k in (1, 2):
        mlp_plane(k).start()

    def came(way, step):
        attn_came(way, step).wait_recv()

    def hand_on(way, step):
        for side in (1, 2):
            attn_plane(way, step, side).start()

    order = [(0, 0)] + [(way, step) for step in range(1, n_dp) for way in range(2)]

    def relay(way, step):
        for side in (1, 2):
            attn_plane(way, step, side, True).wait_recv()
        attn_plane(way, step, 3).start()

    def relayed(way, step):
        attn_plane(way, step, 3, True).wait_recv()

    def where_held(way, step, act):
        if step:
            pl.when(can_take(way, step))(lambda: act(way, step))
        else:
            act(way, step)

    def mlp_first(k):
        mlp_plane(k, True).wait_recv()
        each(0, lambda way: mlp_hop(way, 0, k).start(), True)

    def mlp_next(step, k):
        each(step, lambda way: mlp_came(way, step, k).wait_recv(), False)
        if step < n_dp - 1:
            each(step, lambda way: mlp_hop(way, step, k).start(), True)

    events = [functools.partial(mlp_first, k) for k in (1, 2, 3)] + [
        functools.partial(mlp_next, step, k) for step in range(1, n_dp) for k in range(4)
    ]
    events.reverse()

    def move(count):
        for _ in range(min(count, len(events))):
            events.pop()()

    for step in range(1, n_dp):
        each(step, lambda way: came(way, step), False)
        each(step, lambda way: attn_hop(way, step).start(), True)
        each(step, lambda way: hand_on(way, step), False)
        if step == 1:
            mlp_plane(3).start()
        if step <= 3:
            move(1)
    if n_dp == 1:
        mlp_plane(3).start()
    move(max(0, 4 - n_dp) + 2)
    for way, step in order:
        where_held(way, step, relay)
    move(1)
    for way, step in order:
        where_held(way, step, relayed)
    move(1)

    for block in range(n_dp * 4):
        wide_slots[block * owned : (block + 1) * owned, :] = slots[block].astype(f32)

    def narrow(first, size, carry):
        at = pl.ds(first, size)
        attn_full[at] = wide_slots[at].astype(bf16)
        return carry

    in_rows(width, narrow, 0)
    pick = lax.broadcasted_iota(jnp.int32, (8, 128), 0) == lax.broadcasted_iota(
        jnp.int32, (8, 128), 1
    )
    small = contract_columns(pick.astype(f32).astype(bf16), attn_full[:, 1280:1408])
    gain_rows[...] = small
    row_of = lax.broadcasted_iota(jnp.int32, (width, HD), 0)
    head_of = lax.broadcasted_iota(jnp.int32, (width, HD), 1)
    shift = owned_heads.bit_length() - 1
    chosen = row_of == (head_of >> shift) * owned + (head_of & (owned_heads - 1))
    heads = jnp.dot(
        small.astype(bf16), chosen.astype(f32).astype(bf16), preferred_element_type=f32
    )
    head_rows[...] = heads

    def normalize(first, size, carry):
        at = pl.ds(first, size)
        values = tokens[at].astype(f32)
        normed_out[at] = (values * scale_of(values) * gain_rows[0:1]).astype(bf16)
        return carry

    in_rows(row_count, normalize, 0)

    def project(start, size):
        lin[:, pl.ds(start, size)] = jnp.dot(
            normed_out[...], attn_full[:, pl.ds(start, size)], preferred_element_type=f32
        )

    in_columns(3 * HD, project)
    move(1)

    def turn_keyval(first, size, carry):
        at = pl.ds(first, size)
        values = lin[at, 2 * HD : 3 * HD]
        keys = turned(values * scale_of(values) * head_rows[5:6], cosine[at], sine[at])
        mine = jnp.where(core == 0, keys, values).astype(bf16)
        keyval[core, pl.ds(pl.multiple_of(first + behind, 64), size)] = mine
        return carry

    in_rows(row_count, turn_keyval, 0)
    own_rows, last_rows = pl.ds(behind, row_count), pl.ds(row_count, behind)
    past_rows = pl.ds(0, behind)

    def to_core(came=False):
        block = keyval.at[1 - core if came else core, own_rows]
        return remote(block, block, keyval_send.at[0], keyval_recv.at[0], core_dev)

    def past_to_core(came=False):
        block = keyval.at[1 - core if came else core, past_rows]
        return remote(block, block, keyval_send.at[2], keyval_recv.at[2], core_dev)

    to_next = remote(
        keyval.at[core, last_rows],
        keyval.at[core, past_rows],
        keyval_send.at[1],
        keyval_recv.at[1],
        next_dev,
    )
    pl.when(ctx < 3)(to_next.start)
    to_core().start()

    def turn_query(first, size, carry):
        at = pl.ds(first, size)
        for head in range(2):
            values = lin[at, head * HD : (head + 1) * HD]
            normal = values * scale_of(values) * head_rows[4:5]
            query_out[head, at] = turned(normal, cosine[at], sine[at]).astype(bf16)
        return carry

    in_rows(row_count, turn_query, 0)

    @pl.when(ctx > 0)
    def _():
        to_next.wait_recv()
        past_to_core().start()
        past_to_core(True).wait_recv()

    @pl.when(ctx == 0)
    def _():
        keyval[:, 0:behind] = jnp.zeros((2, behind, HD), bf16)

    to_core(True).wait_recv()
    move(2)

    block_rows = 256
    reach = block_rows + behind

    def attend(first, head):
        at = pl.ds(first, block_rows)
        near = pl.ds(first, reach)
        scores = contract_columns(query_out[head, at], keyval[0, near]) * HD ** (-0.5)
        key_at = first + lax.broadcasted_iota(jnp.int32, (block_rows, reach), 1)
        query_at = first + behind + lax.broadcasted_iota(jnp.int32, (block_rows, reach), 0)
        scores = jnp.where((key_at >= lowest[at]) & (key_at <= query_at), scores, -1e30)
        row_max = jnp.max(scores, axis=1, keepdims=True)
        values = jnp.exp(scores - row_max)
        row_total = jnp.sum(values, axis=1, keepdims=True)
        probs = (values / row_total).astype(bf16)
        log_total[head, at] = row_max + jnp.log(row_total)
        out = jnp.dot(probs, keyval[1, near], preferred_element_type=f32)
        attended[at, head * HD : (head + 1) * HD] = out.astype(bf16)

    for block in range(row_count // block_rows):
        for head in range(2):
            attend(block * block_rows, head)
        move(1)

    def outward(start, size):
        partial[:, pl.ds(start, size)] = contract_columns(
            attended[...], attn_full[pl.ds(start, size), 3 * HD : 5 * HD]
        )

    in_columns(width, outward)

    def give_half(first, size, carry):
        at = pl.ds(pl.multiple_of((1 - core) * half + first, 64), size)
        core_send[pl.ds(first, size)] = partial[at].astype(bf16)
        return carry

    in_rows(half, give_half, 0)
    exchange = remote(core_send, core_take, keyval_send.at[3], keyval_recv.at[3], core_dev)
    exchange.start()
    exchange.wait_recv()

    def finish(first, size, carry):
        at = pl.ds(first, size)
        whole_at = pl.ds(pl.multiple_of(core * half + first, 64), size)
        branch = partial[whole_at] + core_take[at].astype(f32)
        branch_out[at] = branch
        middle = tokens[whole_at].astype(f32) + branch * scale_of(branch) * gain_rows[1:2]
        middle_out[at] = middle
        rows[0, 0, at] = (middle * scale_of(middle) * gain_rows[2:3]).astype(bf16)
        return carry

    in_rows(half, finish, 0)

    def remote_rows(source, target, index, device):
        return remote(source, target, rows_send.at[index], rows_recv.at[index], device)

    gather = gather_copies(remote_rows, rows, 0)
    outs = [
        pltpu.make_async_copy(rows.at[step], rows_out.at[step], rows_sem.at[step])
        for step in range(4)
    ]
    for step in range(4):
        gather_step(gather, step)
        outs[step].start()
        if step == 0:
            keyval_out[...] = keyval[...]
        move(1)
    move(len(events))
    for copy in gather:
        copy.wait_send()
    for copy in outs:
        copy.wait()

    exchange.wait_send()
    to_core().wait_send()
    pl.when(ctx < 3)(to_next.wait_send)
    pl.when(ctx > 0)(past_to_core().wait_send)
    for k in (1, 2, 3):
        mlp_plane(k).wait_send()
    for step in range(n_dp - 1):
        each(step, lambda way: attn_hop(way, step).wait_send(), True)
        for k in range(4):
            each(step, lambda way: mlp_hop(way, step, k).wait_send(), True)

    def left(way, step):
        for side in (1, 2, 3):
            attn_plane(way, step, side).wait_send()

    for way, step in order:
        where_held(way, step, left)


def attend_call(n_dp, owned_heads, behind, tokens, cosine, sine, lowest, attn_pack, mlp_pack):
    row_count, width = tokens.shape
    half = row_count // 2
    owned, attn_cols = attn_pack.shape
    blocks = n_dp * 4
    f32, bf16 = jnp.float32, jnp.bfloat16
    vmem = pl.BlockSpec(memory_space=pltpu.VMEM)
    anywhere = pl.BlockSpec(memory_space=pl.ANY)

    def array(dtype, *shape):
        return jax.ShapeDtypeStruct(shape, dtype)

    dma = pltpu.SemaphoreType.DMA
    return pl.pallas_call(
        functools.partial(attend_kernel, n_dp, owned_heads),
        out_shape=(
            array(bf16, blocks, owned, mlp_pack.shape[2]),
            array(bf16, width, attn_cols),
            array(f32, 8, width),
            array(f32, 8, HD),
            array(bf16, row_count, width),
            array(f32, row_count, 3 * HD),
            array(bf16, 2, row_count, HD),
            array(bf16, 2, behind + row_count, HD),
            array(bf16, row_count, 2 * HD),
            array(f32, 2, row_count, 1),
            array(f32, half, width),
            array(f32, half, width),
            array(bf16, 4, 2, half, width),
        ),
        in_specs=[vmem] * 4 + [anywhere] * 2,
        out_specs=(anywhere,) + (vmem,) * 11 + (anywhere,),
        scratch_shapes=[
            pltpu.VMEM((blocks, owned, attn_cols), bf16),
            pltpu.VMEM((width, attn_cols), f32),
            pltpu.VMEM((2, behind + row_count, HD), bf16),
            pltpu.VMEM((row_count, width), f32),
            pltpu.VMEM((half, width), bf16),
            pltpu.VMEM((half, width), bf16),
            dma((2,)),
            dma((4,)),
            dma((4,)),
            dma((8 * n_dp,)),
            dma((8 * n_dp,)),
            dma((2 * n_dp,)),
            dma((2 * n_dp,)),
            dma((8 * n_dp,)),
            dma((8 * n_dp,)),
            dma((4,)),
            dma((4,)),
            pltpu.VMEM((4, 2, half, width), bf16),
            dma((10,)),
            dma((10,)),
            dma((4,)),
        ],
        compiler_params=pltpu.CompilerParams(
            collective_id=1, has_side_effects=True, vmem_limit_bytes=60 * 2**20
        ),
        cost_estimate=pl.CostEstimate(
            flops=4 * 10**9, bytes_accessed=30 * 2**20, transcendentals=2 * 10**6
        ),
        name="attend",
    )(tokens, cosine, sine, lowest, attn_pack, mlp_pack)


def mlp_kernel(
    rows_in,
    middle,
    cotangent,
    gain,
    weights_in,
    result,
    back_sum,
    gain_sum,
    weights_out,
    rows,
    grads,
    hidden,
    pair,
    weights,
    total,
    waiting,
    core_send,
    core_take,
    plane_send,
    plane_take,
    send_sem,
    recv_sem,
    load_sem,
    out_sem,
):
    half, width = middle.shape
    h = half // 2
    hid = hidden.shape[2]
    step_rows = 2 * half
    part_a, part_b = pl.ds(0, h), pl.ds(h, h)
    x_dev, y_dev, _, core_dev = plane_partners()
    f32, bf16 = jnp.float32, jnp.bfloat16

    loads = [pltpu.make_async_copy(weights_in, weights, load_sem.at[4])] + [
        pltpu.make_async_copy(rows_in.at[step], rows.at[step], load_sem.at[step])
        for step in range(4)
    ]
    for load in (loads[0], loads[4], loads[3], loads[2], loads[1]):
        load.start()
    enter(1, False)

    def remote(source, target, index, device):
        return pltpu.make_async_remote_copy(
            src_ref=source,
            dst_ref=target,
            send_sem=send_sem.at[index],
            recv_sem=recv_sem.at[index],
            device_id=device,
            device_id_type=MESH,
        )

    def scatter_copies(base):
        return [
            remote(plane_send.at[0, part_a], plane_take.at[0, part_a], base, y_dev),
            remote(plane_send.at[0, part_b], plane_take.at[0, part_b], base + 1, x_dev),
            remote(plane_send.at[1, part_a], plane_take.at[1, part_a], base + 2, y_dev),
            remote(plane_send.at[1, part_b], plane_take.at[1, part_b], base + 3, x_dev),
            remote(plane_send.at[2, part_a], plane_take.at[2, part_a], base + 4, x_dev),
            remote(plane_send.at[2, part_b], plane_take.at[2, part_b], base + 5, y_dev),
        ] + [
            remote(core_send.at[step % 2], core_take.at[step], base + 6 + step, core_dev)
            for step in range(4)
        ]

    def scatter_step(copies, step, before, left, first):
        kept = (total, waiting, back_sum, back_sum)[step]
        slot = core_send.at[step % 2]
        if before is not None:
            copies[6 + before].wait_send()

        def body(start, size):
            product = contract_columns(
                left[step], weights[pl.ds(start, size), first : first + left.shape[2]]
            )
            kept[:, pl.ds(start, size)] = product[:half]
            slot[:, pl.ds(start, size)] = product[half:].astype(bf16)

        in_columns(width, body)
        copies[6 + step].start()
        copies[6 + step].wait_recv()
        summed = kept[...] + core_take[step].astype(f32)
        if step < 2:
            kept[...] = summed
        else:
            plane_send[step - 2] = summed.astype(bf16)
            copies[2 * step - 4].start()
            copies[2 * step - 3].start()

    def scatter_end(copies):
        copies[2].wait_recv()
        copies[3].wait_recv()
        plane_send[2] = (waiting[...] + plane_take[1].astype(f32)).astype(bf16)
        copies[4].start()
        copies[5].start()

    def scatter_total(at):
        return total[at] + plane_take[0, at].astype(f32) + plane_take[2, at].astype(f32)

    def scatter_wait(copies):
        for index in (0, 1, 4, 5):
            copies[index].wait_recv()

    def sent(copies):
        for copy in copies:
            copy.wait_send()

    scatter = scatter_copies(0)
    loads[0].wait()
    for step in (3, 2, 1, 0):
        loads[1 + step].wait()

        def activate(j, carry):
            at = pl.multiple_of(j * 256, 256)
            lin = jnp.dot(
                rows[step].reshape(step_rows, width),
                weights[:, pl.ds(at, 256)],
                preferred_element_type=f32,
            )
            gate, up = lin[:, :128], lin[:, 128:]
            square = gate * gate
            curve = jnp.tanh(GELU_SCALE * gate * (1.0 + 0.044715 * square))
            gelu = 0.5 * gate * (1.0 + curve)
            slope = 0.5 * (1.0 + curve) + 0.5 * GELU_SCALE * gate * (1.0 - curve * curve) * (
                1.0 + 3 * 0.044715 * square
            )
            at_half = pl.multiple_of(j * 128, 128)
            hidden[step, :, pl.ds(at_half, 128)] = (gelu * up).astype(bf16)
            pair[step, :, pl.ds(at, 128)] = (slope * up).astype(bf16)
            pair[step, :, pl.ds(pl.multiple_of(at + 128, 128), 128)] = gelu.astype(bf16)
            return carry

        lax.fori_loop(0, hid // 128, activate, 0)
        scatter_step(scatter, step, step + 2 if step < 2 else None, hidden, 2 * hid)
        if step == 1:
            scatter_end(scatter)
    scatter_wait(scatter)
    sent(scatter[:8])

    def norm_rows(first, size, gain_total):
        at = pl.ds(first, size)
        raw = scatter_total(at)
        scale = lax.rsqrt(jnp.mean(raw * raw, axis=1, keepdims=True) + norm_eps)
        normal = raw * scale
        result[at] = (middle[at] + normal * gain[...]).astype(bf16)
        cotangents = cotangent[at].astype(f32)
        scaled = cotangents * gain[...]
        inner = jnp.mean(raw * scaled, axis=1, keepdims=True)
        back = scale * scaled - raw * (scale * scale * scale * inner)
        grads[0, 0, at] = back.astype(bf16)
        return gain_total + jnp.sum(cotangents * normal, axis=0, keepdims=True)

    gain_sum[...] = in_rows(half, norm_rows, jnp.zeros((1, width), f32))

    gather = gather_copies(remote, grads, 10)
    scatter = scatter_copies(20)
    for step in range(4):
        gather_step(gather, step)

        def unfold(start, size):
            hidden_grad = jnp.dot(
                grads[step].reshape(step_rows, width),
                weights[:, pl.ds(pl.multiple_of(2 * hid + start, 128), size)],
                preferred_element_type=f32,
            )
            for tile in range(size // 128):
                piece = hidden_grad[:, tile * 128 : (tile + 1) * 128]
                for side in range(2):
                    at = pl.ds(pl.multiple_of(2 * start + (2 * tile + side) * 128, 128), 128)
                    pair[step, :, at] = (pair[step, :, at].astype(f32) * piece).astype(bf16)

        in_columns(hid, unfold)
        scatter_step(scatter, step, step - 2 if step >= 2 else None, pair, 0)
    sent(gather)

    def weigh(first, right):
        def one(i, carry):
            at = pl.ds(pl.multiple_of(i * 384, 128), 384)
            left = (rows if right is pair else grads)[:, :, :, at].reshape(8 * half, 384)
            product = contract_rows(left, right[...].reshape(8 * half, right.shape[2]))
            weights[at, first : first + right.shape[2]] = product.astype(bf16)
            return carry

        lax.fori_loop(0, width // 384, one, 0)
        columns = pl.ds(first, right.shape[2])
        copy = pltpu.make_async_copy(
            weights.at[:, columns], weights_out.at[:, columns], out_sem.at[first // (2 * hid)]
        )
        copy.start()
        return copy

    down_out = weigh(2 * hid, hidden)
    scatter_end(scatter)
    gate_out = weigh(0, pair)
    scatter_wait(scatter)

    def finish_rows(first, size, carry):
        at = pl.ds(first, size)
        back_sum[at] = scatter_total(at)
        return carry

    in_rows(half, finish_rows, 0)
    sent(scatter[:6] + scatter[8:])
    down_out.wait()
    gate_out.wait()


def mlp_call(rows, middle, cotangent, gain, weights):
    half, width = middle.shape
    hid = weights.shape[1] // 3
    count = 8 * half
    f32, bf16 = jnp.float32, jnp.bfloat16
    vmem = pl.BlockSpec(memory_space=pltpu.VMEM)
    anywhere = pl.BlockSpec(memory_space=pl.ANY)
    return pl.pallas_call(
        mlp_kernel,
        out_shape=(
            jax.ShapeDtypeStruct((half, width), bf16),
            jax.ShapeDtypeStruct((half, width), f32),
            jax.ShapeDtypeStruct((1, width), f32),
            jax.ShapeDtypeStruct((width, 3 * hid), bf16),
        ),
        in_specs=[anywhere, vmem, vmem, vmem, anywhere],
        out_specs=(vmem, vmem, vmem, anywhere),
        scratch_shapes=[
            pltpu.VMEM((4, 2, half, width), bf16),
            pltpu.VMEM((4, 2, half, width), bf16),
            pltpu.VMEM((4, 2 * half, hid), bf16),
            pltpu.VMEM((4, 2 * half, 2 * hid), bf16),
            pltpu.VMEM((width, 3 * hid), bf16),
            pltpu.VMEM((half, width), f32),
            pltpu.VMEM((half, width), f32),
            pltpu.VMEM((2, half, width), bf16),
            pltpu.VMEM((4, half, width), bf16),
            pltpu.VMEM((3, half, width), bf16),
            pltpu.VMEM((3, half, width), bf16),
            pltpu.SemaphoreType.DMA((30,)),
            pltpu.SemaphoreType.DMA((30,)),
            pltpu.SemaphoreType.DMA((5,)),
            pltpu.SemaphoreType.DMA((2,)),
        ],
        compiler_params=pltpu.CompilerParams(
            collective_id=0, has_side_effects=True, vmem_limit_bytes=63 * 2**20
        ),
        cost_estimate=pl.CostEstimate(
            flops=2 * count * width * hid * 9, bytes_accessed=30 * 2**20, transcendentals=count * hid
        ),
        name="feed_forward",
    )(rows, middle, cotangent, gain, weights)


def norm_back(values, gains, grads):
    scale = scale_of(values)
    normal = values * scale
    scaled = grads * gains
    inner = jnp.mean(values * scaled, axis=1, keepdims=True)
    return scale * scaled - values * (scale * scale * scale * inner), grads * normal


def retreat_kernel(
    n_dp,
    line,
    owned_heads,
    back_sum,
    middle,
    branch,
    cotangent_in,
    tokens_in,
    cosine,
    sine,
    lowest,
    gain_rows,
    head_rows,
    gain_three,
    attn_full_in,
    normed_one_in,
    lin_in,
    query_in,
    keyval_in,
    attended_in,
    log_total,
    mlp_grads,
    input_out,
    mlp_reduced,
    attn_reduced,
    line_slots,
    attn_grads,
    attn_blocks,
    attn_plane_take,
    attn_sums,
    attn_slots,
    branch_low,
    attended_grad,
    query_grad,
    lin_grad,
    keyval_grad,
    keyval_send,
    keyval_take,
    past_take,
    partial,
    core_send,
    core_take,
    small_rows,
    small_take,
    line_send_sem,
    line_recv_sem,
    plane_send_sem,
    plane_recv_sem,
    attn_plane_send_sem,
    attn_plane_recv_sem,
    attn_line_send_sem,
    attn_line_recv_sem,
    core_send_sem,
    core_recv_sem,
    load_sem,
    mlp_own,
    cotangent,
    tokens,
    attn_full,
    normed_one,
    lin,
    query,
    keyval,
    attended,
):
    dp, ctx, core = places()
    x_dev, y_dev, far_dev, core_dev = plane_partners()
    plane = ((dp, ctx, core), x_dev, y_dev, far_dev)
    f32, bf16 = jnp.float32, jnp.bfloat16
    row_count, width = tokens.shape
    half = row_count // 2
    owned, hid = mlp_grads.shape[1], mlp_grads.shape[2] // 3
    behind = keyval.shape[1] - row_count
    last_dp = line - 1
    here_dp = dp if line > 1 else 0
    sources = (
        (cotangent_in, cotangent),
        (attn_full_in, attn_full),
        (query_in, query),
        (keyval_in, keyval),
        (mlp_grads, mlp_own),
        (lin_in, lin),
        (attended_in, attended),
        (normed_one_in, normed_one),
        (tokens_in, tokens),
    )
    held = [
        pltpu.make_async_copy(source, target, load_sem.at[3 + index])
        for index, (source, target) in enumerate(sources)
    ]
    loads = [
        pltpu.make_async_copy(
            source,
            attn_grads.at[pl.ds(index * half, half), pl.ds(0, width)],
            load_sem.at[index],
        )
        for index, source in enumerate((middle, branch, back_sum))
    ]
    for load in loads + held:
        load.start()
    enter(n_dp, line > 1)

    def remote(source, target, send, recv, device):
        return pltpu.make_async_remote_copy(
            src_ref=source,
            dst_ref=target,
            send_sem=send,
            recv_sem=recv,
            device_id=device,
            device_id_type=MESH,
        )

    def goal(way, far):
        return dp + far if way == 0 else dp - far

    def has_goal(way, far):
        return dp + far <= last_dp if way == 0 else dp >= far

    def is_first(way):
        return dp == 0 if way == 0 else dp == last_dp

    def not_first(way):
        return dp > 0 if way == 0 else dp < last_dp

    def line_dev(way):
        return (dp + 1, ctx, core) if way == 0 else (dp - 1, ctx, core)

    def slot_of(way, far, k):
        return (way * last_dp + far - 1) * 4 + k

    def own_mlp(place, k):
        return mlp_own[place * 4 + plane[k][1]].astype(f32)

    def first_hop(way, far, k):
        slot = slot_of(way, far, k)
        return remote(
            mlp_grads.at[goal(way, far) * 4 + plane[k][1]],
            line_slots.at[slot],
            line_send_sem.at[slot],
            line_recv_sem.at[slot],
            line_dev(way),
        )

    def next_hop(way, far, k):
        slot = slot_of(way, far, k)
        return remote(
            line_slots.at[slot_of(way, far + 1, k)],
            line_slots.at[slot],
            line_send_sem.at[slot],
            line_recv_sem.at[slot],
            line_dev(way),
        )

    def came(way, far, k):
        slot = slot_of(way, far, k)
        block = line_slots.at[slot]
        remote(
            block, block, line_send_sem.at[slot], line_recv_sem.at[slot], line_dev(way)
        ).wait_recv()

    turn = (3, 1, 2, 0)

    def start_first(blocks):
        def start(way):
            for far, k in blocks:
                first_hop(way, far, k).start()

        for way in range(2):
            if line > 1:
                pl.when(is_first(way))(functools.partial(start, way))

    start_first([(far, k) for far in range(last_dp, 1, -1) for k in turn])

    def pass_on(way, far, k):
        came(way, far + 1, k)
        slot = slot_of(way, far + 1, k)
        line_slots[slot] = (line_slots[slot].astype(f32) + own_mlp(goal(way, far), k)).astype(bf16)
        next_hop(way, far, k).start()

    def mlp_step(far, k):
        for way in range(2):
            pl.when(not_first(way) & has_goal(way, far))(functools.partial(pass_on, way, far, k))

    def to_owner(k, came=False):
        place = plane[k][1] if came else ctx
        return remote(
            line_slots.at[k], mlp_reduced.at[place], plane_send_sem.at[k], plane_recv_sem.at[k], plane[k]
        )

    own_done = pltpu.make_async_copy(line_slots.at[0], mlp_reduced.at[ctx], plane_send_sem.at[0])

    def mlp_last(k):
        if line > 1:
            for way in range(2):
                pl.when(not_first(way))(functools.partial(came, way, 1, k))
        total = own_mlp(here_dp, k)
        for way in range(2):
            if line > 1:
                arrived = line_slots[slot_of(way, 1, k)].astype(f32)
                total = total + jnp.where(not_first(way), arrived, 0.0)
        line_slots[k] = total.astype(bf16)
        if k:
            to_owner(k).start()
        else:
            own_done.start()

    events = [
        functools.partial(mlp_step, far, k) for far in range(line - 2, 0, -1) for k in turn
    ] + [functools.partial(mlp_last, k) for k in turn]
    events.reverse()

    def move(count):
        for _ in range(min(count, len(events))):
            events.pop()()

    for load in loads + held[:1]:
        load.wait()

    def loaded(index, first, size):
        return attn_grads[pl.ds(pl.multiple_of(first + index * half, 64), size), 0:width]

    def norms(first, size, carry):
        at = pl.ds(first, size)
        part, gain_two = norm_back(loaded(0, first, size), gain_rows[2:3], loaded(2, first, size))
        middle_grad = cotangent[at].astype(f32) + part
        input_out[at] = middle_grad
        grad, gain_one = norm_back(loaded(1, first, size), gain_rows[1:2], middle_grad)
        branch_low[pl.ds(pl.multiple_of(core * half + first, 64), size)] = grad.astype(bf16)
        return (
            carry[0] + jnp.sum(gain_one, axis=0, keepdims=True),
            carry[1] + jnp.sum(gain_two, axis=0, keepdims=True),
        )

    nothing = jnp.zeros((1, width), f32)
    small_rows[...] = jnp.zeros_like(small_rows)
    gain_one, gain_two = in_rows(half, norms, (nothing, nothing))
    small_rows[1:2] = gain_one
    small_rows[2:3] = gain_two
    small_rows[3:4] = gain_three[...]

    def halves(came):
        rows = pl.ds(pl.multiple_of((1 - core if came else core) * half, 64), half)
        return remote(
            branch_low.at[rows], branch_low.at[rows], core_send_sem.at[0], core_recv_sem.at[0], core_dev
        )

    halves(False).start()
    halves(True).wait_recv()

    def inward(start, size):
        grad = jnp.dot(
            branch_low[...],
            attn_full[:, pl.ds(pl.multiple_of(3 * HD + start, 128), size)],
            preferred_element_type=f32,
        )
        attended_grad[:, pl.ds(start, size)] = grad.astype(bf16)

    held[1].wait()
    in_columns(2 * HD, inward)

    block_rows = 256
    reach = block_rows + behind
    keyval_grad[...] = jnp.zeros_like(keyval_grad)
    for load in held[2:5]:
        load.wait()

    def retreat(first, head):
        at = pl.ds(first, block_rows)
        near = pl.ds(first, reach)
        columns = slice(head * HD, (head + 1) * HD)
        scores = contract_columns(query[head, at], keyval[0, near]) * HD ** (-0.5)
        key_at = first + lax.broadcasted_iota(jnp.int32, (block_rows, reach), 1)
        query_at = first + behind + lax.broadcasted_iota(jnp.int32, (block_rows, reach), 0)
        scores = jnp.where((key_at >= lowest[at]) & (key_at <= query_at), scores, -1e30)
        probs = jnp.exp(scores - log_total[head, at])
        grads = attended_grad[at, columns]
        probs_grad = contract_columns(grads, keyval[1, near])
        delta = jnp.sum(probs * probs_grad, axis=1, keepdims=True)
        score_grad = (probs * (probs_grad - delta)).astype(bf16)
        query_grad[at, columns] = (
            jnp.dot(score_grad, keyval[0, near], preferred_element_type=f32) * HD ** (-0.5)
        )
        keyval_grad[0, near] += contract_rows(score_grad, query[head, at]) * HD ** (-0.5)
        keyval_grad[1, near] += contract_rows(probs.astype(bf16), grads)

    for block in range(row_count // block_rows):
        for head in range(2):
            retreat(block * block_rows, head)
    move(2)

    keyval_send[0] = keyval_grad[1 - core].astype(bf16)
    to_core = remote(
        keyval_send.at[0], keyval_take, core_send_sem.at[1], core_recv_sem.at[1], core_dev
    )
    to_core.start()

    def query_rows(first, size, carry):
        at = pl.ds(first, size)
        total = carry
        for head in range(2):
            columns = slice(head * HD, (head + 1) * HD)
            grads = turned(query_grad[at, columns], cosine[at], -sine[at])
            grad, gain = norm_back(lin[at, columns], head_rows[4:5], grads)
            lin_grad[at, columns] = grad.astype(bf16)
            total = total + jnp.sum(gain, axis=0, keepdims=True)
        return total

    for load in held[5:]:
        load.wait()
    head_zero = in_rows(row_count, query_rows, jnp.zeros((1, HD), f32))
    move(1)
    to_core.wait_recv()
    keyval_grad[core] = keyval_grad[core] + keyval_take[...].astype(f32)
    keyval_send[1, 0:behind] = keyval_grad[core, 0:behind].astype(bf16)
    to_past = remote(
        keyval_send.at[1, pl.ds(0, behind)],
        past_take,
        core_send_sem.at[2],
        core_recv_sem.at[2],
        (dp, ctx - 1, core),
    )
    pl.when(ctx > 0)(to_past.start)

    def outward(start, size):
        attn_grads[0:width, pl.ds(pl.multiple_of(3 * HD + start, 128), size)] = contract_rows(
            branch_low[...], attended[:, pl.ds(start, size)]
        )

    in_columns(2 * HD, outward)

    @pl.when(ctx < 3)
    def _():
        to_past.wait_recv()
        late = pl.ds(row_count, behind)
        keyval_grad[core, late] = keyval_grad[core, late] + past_take[...].astype(f32)

    def keyval_rows(first, size, carry):
        at = pl.ds(first, size)
        values = keyval_grad[core, pl.ds(pl.multiple_of(first + behind, 64), size)]
        grads = turned(values, cosine[at], -sine[at])
        grad, gain = norm_back(lin[at, 2 * HD : 3 * HD], head_rows[5:6], grads)
        lin_grad[at, 2 * HD : 3 * HD] = jnp.where(core == 0, grad, values).astype(bf16)
        return carry + jnp.sum(gain, axis=0, keepdims=True)

    head_one = in_rows(row_count, keyval_rows, jnp.zeros((1, HD), f32))
    head_one = jnp.where(core == 0, head_one, 0.0)

    def weigh(start, size):
        attn_grads[0:width, pl.ds(start, size)] = contract_rows(
            normed_one[...], lin_grad[:, pl.ds(start, size)]
        )

    in_columns(3 * HD, weigh)
    move(1)
    start_first([(1, k) for k in turn[:2]])

    def back(start, size):
        columns = pl.ds(start, size)
        product = contract_columns(lin_grad[...], attn_full[columns, 0 : 3 * HD])
        first, second = product[:half], product[half:]
        partial[:, columns] = jnp.where(core == 0, first, second)
        core_send[:, columns] = jnp.where(core == 0, second, first).astype(bf16)

    in_columns(width, back)
    exchange = remote(core_send, core_take, core_send_sem.at[3], core_recv_sem.at[3], core_dev)
    exchange.start()
    exchange.wait_recv()

    def finish(first, size, carry):
        at = pl.ds(first, size)
        whole_at = pl.ds(pl.multiple_of(core * half + first, 64), size)
        grads = partial[at] + core_take[at].astype(f32)
        part, gain = norm_back(tokens[whole_at].astype(f32), gain_rows[0:1], grads)
        input_out[at] = input_out[at] + part
        return carry + jnp.sum(gain, axis=0, keepdims=True)

    small_rows[0:1] = in_rows(half, finish, nothing)

    row_of = lax.broadcasted_iota(jnp.int32, (width, HD), 0)
    head_of = lax.broadcasted_iota(jnp.int32, (width, HD), 1)
    shift = owned_heads.bit_length() - 1
    chosen = row_of == (head_of >> shift) * owned + (head_of & (owned_heads - 1))
    heads = jnp.concatenate([head_zero, head_one, jnp.zeros((6, HD), f32)], axis=0)
    spread = contract_columns(heads.astype(bf16), chosen.astype(f32).astype(bf16))
    small_rows[4:6] = spread[0:2]
    smalls = remote(
        small_rows.at[pl.ds(0, 8)], small_take, core_send_sem.at[4], core_recv_sem.at[4], core_dev
    )
    smalls.start()
    smalls.wait_recv()
    smalls.wait_send()
    small_rows[0:8] = small_rows[0:8] + small_take[...]
    attn_grads[0:width, 5 * HD : 5 * HD + 128] = small_rows[...].T

    for block in range(n_dp * 4):
        attn_blocks[block] = attn_grads[block * owned : (block + 1) * owned, :].astype(bf16)

    def attn_plane(k, place):
        index = (k - 1) * n_dp + place
        return remote(
            attn_blocks.at[place * 4 + plane[k][1]],
            attn_plane_take.at[index],
            attn_plane_send_sem.at[index],
            attn_plane_recv_sem.at[index],
            plane[k],
        )

    for place in range(n_dp):
        for k in (3, 1, 2):
            attn_plane(k, place).start()
    move(len(events) - 4)
    for place in range(n_dp):
        total = attn_blocks[place * 4 + ctx].astype(f32)
        for k in (1, 2, 3):
            attn_plane(k, place).wait_recv()
            total = total + attn_plane_take[(k - 1) * n_dp + place].astype(f32)
        attn_sums[place] = total.astype(bf16)

    def attn_hop(way, far, first):
        source = attn_sums.at[goal(way, far)] if first else attn_slots.at[way * line + far + 1]
        index = way * line + far
        return remote(
            source,
            attn_slots.at[index],
            attn_line_send_sem.at[index],
            attn_line_recv_sem.at[index],
            line_dev(way),
        )

    def attn_came(way, far):
        index = way * line + far
        block = attn_slots.at[index]
        remote(
            block, block, attn_line_send_sem.at[index], attn_line_recv_sem.at[index], line_dev(way)
        ).wait_recv()

    def attn_start(way):
        for far in range(last_dp, 0, -1):
            attn_hop(way, far, True).start()

    def attn_pass(way, far):
        attn_came(way, far + 1)
        index = way * line + far + 1
        total = attn_slots[index].astype(f32) + attn_sums[goal(way, far)].astype(f32)
        attn_slots[index] = total.astype(bf16)
        attn_hop(way, far, False).start()

    for way in range(2):
        if line > 1:
            pl.when(is_first(way))(functools.partial(attn_start, way))
    start_first([(1, k) for k in turn[2:]])
    for far in range(line - 2, 0, -1):
        for way in range(2):
            pl.when(not_first(way) & has_goal(way, far))(functools.partial(attn_pass, way, far))
    move(4)
    if line == 1:
        attn_reduced[...] = attn_sums[...]
    else:
        total = attn_sums[dp].astype(f32)
        for way in range(2):
            pl.when(not_first(way))(functools.partial(attn_came, way, 1))
            arrived = attn_slots[way * line + 1].astype(f32)
            total = total + jnp.where(not_first(way), arrived, 0.0)
        attn_reduced[0] = total.astype(bf16)

    for k in (1, 2, 3):
        to_owner(k, True).wait_recv()
        to_owner(k).wait_send()
    own_done.wait()
    halves(False).wait_send()
    to_core.wait_send()
    pl.when(ctx > 0)(to_past.wait_send)
    exchange.wait_send()
    for place in range(n_dp):
        for k in (1, 2, 3):
            attn_plane(k, place).wait_send()

    def first_left(way):
        for far in range(last_dp, 0, -1):
            attn_hop(way, far, True).wait_send()
            for k in turn:
                first_hop(way, far, k).wait_send()

    def left(way, far):
        attn_hop(way, far, False).wait_send()
        for k in turn:
            next_hop(way, far, k).wait_send()

    for way in range(2):
        if line > 1:
            pl.when(is_first(way))(functools.partial(first_left, way))
        for far in range(line - 2, 0, -1):
            pl.when(not_first(way) & has_goal(way, far))(functools.partial(left, way, far))


def retreat_call(n_dp, line, owned_heads, *arrays):
    tokens, attn_full, keyval = arrays[4], arrays[11], arrays[15]
    mlp_grads = arrays[18]
    row_count, width = tokens.shape
    half = row_count // 2
    blocks = n_dp * 4
    owned, hid = mlp_grads.shape[1], mlp_grads.shape[2] // 3
    attn_cols = attn_full.shape[1]
    reach = keyval.shape[1]
    behind = reach - row_count
    f32, bf16 = jnp.float32, jnp.bfloat16
    vmem = pl.BlockSpec(memory_space=pltpu.VMEM)
    anywhere = pl.BlockSpec(memory_space=pl.ANY)
    dma = pltpu.SemaphoreType.DMA
    return pl.pallas_call(
        functools.partial(retreat_kernel, n_dp, line, owned_heads),
        out_shape=(
            jax.ShapeDtypeStruct((half, width), f32),
            jax.ShapeDtypeStruct((4, owned, 3 * hid), bf16),
            jax.ShapeDtypeStruct((n_dp if line == 1 else 1, owned, attn_cols), bf16),
        ),
        in_specs=[
            anywhere if index < 5 or 11 <= index <= 16 or index == 18 else vmem
            for index in range(len(arrays))
        ],
        out_specs=(vmem, anywhere, vmem),
        scratch_shapes=[
            pltpu.VMEM((max(8 * (line - 1), 4), owned, 3 * hid), bf16),
            pltpu.VMEM((max(width, 3 * half), attn_cols), f32),
            pltpu.VMEM((blocks, owned, attn_cols), bf16),
            pltpu.VMEM((3 * n_dp, owned, attn_cols), bf16),
            pltpu.VMEM((n_dp, owned, attn_cols), bf16),
            pltpu.VMEM((2 * line, owned, attn_cols), bf16),
            pltpu.VMEM((row_count, width), bf16),
            pltpu.VMEM((row_count, 2 * HD), bf16),
            pltpu.VMEM((row_count, 2 * HD), f32),
            pltpu.VMEM((row_count, 3 * HD), bf16),
            pltpu.VMEM((2, reach, HD), f32),
            pltpu.VMEM((2, reach, HD), bf16),
            pltpu.VMEM((reach, HD), bf16),
            pltpu.VMEM((behind, HD), bf16),
            pltpu.VMEM((half, width), f32),
            pltpu.VMEM((half, width), bf16),
            pltpu.VMEM((half, width), bf16),
            pltpu.VMEM((128, width), f32),
            pltpu.VMEM((8, width), f32),
            dma((8 * line,)),
            dma((8 * line,)),
            dma((4,)),
            dma((4,)),
            dma((4 * n_dp,)),
            dma((4 * n_dp,)),
            dma((2 * line,)),
            dma((2 * line,)),
            dma((5,)),
            dma((5,)),
            dma((12,)),
            pltpu.VMEM(mlp_grads.shape, bf16),
        ]
        + [
            pltpu.VMEM(arrays[index].shape, arrays[index].dtype)
            for index in (3, 4, 11, 12, 13, 14, 15, 16)
        ],
        compiler_params=pltpu.CompilerParams(
            collective_id=2, has_side_effects=True, vmem_limit_bytes=63 * 2**20
        ),
        cost_estimate=pl.CostEstimate(
            flops=10**10, bytes_accessed=40 * 2**20, transcendentals=2 * 10**6
        ),
        name="retreat",
    )(*arrays)


def on_device(
    tokens,
    out_cotangent,
    lengths,
    norm_gains,
    gain_first,
    gain_second,
    head_gains,
    head_first,
    head_second,
    query_weight,
    query_first,
    query_second,
    keyval_weight,
    keyval_first,
    keyval_second,
    output_weight,
    output_first,
    output_second,
    gate_up,
    gate_first,
    gate_second,
    down_weight,
    down_first,
    down_second,
):
    bf16, f32 = jnp.bfloat16, jnp.float32
    row_count = tokens.shape[0]
    owned = query_weight.shape[0]
    owned_heads = head_gains.shape[0]
    n_dp, n_ctx = lax.axis_size("dp"), lax.axis_size("ctx")
    half_ff = gate_up.shape[2]
    wide = -(-half_ff // (n_ctx * 128)) * 128
    behind = WIN
    ctx_place = lax.axis_index("ctx")
    core_first = lax.axis_index("tensor") == 0
    score_scale = HD ** (-0.5)

    head_columns = jnp.pad(head_gains, ((0, owned - owned_heads), (0, 0)))
    small = jnp.concatenate([norm_gains, head_columns], axis=1).astype(bf16)
    attn_pack = jnp.concatenate(
        [
            query_weight.astype(bf16),
            half_of(keyval_weight, 1).astype(bf16),
            output_weight.astype(bf16),
            jnp.pad(small, ((0, 0), (0, 122))),
        ],
        axis=1,
    )
    cols = query_weight.shape[1]

    def in_parts(array):
        padded = jnp.pad(array.astype(bf16), ((0, 0), (0, n_ctx * wide - half_ff)))
        return padded.reshape(owned, n_ctx, wide // 128, 128)

    gate_parts = jnp.stack([in_parts(gate_up[:, side]) for side in range(2)], axis=3)
    mlp_pack = jnp.concatenate(
        [
            gate_parts.reshape(owned, n_ctx, 2 * wide),
            in_parts(down_weight).reshape(owned, n_ctx, wide),
        ],
        axis=2,
    )
    mlp_pack = jnp.moveaxis(mlp_pack, 1, 0)

    start_row = ctx_place * row_count
    row_index = jnp.arange(row_count, dtype=jnp.int32)
    query_position = token_layout(lengths[0], start_row + row_index)[1]
    query_cosine, query_sine = rope_tables(query_position)
    lowest = jnp.maximum(row_index - query_position + behind, row_index + 1)[:, None]
    (
        mlp_full,
        attn_full,
        gain_rows,
        head_rows,
        normed_one,
        lin,
        query_rot,
        keyval_all,
        attended_low,
        log_total,
        branch_raw,
        middle,
        group_rows,
    ) = attend_call(
        n_dp, owned_heads, behind, tokens, query_cosine, query_sine, lowest, attn_pack, mlp_pack
    )
    cotangent_half = half_of(out_cotangent, 0)
    (
        result_half,
        normed_two_grad,
        gain_three_part,
        mlp_grads,
    ) = mlp_call(
        group_rows,
        middle,
        cotangent_half,
        gain_rows[3:4],
        mlp_full.reshape(n_dp * n_ctx * owned, 3 * wide),
    )
    result = core_ordered(result_half, from_partner(result_half, "tensor", 1))

    line = n_dp if n_dp <= 4 else 1

    mlp_grads = mlp_grads.reshape(n_dp, n_ctx, owned, 3 * wide)
    if line == 1:
        mlp_grads = lax.psum_scatter(mlp_grads, "dp", scatter_dimension=0, tiled=True)
    mlp_grads = mlp_grads.reshape(line * n_ctx, owned, 3 * wide)
    input_half, mlp_reduced, attn_reduced = retreat_call(
        n_dp,
        line,
        owned_heads,
        normed_two_grad,
        middle,
        branch_raw,
        cotangent_half,
        tokens,
        query_cosine,
        query_sine,
        lowest,
        gain_rows,
        head_rows,
        gain_three_part,
        attn_full,
        normed_one,
        lin,
        query_rot,
        keyval_all,
        attended_low,
        log_total,
        mlp_grads,
    )
    input_grad = core_ordered(input_half, from_partner(input_half, "tensor", 1))

    if line == 1:
        attn_reduced = lax.psum_scatter(attn_reduced, "dp", scatter_dimension=0, tiled=True)
    attn_reduced = attn_reduced[0].astype(f32)

    def from_parts(tiles):
        return jnp.moveaxis(tiles, 0, 1).reshape(owned, n_ctx * wide)[:, :half_ff].astype(f32)

    gate_arrived = mlp_reduced[:, :, : 2 * wide].reshape(n_ctx, owned, wide // 128, 2, 128)
    gate_reduced = jnp.stack(
        [from_parts(gate_arrived[:, :, :, side].reshape(n_ctx, owned, wide)) for side in range(2)],
        axis=1,
    )
    down_reduced = from_parts(mlp_reduced[:, :, 2 * wide :])
    query_reduced = attn_reduced[:, :cols]
    keyval_half = attn_reduced[:, cols : cols + HD]
    output_reduced = attn_reduced[:, cols + HD : 2 * cols + HD]
    keyval_not = from_partner(keyval_half, "tensor", 1)
    keyval_reduced = jnp.concatenate(
        [
            jnp.where(core_first, keyval_half, keyval_not),
            jnp.where(core_first, keyval_not, keyval_half),
        ],
        axis=1,
    )
    gains_reduced = attn_reduced[:, 2 * cols + HD : 2 * cols + HD + 4]
    heads_reduced = attn_reduced[:owned_heads, 2 * cols + HD + 4 : 2 * cols + HD + 6]

    gains_new, gain_first_new, gain_second_new = adam_step(
        norm_gains, gains_reduced, gain_first, gain_second, 0.5, 0.0
    )
    heads_new, head_first_new, head_second_new = adam_step(
        head_gains, heads_reduced, head_first, head_second, 0.5, 0.0
    )
    query_new, query_first_new, query_second_new = adam_step(
        query_weight, query_reduced, query_first, query_second, D ** (-0.5), decay_rate
    )
    keyval_new, keyval_first_new, keyval_second_new = adam_step(
        keyval_weight, keyval_reduced, keyval_first, keyval_second, D ** (-0.5), decay_rate
    )
    output_new, output_first_new, output_second_new = adam_step(
        output_weight, output_reduced, output_first, output_second, (HQ * HD) ** (-0.5), decay_rate
    )
    gate_new, gate_first_new, gate_second_new = adam_step(
        gate_up, gate_reduced, gate_first, gate_second, D ** (-0.5), decay_rate
    )
    down_new, down_first_new, down_second_new = adam_step(
        down_weight, down_reduced, down_first, down_second, FF ** (-0.5), decay_rate
    )
    return (
        result,
        input_grad,
        gains_new,
        gain_first_new,
        gain_second_new,
        heads_new,
        head_first_new,
        head_second_new,
        query_new,
        query_first_new,
        query_second_new,
        keyval_new,
        keyval_first_new,
        keyval_second_new,
        output_new,
        output_first_new,
        output_second_new,
        gate_new,
        gate_first_new,
        gate_second_new,
        down_new,
        down_first_new,
        down_second_new,
    )


def solution(mesh):
    placed = (
        P(("dp", "ctx"), None),
        P(("dp", "ctx"), None),
        P("dp", None),
        P(("dp", "ctx"), None),
        P(("dp", "ctx"), None),
        P(("dp", "ctx"), None),
        P(("dp", "ctx"), None),
        P(("dp", "ctx"), None),
        P(("dp", "ctx"), None),
        P(("dp", "ctx"), "tensor"),
        P(("dp", "ctx"), "tensor"),
        P(("dp", "ctx"), "tensor"),
        P(("dp", "ctx"), None),
        P(("dp", "ctx"), None),
        P(("dp", "ctx"), None),
        P(("dp", "ctx"), "tensor"),
        P(("dp", "ctx"), "tensor"),
        P(("dp", "ctx"), "tensor"),
        P(("dp", "ctx"), None, "tensor"),
        P(("dp", "ctx"), None, "tensor"),
        P(("dp", "ctx"), None, "tensor"),
        P(("dp", "ctx"), "tensor"),
        P(("dp", "ctx"), "tensor"),
        P(("dp", "ctx"), "tensor"),
    )
    return jax.shard_map(
        on_device,
        mesh=mesh,
        in_specs=placed,
        out_specs=(
            P(("dp", "ctx"), None),
            P(("dp", "ctx"), None),
            P(("dp", "ctx"), None),
            P(("dp", "ctx"), None),
            P(("dp", "ctx"), None),
            P(("dp", "ctx"), None),
            P(("dp", "ctx"), None),
            P(("dp", "ctx"), None),
            P(("dp", "ctx"), "tensor"),
            P(("dp", "ctx"), "tensor"),
            P(("dp", "ctx"), "tensor"),
            P(("dp", "ctx"), None),
            P(("dp", "ctx"), None),
            P(("dp", "ctx"), None),
            P(("dp", "ctx"), "tensor"),
            P(("dp", "ctx"), "tensor"),
            P(("dp", "ctx"), "tensor"),
            P(("dp", "ctx"), None, "tensor"),
            P(("dp", "ctx"), None, "tensor"),
            P(("dp", "ctx"), None, "tensor"),
            P(("dp", "ctx"), "tensor"),
            P(("dp", "ctx"), "tensor"),
            P(("dp", "ctx"), "tensor"),
        ),
        check_vma=False,
    )
```

```python
import functools

import jax
import jax.numpy as jnp
import numpy as np
from jax import lax
from jax.experimental import pallas as pl
from jax.experimental.pallas import tpu as pltpu
from jax.sharding import PartitionSpec as P

D = 1152
HQ = 4
HD = 256
FF = 6912
WIN = 512
STEP = 10


norm_eps = 1e-06
beta_one = 0.9
beta_two = 0.95
adam_eps = 1e-08
decay_rate = 0.1
rope_base = 10000.0
GELU_SCALE = float(np.sqrt(2.0 / np.pi))
MESH = pl.DeviceIdType.MESH


def half_of(array, dim):
    size = array.shape[dim] // 2
    return lax.dynamic_slice_in_dim(array, lax.axis_index("tensor") * size, size, axis=dim)


def token_layout(lengths, places):
    count = lengths.shape[0]
    before = jnp.arange(count)[:, None] <= jnp.arange(count)[None, :]
    stop_at = jnp.sum(jnp.where(before, lengths[:, None], 0), axis=0)
    start_at = stop_at - lengths
    segment = jnp.sum((places[:, None] >= stop_at[None, :]).astype(jnp.int32), axis=1)
    owned_by = segment[:, None] == jnp.arange(lengths.shape[0], dtype=jnp.int32)[None, :]
    seg_begin = jnp.sum(jnp.where(owned_by, start_at[None, :], 0), axis=1)
    return (segment, places - seg_begin)


def rope_tables(position):
    half_dim = HD // 2
    exponent = jnp.arange(half_dim, dtype=jnp.float32) * (2.0 / HD)
    inverse = jnp.power(jnp.float32(rope_base), -exponent)
    angles = position.astype(jnp.float32)[:, None] * inverse[None, :]
    return (jnp.cos(angles), jnp.sin(angles))


def contract_rows(left_side, right_side):
    return lax.dot_general(
        left_side, right_side, (((0,), (0,)), ((), ())), preferred_element_type=jnp.float32
    )


def contract_columns(left_side, right_side):
    return lax.dot_general(
        left_side, right_side, (((1,), (1,)), ((), ())), preferred_element_type=jnp.float32
    )


def adam_step(weight_value, gradient, first_moment, second_moment, step_rate, decay_factor):
    first_moment = beta_one * first_moment + (1.0 - beta_one) * gradient
    second_moment = beta_two * second_moment + (1.0 - beta_two) * gradient * gradient
    first_hat = first_moment / (1.0 - beta_one**STEP)
    second_hat = second_moment / (1.0 - beta_two**STEP)
    update = first_hat / (jnp.sqrt(second_hat) + adam_eps)
    return (
        weight_value - step_rate * (update + decay_factor * weight_value),
        first_moment,
        second_moment,
    )


def places():
    return lax.axis_index("dp"), lax.axis_index("ctx"), lax.axis_index("tensor")


def plane_partners():
    dp, ctx, core = places()
    beside = ctx + 1 - 2 * lax.rem(ctx, 2)
    across = lax.rem(ctx + 2, 4)
    return (dp, beside, core), (dp, across, core), (dp, 3 - ctx, core), (dp, ctx, 1 - core)


def enter(n_dp, line):
    dp, ctx, core = places()
    barrier = pltpu.get_barrier_semaphore()

    def greet(device):
        pl.semaphore_signal(barrier, inc=1, device_id=device, device_id_type=MESH)

    for device in plane_partners():
        greet(device)
    if line:
        pl.when(dp < n_dp - 1)(lambda: greet((dp + 1, ctx, core)))
        pl.when(dp > 0)(lambda: greet((dp - 1, ctx, core)))
    ends = jnp.minimum(dp, 1) + jnp.minimum(n_dp - 1 - dp, 1) if line else 0
    pl.semaphore_wait(barrier, 4 + ends)


def in_columns(count, body):
    whole = count // 256

    def one(i, carry):
        body(pl.multiple_of(i * 256, 256), 256)
        return carry

    lax.fori_loop(0, whole, one, 0)
    if count % 256:
        body(whole * 256, count % 256)


def in_rows(count, body, start):
    size = 64

    def one(i, carry):
        return body(pl.multiple_of(i * size, size), size, carry)

    return lax.fori_loop(0, count // size, one, start)


def gather_copies(remote, buffer, base):
    x_dev, y_dev, _, core_dev = plane_partners()
    h = buffer.shape[2] // 2
    part_a, part_b = pl.ds(0, h), pl.ds(h, h)

    def piece(step, side):
        return buffer.at[step, 0, side]

    return [
        remote(piece(0, part_a), piece(1, part_a), base, x_dev),
        remote(piece(0, part_b), piece(1, part_b), base + 1, y_dev),
        remote(piece(0, part_b), piece(2, part_b), base + 2, x_dev),
        remote(piece(0, part_a), piece(2, part_a), base + 3, y_dev),
        remote(piece(1, part_a), piece(3, part_a), base + 4, y_dev),
        remote(piece(1, part_b), piece(3, part_b), base + 5, x_dev),
    ] + [
        remote(buffer.at[step, 0], buffer.at[step, 1], base + 6 + step, core_dev)
        for step in range(4)
    ]


def gather_step(copies, step):
    if step == 0:
        for copy in copies[:4]:
            copy.start()
    elif step == 1:
        copies[0].wait_recv()
        copies[1].wait_recv()
        copies[4].start()
        copies[5].start()
    else:
        copies[2 * step - 2].wait_recv()
        copies[2 * step - 1].wait_recv()
    copies[6 + step].start()
    copies[6 + step].wait_recv()


def turned(values, cosine, sine):
    half_dim = values.shape[-1] // 2
    lower, upper = values[:, :half_dim], values[:, half_dim:]
    return jnp.concatenate([lower * cosine - upper * sine, upper * cosine + lower * sine], axis=1)


def scale_of(values):
    return lax.rsqrt(jnp.mean(values * values, axis=1, keepdims=True) + norm_eps)


def attend_kernel(
    n_dp,
    owned_heads,
    tokens,
    cosine,
    sine,
    lowest,
    attn_pack,
    mlp_pack,
    mlp_full,
    gain_rows,
    head_rows,
    log_total,
    attn_full_out,
    normed_out_out,
    lin_out,
    query_out_out,
    keyval_out,
    attended_out,
    branch_out_out,
    middle_out_out,
    rows_out,
    slots,
    wide_slots,
    keyval,
    partial,
    core_send,
    core_take,
    own_sem,
    mlp_plane_send,
    mlp_plane_recv,
    mlp_line_send,
    mlp_line_recv,
    attn_line_send,
    attn_line_recv,
    attn_plane_send,
    attn_plane_recv,
    keyval_send,
    keyval_recv,
    rows,
    rows_send,
    rows_recv,
    rows_sem,
    attn_full,
    normed_out,
    lin,
    query_out,
    attended,
    branch_out,
    middle_out,
    out_sem,
):
    dp, ctx, core = places()
    x_dev, y_dev, far_dev, core_dev = plane_partners()
    plane = ((dp, ctx, core), x_dev, y_dev, far_dev)
    f32, bf16 = jnp.float32, jnp.bfloat16
    row_count, width = tokens.shape
    half = row_count // 2
    owned = attn_pack.shape[0]
    behind = keyval.shape[1] - row_count
    next_dev = (dp, ctx + 1, core)
    enter(n_dp, True)

    def remote(source, target, send, recv, device):
        return pltpu.make_async_remote_copy(
            src_ref=source, dst_ref=target, send_sem=send, recv_sem=recv, device_id=device,
            device_id_type=MESH,
        )

    def line_block(way, step, k):
        origin = dp - step if way == 0 else dp + step
        return origin * 4 + plane[k][1]

    def can_take(way, step):
        return dp >= step if way == 0 else dp <= n_dp - 1 - step

    def can_give(way):
        return dp < n_dp - 1 if way == 0 else dp > 0

    def line_dev(way):
        return (dp + 1, ctx, core) if way == 0 else (dp - 1, ctx, core)

    def mlp_hop(way, step, k):
        block = mlp_full.at[line_block(way, step, k)]
        index = (way * n_dp + step) * 4 + k
        return remote(block, block, mlp_line_send.at[index], mlp_line_recv.at[index], line_dev(way))

    def mlp_came(way, step, k):
        block = mlp_full.at[line_block(way, step, k)]
        index = (way * n_dp + step - 1) * 4 + k
        return remote(block, block, mlp_line_send.at[index], mlp_line_recv.at[index], line_dev(way))

    def attn_hop(way, step):
        block = slots.at[line_block(way, step, 0)]
        index = way * n_dp + step
        return remote(block, block, attn_line_send.at[index], attn_line_recv.at[index], line_dev(way))

    def attn_came(way, step):
        block = slots.at[line_block(way, step, 0)]
        index = way * n_dp + step - 1
        return remote(block, block, attn_line_send.at[index], attn_line_recv.at[index], line_dev(way))

    def each(step, act, give):
        for way in range(2):
            if give:
                fits = can_give(way) & can_take(way, step) if step else can_give(way)
            else:
                fits = can_take(way, step)
            pl.when(fits)(functools.partial(act, way))

    def attn_plane(way, step, side, came=False):
        from_k = {1: 0, 2: 0, 3: 1 if step % 2 == 0 else 2}[side]
        device = {1: x_dev, 2: y_dev, 3: y_dev if step % 2 == 0 else x_dev}[side]
        block = slots.at[line_block(way, step, side if came else from_k)]
        index = (way * n_dp + step) * 4 + side
        return remote(block, block, attn_plane_send.at[index], attn_plane_recv.at[index], device)

    pending = []

    def give(source, target):
        copy = pltpu.make_async_copy(source, target, out_sem.at[len(pending)])
        copy.start()
        pending.append(copy)

    def first_hop(way, source, blocks, send, recv):
        return remote(source, blocks.at[dp * 4 + ctx], send, recv, line_dev(way))

    def attn_first(way):
        index = way * n_dp
        return first_hop(
            way, attn_pack, slots, attn_line_send.at[index], attn_line_recv.at[index]
        )

    def mlp_own(way):
        index = way * n_dp * 4
        return first_hop(
            way, mlp_pack.at[ctx], mlp_full, mlp_line_send.at[index], mlp_line_recv.at[index]
        )

    def attn_near(side):
        return remote(
            attn_pack,
            slots.at[dp * 4 + ctx],
            attn_plane_send.at[side],
            attn_plane_recv.at[side],
            plane[side],
        )

    own_attn = pltpu.make_async_copy(attn_pack, slots.at[dp * 4 + ctx], own_sem.at[0])
    own_mlp = pltpu.make_async_copy(mlp_pack.at[ctx], mlp_full.at[dp * 4 + ctx], own_sem.at[1])
    own_attn.start()
    own_mlp.start()
    each(0, lambda way: attn_first(way).start(), True)
    for side in (1, 2):
        attn_near(side).start()
    each(0, lambda way: mlp_own(way).start(), True)

    def mlp_plane(k, came=False):
        return remote(
            mlp_pack.at[plane[k][1]],
            mlp_full.at[dp * 4 + (plane[k][1] if came else ctx)],
            mlp_plane_send.at[k],
            mlp_plane_recv.at[k],
            plane[k],
        )

    for k in (1, 2):
        mlp_plane(k).start()

    def came(way, step):
        attn_came(way, step).wait_recv()

    def hand_on(way, step):
        for side in (1, 2):
            attn_plane(way, step, side).start()

    order = [(0, 0)] + [(way, step) for step in range(1, n_dp) for way in range(2)]

    def relay(way, step):
        for side in (1, 2):
            attn_plane(way, step, side, True).wait_recv()
        attn_plane(way, step, 3).start()

    def relayed(way, step):
        attn_plane(way, step, 3, True).wait_recv()

    def where_held(way, step, act):
        if step:
            pl.when(can_take(way, step))(lambda: act(way, step))
        else:
            act(way, step)

    def mlp_first(k):
        mlp_plane(k, True).wait_recv()
        each(0, lambda way: mlp_hop(way, 0, k).start(), True)

    def mlp_next(step, k):
        each(step, lambda way: mlp_came(way, step, k).wait_recv(), False)
        if step < n_dp - 1:
            each(step, lambda way: mlp_hop(way, step, k).start(), True)

    events = [functools.partial(mlp_first, k) for k in (1, 2, 3)] + [
        functools.partial(mlp_next, step, k) for step in range(1, n_dp) for k in range(4)
    ]
    events.reverse()

    def move(count):
        for _ in range(min(count, len(events))):
            events.pop()()

    own_attn.wait()
    for step in range(1, n_dp):
        each(step, lambda way: came(way, step), False)
        each(step, lambda way: attn_hop(way, step).start(), True)
        each(step, lambda way: hand_on(way, step), False)
        if step == 1:
            mlp_plane(3).start()
        if step <= 3:
            move(1)
    if n_dp == 1:
        mlp_plane(3).start()
    move(max(0, 4 - n_dp) + 2)
    for way, step in order:
        where_held(way, step, relay)
    move(1)
    for way, step in order:
        where_held(way, step, relayed)
    move(1)

    for block in range(n_dp * 4):
        wide_slots[block * owned : (block + 1) * owned, :] = slots[block].astype(f32)

    def narrow(first, size, carry):
        at = pl.ds(first, size)
        attn_full[at] = wide_slots[at].astype(bf16)
        return carry

    in_rows(width, narrow, 0)
    give(attn_full, attn_full_out)
    pick = lax.broadcasted_iota(jnp.int32, (8, 128), 0) == lax.broadcasted_iota(
        jnp.int32, (8, 128), 1
    )
    small = contract_columns(pick.astype(f32).astype(bf16), attn_full[:, 1280:1408])
    gain_rows[...] = small
    row_of = lax.broadcasted_iota(jnp.int32, (width, HD), 0)
    head_of = lax.broadcasted_iota(jnp.int32, (width, HD), 1)
    shift = owned_heads.bit_length() - 1
    chosen = row_of == (head_of >> shift) * owned + (head_of & (owned_heads - 1))
    heads = jnp.dot(
        small.astype(bf16), chosen.astype(f32).astype(bf16), preferred_element_type=f32
    )
    head_rows[...] = heads

    def normalize(first, size, carry):
        at = pl.ds(first, size)
        values = tokens[at].astype(f32)
        normed_out[at] = (values * scale_of(values) * gain_rows[0:1]).astype(bf16)
        return carry

    in_rows(row_count, normalize, 0)

    def project(start, size):
        lin[:, pl.ds(start, size)] = jnp.dot(
            normed_out[...], attn_full[:, pl.ds(start, size)], preferred_element_type=f32
        )

    in_columns(3 * HD, project)
    give(normed_out, normed_out_out)
    give(lin, lin_out)

    def turn_keyval(first, size, carry):
        at = pl.ds(first, size)
        values = lin[at, 2 * HD : 3 * HD]
        keys = turned(values * scale_of(values) * head_rows[5:6], cosine[at], sine[at])
        mine = jnp.where(core == 0, keys, values).astype(bf16)
        keyval[core, pl.ds(pl.multiple_of(first + behind, 64), size)] = mine
        return carry

    in_rows(row_count, turn_keyval, 0)
    own_rows, last_rows = pl.ds(behind, row_count), pl.ds(row_count, behind)
    past_rows = pl.ds(0, behind)

    def to_core(came=False):
        block = keyval.at[1 - core if came else core, own_rows]
        return remote(block, block, keyval_send.at[0], keyval_recv.at[0], core_dev)

    def past_to_core(came=False):
        block = keyval.at[1 - core if came else core, past_rows]
        return remote(block, block, keyval_send.at[2], keyval_recv.at[2], core_dev)

    to_next = remote(
        keyval.at[core, last_rows],
        keyval.at[core, past_rows],
        keyval_send.at[1],
        keyval_recv.at[1],
        next_dev,
    )
    pl.when(ctx < 3)(to_next.start)
    to_core().start()

    def turn_query(first, size, carry):
        at = pl.ds(first, size)
        for head in range(2):
            values = lin[at, head * HD : (head + 1) * HD]
            normal = values * scale_of(values) * head_rows[4:5]
            query_out[head, at] = turned(normal, cosine[at], sine[at]).astype(bf16)
        return carry

    in_rows(row_count, turn_query, 0)
    give(query_out, query_out_out)

    @pl.when(ctx > 0)
    def _():
        to_next.wait_recv()
        past_to_core().start()
        past_to_core(True).wait_recv()

    @pl.when(ctx == 0)
    def _():
        keyval[:, 0:behind] = jnp.zeros((2, behind, HD), bf16)

    to_core(True).wait_recv()

    block_rows = 256
    reach = block_rows + behind

    def attend(first, head):
        at = pl.ds(first, block_rows)
        near = pl.ds(first, reach)
        scores = contract_columns(query_out[head, at], keyval[0, near]) * HD ** (-0.5)
        key_at = first + lax.broadcasted_iota(jnp.int32, (block_rows, reach), 1)
        query_at = first + behind + lax.broadcasted_iota(jnp.int32, (block_rows, reach), 0)
        scores = jnp.where((key_at >= lowest[at]) & (key_at <= query_at), scores, -1e30)
        row_max = jnp.max(scores, axis=1, keepdims=True)
        values = jnp.exp(scores - row_max)
        row_total = jnp.sum(values, axis=1, keepdims=True)
        probs = (values / row_total).astype(bf16)
        log_total[head, at] = row_max + jnp.log(row_total)
        out = jnp.dot(probs, keyval[1, near], preferred_element_type=f32)
        attended[at, head * HD : (head + 1) * HD] = out.astype(bf16)

    for block in range(row_count // block_rows):
        for head in range(2):
            attend(block * block_rows, head)
    give(attended, attended_out)
    give(keyval, keyval_out)
    move(2)

    def outward(start, size):
        partial[:, pl.ds(start, size)] = contract_columns(
            attended[...], attn_full[pl.ds(start, size), 3 * HD : 5 * HD]
        )

    in_columns(width, outward)

    def give_half(first, size, carry):
        at = pl.ds(pl.multiple_of((1 - core) * half + first, 64), size)
        core_send[pl.ds(first, size)] = partial[at].astype(bf16)
        return carry

    in_rows(half, give_half, 0)
    exchange = remote(core_send, core_take, keyval_send.at[3], keyval_recv.at[3], core_dev)
    exchange.start()
    move(1)
    exchange.wait_recv()

    def finish(first, size, carry):
        at = pl.ds(first, size)
        whole_at = pl.ds(pl.multiple_of(core * half + first, 64), size)
        branch = partial[whole_at] + core_take[at].astype(f32)
        branch_out[at] = branch
        middle = tokens[whole_at].astype(f32) + branch * scale_of(branch) * gain_rows[1:2]
        middle_out[at] = middle
        rows[0, 0, at] = (middle * scale_of(middle) * gain_rows[2:3]).astype(bf16)
        return carry

    in_rows(half, finish, 0)

    give(branch_out, branch_out_out)
    give(middle_out, middle_out_out)

    def remote_rows(source, target, index, device):
        return remote(source, target, rows_send.at[index], rows_recv.at[index], device)

    gather = gather_copies(remote_rows, rows, 0)
    outs = [
        pltpu.make_async_copy(rows.at[step], rows_out.at[step], rows_sem.at[step])
        for step in range(4)
    ]
    for step in range(4):
        gather_step(gather, step)
        outs[step].start()
        if step == 0:
            move(1)
    move(len(events))
    for copy in gather:
        copy.wait_send()
    for copy in outs + pending + [own_mlp]:
        copy.wait()

    exchange.wait_send()
    to_core().wait_send()
    pl.when(ctx < 3)(to_next.wait_send)
    pl.when(ctx > 0)(past_to_core().wait_send)
    for k in (1, 2, 3):
        mlp_plane(k).wait_send()
    each(0, lambda way: attn_first(way).wait_send(), True)
    each(0, lambda way: mlp_own(way).wait_send(), True)
    for step in range(n_dp - 1):
        if step:
            each(step, lambda way: attn_hop(way, step).wait_send(), True)
        for k in range(4):
            if step or k:
                each(step, lambda way: mlp_hop(way, step, k).wait_send(), True)

    def left(way, step):
        for side in (1, 2, 3):
            if step or side == 3:
                attn_plane(way, step, side).wait_send()
            else:
                attn_near(side).wait_send()

    for way, step in order:
        where_held(way, step, left)


def attend_call(n_dp, owned_heads, behind, tokens, cosine, sine, lowest, attn_pack, mlp_pack):
    row_count, width = tokens.shape
    half = row_count // 2
    owned, attn_cols = attn_pack.shape
    blocks = n_dp * 4
    f32, bf16 = jnp.float32, jnp.bfloat16
    vmem = pl.BlockSpec(memory_space=pltpu.VMEM)
    anywhere = pl.BlockSpec(memory_space=pl.ANY)

    def array(dtype, *shape):
        return jax.ShapeDtypeStruct(shape, dtype)

    dma = pltpu.SemaphoreType.DMA
    return pl.pallas_call(
        functools.partial(attend_kernel, n_dp, owned_heads),
        out_shape=(
            array(bf16, blocks, owned, mlp_pack.shape[2]),
            array(f32, 8, width),
            array(f32, 8, HD),
            array(f32, 2, row_count, 1),
            array(bf16, width, attn_cols),
            array(bf16, row_count, width),
            array(f32, row_count, 3 * HD),
            array(bf16, 2, row_count, HD),
            array(bf16, 2, behind + row_count, HD),
            array(bf16, row_count, 2 * HD),
            array(f32, half, width),
            array(f32, half, width),
            array(bf16, 4, 2, half, width),
        ),
        in_specs=[vmem] * 4 + [anywhere] * 2,
        out_specs=(anywhere, vmem, vmem, vmem) + (anywhere,) * 9,
        scratch_shapes=[
            pltpu.VMEM((blocks, owned, attn_cols), bf16),
            pltpu.VMEM((width, attn_cols), f32),
            pltpu.VMEM((2, behind + row_count, HD), bf16),
            pltpu.VMEM((row_count, width), f32),
            pltpu.VMEM((half, width), bf16),
            pltpu.VMEM((half, width), bf16),
            dma((2,)),
            dma((4,)),
            dma((4,)),
            dma((8 * n_dp,)),
            dma((8 * n_dp,)),
            dma((2 * n_dp,)),
            dma((2 * n_dp,)),
            dma((8 * n_dp,)),
            dma((8 * n_dp,)),
            dma((4,)),
            dma((4,)),
            pltpu.VMEM((4, 2, half, width), bf16),
            dma((10,)),
            dma((10,)),
            dma((4,)),
            pltpu.VMEM((width, attn_cols), bf16),
            pltpu.VMEM((row_count, width), bf16),
            pltpu.VMEM((row_count, 3 * HD), f32),
            pltpu.VMEM((2, row_count, HD), bf16),
            pltpu.VMEM((row_count, 2 * HD), bf16),
            pltpu.VMEM((half, width), f32),
            pltpu.VMEM((half, width), f32),
            dma((8,)),
        ],
        compiler_params=pltpu.CompilerParams(
            collective_id=1, has_side_effects=True, vmem_limit_bytes=60 * 2**20
        ),
        cost_estimate=pl.CostEstimate(
            flops=4 * 10**9, bytes_accessed=30 * 2**20, transcendentals=2 * 10**6
        ),
        name="attend",
    )(tokens, cosine, sine, lowest, attn_pack, mlp_pack)


def mlp_kernel(
    rows_in,
    middle,
    cotangent,
    gain_rows,
    weights_in,
    result_out,
    back_sum,
    gain_sum,
    weights_out,
    result,
    rows,
    grads,
    hidden,
    pair,
    weights,
    total,
    waiting,
    core_send,
    core_take,
    plane_send,
    plane_take,
    send_sem,
    recv_sem,
    load_sem,
    out_sem,
):
    half, width = middle.shape
    h = half // 2
    hid = hidden.shape[2]
    step_rows = 2 * half
    part_a, part_b = pl.ds(0, h), pl.ds(h, h)
    x_dev, y_dev, _, core_dev = plane_partners()
    core = lax.axis_index("tensor")
    gain = gain_rows.at[pl.ds(3, 1)]
    f32, bf16 = jnp.float32, jnp.bfloat16

    loads = [pltpu.make_async_copy(weights_in, weights, load_sem.at[4])] + [
        pltpu.make_async_copy(rows_in.at[step], rows.at[step], load_sem.at[step])
        for step in range(4)
    ]
    for load in (loads[0], loads[4], loads[3], loads[2], loads[1]):
        load.start()
    enter(1, False)

    def remote(source, target, index, device):
        return pltpu.make_async_remote_copy(
            src_ref=source,
            dst_ref=target,
            send_sem=send_sem.at[index],
            recv_sem=recv_sem.at[index],
            device_id=device,
            device_id_type=MESH,
        )

    def scatter_copies(base):
        return [
            remote(plane_send.at[0, part_a], plane_take.at[0, part_a], base, y_dev),
            remote(plane_send.at[0, part_b], plane_take.at[0, part_b], base + 1, x_dev),
            remote(plane_send.at[1, part_a], plane_take.at[1, part_a], base + 2, y_dev),
            remote(plane_send.at[1, part_b], plane_take.at[1, part_b], base + 3, x_dev),
            remote(plane_send.at[2, part_a], plane_take.at[2, part_a], base + 4, x_dev),
            remote(plane_send.at[2, part_b], plane_take.at[2, part_b], base + 5, y_dev),
        ] + [
            remote(core_send.at[step % 2], core_take.at[step], base + 6 + step, core_dev)
            for step in range(4)
        ]

    def scatter_step(copies, step, before, left, first):
        kept = (total, waiting, back_sum, back_sum)[step]
        slot = core_send.at[step % 2]
        if before is not None:
            copies[6 + before].wait_send()

        def part(rows, start, size):
            right = weights[pl.ds(start, size), first : first + left.shape[2]]
            return contract_columns(left[step, rows], right)

        def give(start, size):
            slot[:, pl.ds(start, size)] = part(pl.ds(half, half), start, size).astype(bf16)

        def keep(start, size):
            kept[:, pl.ds(start, size)] = part(pl.ds(0, half), start, size)

        in_columns(width, give)
        copies[6 + step].start()
        in_columns(width, keep)

    def scatter_rest(copies, step):
        kept = (total, waiting, back_sum, back_sum)[step]
        copies[6 + step].wait_recv()
        summed = kept[...] + core_take[step].astype(f32)
        if step < 2:
            kept[...] = summed
        else:
            plane_send[step - 2] = summed.astype(bf16)
            copies[2 * step - 4].start()
            copies[2 * step - 3].start()

    def scatter_end(copies):
        copies[2].wait_recv()
        copies[3].wait_recv()
        plane_send[2] = (waiting[...] + plane_take[1].astype(f32)).astype(bf16)
        copies[4].start()
        copies[5].start()

    def scatter_total(at):
        return total[at] + plane_take[0, at].astype(f32) + plane_take[2, at].astype(f32)

    def scatter_wait(copies):
        for index in (0, 1, 4, 5):
            copies[index].wait_recv()

    def sent(copies):
        for copy in copies:
            copy.wait_send()

    scatter = scatter_copies(0)
    loads[0].wait()
    for step in (3, 2, 1, 0):
        loads[1 + step].wait()

        def activate(start, size):
            def lin(first):
                return jnp.dot(
                    rows[step].reshape(step_rows, width),
                    weights[:, pl.ds(pl.multiple_of(first + start, 128), size)],
                    preferred_element_type=f32,
                )

            gate, up = lin(0), lin(hid)
            square = gate * gate
            chance = 0.5 + 0.5 * jnp.tanh(gate * (GELU_SCALE + GELU_SCALE * 0.044715 * square))
            gelu = gate * chance
            slope = chance + gelu * (1.0 - chance) * (
                2 * GELU_SCALE + 6 * GELU_SCALE * 0.044715 * square
            )
            hidden[step, :, pl.ds(start, size)] = (gelu * up).astype(bf16)
            pair[step, :, pl.ds(start, size)] = (slope * up).astype(bf16)
            pair[step, :, pl.ds(pl.multiple_of(hid + start, 128), size)] = gelu.astype(bf16)

        in_columns(hid, activate)
        scatter_step(scatter, step, step + 2 if step < 2 else None, hidden, 2 * hid)
        scatter_rest(scatter, step)
        if step == 1:
            scatter_end(scatter)
    scatter_wait(scatter)
    sent(scatter[:8])

    def norm_rows(first, size, gain_total):
        at = pl.ds(first, size)
        raw = scatter_total(at)
        scale = lax.rsqrt(jnp.mean(raw * raw, axis=1, keepdims=True) + norm_eps)
        normal = raw * scale
        result[at] = (middle[at] + normal * gain[...]).astype(bf16)
        cotangents = cotangent[pl.ds(pl.multiple_of(core * half + first, 64), size)].astype(f32)
        scaled = cotangents * gain[...]
        inner = jnp.mean(raw * scaled, axis=1, keepdims=True)
        back = scale * scaled - raw * (scale * scale * scale * inner)
        grads[0, 0, at] = back.astype(bf16)
        return gain_total + jnp.sum(cotangents * normal, axis=0, keepdims=True)

    gain_sum[...] = in_rows(half, norm_rows, jnp.zeros((1, width), f32))

    def result_rows(place):
        return result_out.at[pl.ds(pl.multiple_of(place * half, 64), half)]

    own_result = pltpu.make_async_copy(result, result_rows(core), out_sem.at[2])
    far_result = remote(result, result_rows(core), 30, core_dev)
    own_result.start()
    far_result.start()

    gather = gather_copies(remote, grads, 10)
    scatter = scatter_copies(20)
    for step in range(4):
        gather_step(gather, step)

        def unfold(start, size):
            hidden_grad = jnp.dot(
                grads[step].reshape(step_rows, width),
                weights[:, pl.ds(pl.multiple_of(2 * hid + start, 128), size)],
                preferred_element_type=f32,
            )
            hidden_grad = hidden_grad.astype(bf16)
            for first in (0, hid):
                at = pl.ds(pl.multiple_of(first + start, 128), size)
                pair[step, :, at] = pair[step, :, at] * hidden_grad

        in_columns(hid, unfold)
        if step:
            scatter_rest(scatter, step - 1)
        scatter_step(scatter, step, step - 2 if step >= 2 else None, pair, 0)
    scatter_rest(scatter, 3)
    sent(gather)

    def weigh(first, right):
        def one(i, carry):
            at = pl.ds(pl.multiple_of(i * 384, 128), 384)
            left = (rows if right is pair else grads)[:, :, :, at].reshape(8 * half, 384)
            product = contract_rows(left, right[...].reshape(8 * half, right.shape[2]))
            weights[at, first : first + right.shape[2]] = product.astype(bf16)
            return carry

        lax.fori_loop(0, width // 384, one, 0)
        columns = pl.ds(first, right.shape[2])
        copy = pltpu.make_async_copy(
            weights.at[:, columns], weights_out.at[:, columns], out_sem.at[first // (2 * hid)]
        )
        copy.start()
        return copy

    down_out = weigh(2 * hid, hidden)
    scatter_end(scatter)
    gate_out = weigh(0, pair)
    scatter_wait(scatter)

    def finish_rows(first, size, carry):
        at = pl.ds(first, size)
        back_sum[at] = scatter_total(at)
        return carry

    in_rows(half, finish_rows, 0)
    sent(scatter[:6] + scatter[8:])
    down_out.wait()
    gate_out.wait()
    own_result.wait()
    far_result.wait_send()
    remote(result, result_rows(1 - core), 30, core_dev).wait_recv()


def mlp_call(rows, middle, cotangent, gain_rows, weights):
    half, width = middle.shape
    hid = weights.shape[1] // 3
    count = 8 * half
    f32, bf16 = jnp.float32, jnp.bfloat16
    vmem = pl.BlockSpec(memory_space=pltpu.VMEM)
    anywhere = pl.BlockSpec(memory_space=pl.ANY)
    return pl.pallas_call(
        mlp_kernel,
        out_shape=(
            jax.ShapeDtypeStruct(cotangent.shape, bf16),
            jax.ShapeDtypeStruct((half, width), f32),
            jax.ShapeDtypeStruct((1, width), f32),
            jax.ShapeDtypeStruct((width, 3 * hid), bf16),
        ),
        in_specs=[anywhere, vmem, vmem, vmem, anywhere],
        out_specs=(anywhere, vmem, vmem, anywhere),
        scratch_shapes=[
            pltpu.VMEM((half, width), bf16),
            pltpu.VMEM((4, 2, half, width), bf16),
            pltpu.VMEM((4, 2, half, width), bf16),
            pltpu.VMEM((4, 2 * half, hid), bf16),
            pltpu.VMEM((4, 2 * half, 2 * hid), bf16),
            pltpu.VMEM((width, 3 * hid), bf16),
            pltpu.VMEM((half, width), f32),
            pltpu.VMEM((half, width), f32),
            pltpu.VMEM((2, half, width), bf16),
            pltpu.VMEM((4, half, width), bf16),
            pltpu.VMEM((3, half, width), bf16),
            pltpu.VMEM((3, half, width), bf16),
            pltpu.SemaphoreType.DMA((31,)),
            pltpu.SemaphoreType.DMA((31,)),
            pltpu.SemaphoreType.DMA((5,)),
            pltpu.SemaphoreType.DMA((3,)),
        ],
        compiler_params=pltpu.CompilerParams(
            collective_id=0, has_side_effects=True, vmem_limit_bytes=63 * 2**20
        ),
        cost_estimate=pl.CostEstimate(
            flops=2 * count * width * hid * 9, bytes_accessed=30 * 2**20, transcendentals=count * hid
        ),
        name="feed_forward",
    )(rows, middle, cotangent, gain_rows, weights)


def norm_back(values, gains, grads):
    scale = scale_of(values)
    normal = values * scale
    scaled = grads * gains
    inner = jnp.mean(values * scaled, axis=1, keepdims=True)
    return scale * scaled - values * (scale * scale * scale * inner), grads * normal


def retreat_kernel(
    n_dp,
    line,
    owned_heads,
    back_sum,
    middle,
    branch,
    cotangent_in,
    tokens_in,
    cosine,
    sine,
    lowest,
    gain_rows,
    head_rows,
    gain_three,
    attn_full_in,
    normed_one_in,
    lin_in,
    query_in,
    keyval_in,
    attended_in,
    log_total,
    mlp_grads,
    input_whole,
    gate_reduced,
    down_reduced,
    attn_reduced,
    keyval_reduced,
    input_out,
    line_slots,
    attn_grads,
    attn_blocks,
    attn_plane_take,
    attn_sums,
    attn_slots,
    branch_low,
    attended_grad,
    query_grad,
    lin_grad,
    keyval_grad,
    keyval_send,
    keyval_take,
    past_take,
    partial,
    core_send,
    core_take,
    small_rows,
    small_take,
    line_send_sem,
    line_recv_sem,
    plane_send_sem,
    plane_recv_sem,
    attn_plane_send_sem,
    attn_plane_recv_sem,
    attn_line_send_sem,
    attn_line_recv_sem,
    core_send_sem,
    core_recv_sem,
    load_sem,
    mlp_own,
    cotangent,
    tokens,
    attn_full,
    normed_one,
    lin,
    query,
    keyval,
    attended,
):
    dp, ctx, core = places()
    x_dev, y_dev, far_dev, core_dev = plane_partners()
    plane = ((dp, ctx, core), x_dev, y_dev, far_dev)
    f32, bf16 = jnp.float32, jnp.bfloat16
    row_count, width = tokens.shape
    half = row_count // 2
    owned, hid = mlp_grads.shape[1], mlp_grads.shape[2] // 3
    behind = keyval.shape[1] - row_count
    last_dp = line - 1
    here_dp = dp if line > 1 else 0
    sources = (
        (cotangent_in, cotangent),
        (attn_full_in, attn_full),
        (query_in, query),
        (keyval_in, keyval),
        (mlp_grads, mlp_own),
        (lin_in, lin),
        (attended_in, attended),
        (normed_one_in, normed_one),
        (tokens_in, tokens),
    )
    held = [
        pltpu.make_async_copy(source, target, load_sem.at[3 + index])
        for index, (source, target) in enumerate(sources)
    ]
    loads = [
        pltpu.make_async_copy(
            source,
            attn_grads.at[pl.ds(index * half, half), pl.ds(0, width)],
            load_sem.at[index],
        )
        for index, source in enumerate((middle, branch, back_sum))
    ]
    for load in loads + held:
        load.start()
    enter(n_dp, line > 1)

    def remote(source, target, send, recv, device):
        return pltpu.make_async_remote_copy(
            src_ref=source,
            dst_ref=target,
            send_sem=send,
            recv_sem=recv,
            device_id=device,
            device_id_type=MESH,
        )

    def goal(way, far):
        return dp + far if way == 0 else dp - far

    def has_goal(way, far):
        return dp + far <= last_dp if way == 0 else dp >= far

    def is_first(way):
        return dp == 0 if way == 0 else dp == last_dp

    def not_first(way):
        return dp > 0 if way == 0 else dp < last_dp

    def line_dev(way):
        return (dp + 1, ctx, core) if way == 0 else (dp - 1, ctx, core)

    def slot_of(way, far, k):
        return (way * last_dp + far - 1) * 4 + k

    def own_mlp(place, k):
        return mlp_own[place * 4 + plane[k][1]].astype(f32)

    def first_hop(way, far, k):
        slot = slot_of(way, far, k)
        return remote(
            mlp_grads.at[goal(way, far) * 4 + plane[k][1]],
            line_slots.at[slot],
            line_send_sem.at[slot],
            line_recv_sem.at[slot],
            line_dev(way),
        )

    def next_hop(way, far, k):
        slot = slot_of(way, far, k)
        return remote(
            line_slots.at[slot_of(way, far + 1, k)],
            line_slots.at[slot],
            line_send_sem.at[slot],
            line_recv_sem.at[slot],
            line_dev(way),
        )

    def came(way, far, k):
        slot = slot_of(way, far, k)
        block = line_slots.at[slot]
        remote(
            block, block, line_send_sem.at[slot], line_recv_sem.at[slot], line_dev(way)
        ).wait_recv()

    turn = (3, 1, 2, 0)

    def start_first(blocks):
        def start(way):
            for far, k in blocks:
                first_hop(way, far, k).start()

        for way in range(2):
            if line > 1:
                pl.when(is_first(way))(functools.partial(start, way))

    start_first([(far, k) for far in range(last_dp, 1, -1) for k in turn])

    def pass_on(way, far, k):
        came(way, far + 1, k)
        slot = slot_of(way, far + 1, k)
        line_slots[slot] = (line_slots[slot].astype(f32) + own_mlp(goal(way, far), k)).astype(bf16)
        next_hop(way, far, k).start()

    def mlp_step(far, k):
        for way in range(2):
            pl.when(not_first(way) & has_goal(way, far))(functools.partial(pass_on, way, far, k))

    parts = ((gate_reduced, pl.ds(0, 2 * hid)), (down_reduced, pl.ds(2 * hid, hid)))

    def to_owner(k, came=False):
        place = plane[k][1] if came else ctx
        return [
            remote(
                line_slots.at[k, :, columns],
                target.at[place],
                plane_send_sem.at[2 * k + index],
                plane_recv_sem.at[2 * k + index],
                plane[k],
            )
            for index, (target, columns) in enumerate(parts)
        ]

    own_done = [
        pltpu.make_async_copy(line_slots.at[0, :, columns], target.at[ctx], plane_send_sem.at[index])
        for index, (target, columns) in enumerate(parts)
    ]

    def mlp_last(k):
        if line > 1:
            for way in range(2):
                pl.when(not_first(way))(functools.partial(came, way, 1, k))
        total = own_mlp(here_dp, k)
        for way in range(2):
            if line > 1:
                arrived = line_slots[slot_of(way, 1, k)].astype(f32)
                total = total + jnp.where(not_first(way), arrived, 0.0)
        line_slots[k] = total.astype(bf16)
        for copy in to_owner(k) if k else own_done:
            copy.start()

    events = [
        functools.partial(mlp_step, far, k) for far in range(line - 2, 0, -1) for k in turn
    ] + [functools.partial(mlp_last, k) for k in turn]
    events.reverse()

    def move(count):
        for _ in range(min(count, len(events))):
            events.pop()()

    for load in loads + held[:1]:
        load.wait()

    def loaded(index, first, size):
        return attn_grads[pl.ds(pl.multiple_of(first + index * half, 64), size), 0:width]

    def norms(first, size, carry):
        at = pl.ds(first, size)
        part, gain_two = norm_back(loaded(0, first, size), gain_rows[2:3], loaded(2, first, size))
        whole_at = pl.ds(pl.multiple_of(core * half + first, 64), size)
        middle_grad = cotangent[whole_at].astype(f32) + part
        input_out[at] = middle_grad
        grad, gain_one = norm_back(loaded(1, first, size), gain_rows[1:2], middle_grad)
        branch_low[whole_at] = grad.astype(bf16)
        return (
            carry[0] + jnp.sum(gain_one, axis=0, keepdims=True),
            carry[1] + jnp.sum(gain_two, axis=0, keepdims=True),
        )

    nothing = jnp.zeros((1, width), f32)
    small_rows[...] = jnp.zeros_like(small_rows)
    gain_one, gain_two = in_rows(half, norms, (nothing, nothing))
    small_rows[1:2] = gain_one
    small_rows[2:3] = gain_two
    small_rows[3:4] = gain_three[...]

    def halves(came):
        rows = pl.ds(pl.multiple_of((1 - core if came else core) * half, 64), half)
        return remote(
            branch_low.at[rows], branch_low.at[rows], core_send_sem.at[0], core_recv_sem.at[0], core_dev
        )

    halves(False).start()
    halves(True).wait_recv()

    def inward(start, size):
        grad = jnp.dot(
            branch_low[...],
            attn_full[:, pl.ds(pl.multiple_of(3 * HD + start, 128), size)],
            preferred_element_type=f32,
        )
        attended_grad[:, pl.ds(start, size)] = grad.astype(bf16)

    held[1].wait()
    in_columns(2 * HD, inward)

    block_rows = 256
    reach = block_rows + behind
    keyval_grad[...] = jnp.zeros_like(keyval_grad)
    for load in held[2:5]:
        load.wait()

    def retreat(first, head):
        at = pl.ds(first, block_rows)
        near = pl.ds(first, reach)
        columns = slice(head * HD, (head + 1) * HD)
        scores = contract_columns(query[head, at], keyval[0, near]) * HD ** (-0.5)
        key_at = first + lax.broadcasted_iota(jnp.int32, (block_rows, reach), 1)
        query_at = first + behind + lax.broadcasted_iota(jnp.int32, (block_rows, reach), 0)
        scores = jnp.where((key_at >= lowest[at]) & (key_at <= query_at), scores, -1e30)
        probs = jnp.exp(scores - log_total[head, at])
        grads = attended_grad[at, columns]
        probs_grad = contract_columns(grads, keyval[1, near])
        delta = jnp.sum(probs * probs_grad, axis=1, keepdims=True)
        score_grad = (probs * (probs_grad - delta)).astype(bf16)
        query_grad[at, columns] = (
            jnp.dot(score_grad, keyval[0, near], preferred_element_type=f32) * HD ** (-0.5)
        )
        keyval_grad[0, near] += contract_rows(score_grad, query[head, at]) * HD ** (-0.5)
        keyval_grad[1, near] += contract_rows(probs.astype(bf16), grads)

    for block in range(row_count // block_rows):
        for head in range(2):
            retreat(block * block_rows, head)
    move(2)

    keyval_send[0] = keyval_grad[1 - core].astype(bf16)
    to_core = remote(
        keyval_send.at[0], keyval_take, core_send_sem.at[1], core_recv_sem.at[1], core_dev
    )
    to_core.start()

    def query_rows(first, size, carry):
        at = pl.ds(first, size)
        total = carry
        for head in range(2):
            columns = slice(head * HD, (head + 1) * HD)
            grads = turned(query_grad[at, columns], cosine[at], -sine[at])
            grad, gain = norm_back(lin[at, columns], head_rows[4:5], grads)
            lin_grad[at, columns] = grad.astype(bf16)
            total = total + jnp.sum(gain, axis=0, keepdims=True)
        return total

    for load in held[5:]:
        load.wait()
    head_zero = in_rows(row_count, query_rows, jnp.zeros((1, HD), f32))
    move(1)
    to_core.wait_recv()
    keyval_grad[core] = keyval_grad[core] + keyval_take[...].astype(f32)
    keyval_send[1, 0:behind] = keyval_grad[core, 0:behind].astype(bf16)
    to_past = remote(
        keyval_send.at[1, pl.ds(0, behind)],
        past_take,
        core_send_sem.at[2],
        core_recv_sem.at[2],
        (dp, ctx - 1, core),
    )
    pl.when(ctx > 0)(to_past.start)

    def outward(start, size):
        attn_grads[0:width, pl.ds(pl.multiple_of(3 * HD + start, 128), size)] = contract_rows(
            branch_low[...], attended[:, pl.ds(start, size)]
        )

    in_columns(2 * HD, outward)

    @pl.when(ctx < 3)
    def _():
        to_past.wait_recv()
        late = pl.ds(row_count, behind)
        keyval_grad[core, late] = keyval_grad[core, late] + past_take[...].astype(f32)

    def keyval_rows(first, size, carry):
        at = pl.ds(first, size)
        values = keyval_grad[core, pl.ds(pl.multiple_of(first + behind, 64), size)]
        grads = turned(values, cosine[at], -sine[at])
        grad, gain = norm_back(lin[at, 2 * HD : 3 * HD], head_rows[5:6], grads)
        lin_grad[at, 2 * HD : 3 * HD] = jnp.where(core == 0, grad, values).astype(bf16)
        return carry + jnp.sum(gain, axis=0, keepdims=True)

    head_one = in_rows(row_count, keyval_rows, jnp.zeros((1, HD), f32))
    head_one = jnp.where(core == 0, head_one, 0.0)

    def weigh(start, size):
        attn_grads[0:width, pl.ds(start, size)] = contract_rows(
            normed_one[...], lin_grad[:, pl.ds(start, size)]
        )

    in_columns(3 * HD, weigh)
    move(1)
    start_first([(1, k) for k in turn[:2]])

    def back(start, size):
        columns = pl.ds(start, size)
        product = contract_columns(lin_grad[...], attn_full[columns, 0 : 3 * HD])
        first, second = product[:half], product[half:]
        partial[:, columns] = jnp.where(core == 0, first, second)
        core_send[:, columns] = jnp.where(core == 0, second, first).astype(bf16)

    in_columns(width, back)
    exchange = remote(core_send, core_take, core_send_sem.at[3], core_recv_sem.at[3], core_dev)
    exchange.start()
    exchange.wait_recv()

    def finish(first, size, carry):
        at = pl.ds(first, size)
        whole_at = pl.ds(pl.multiple_of(core * half + first, 64), size)
        grads = partial[at] + core_take[at].astype(f32)
        part, gain = norm_back(tokens[whole_at].astype(f32), gain_rows[0:1], grads)
        input_out[at] = input_out[at] + part
        return carry + jnp.sum(gain, axis=0, keepdims=True)

    small_rows[0:1] = in_rows(half, finish, nothing)

    def input_rows(place):
        return input_whole.at[pl.ds(pl.multiple_of(place * half, 64), half)]

    own_input = pltpu.make_async_copy(input_out, input_rows(core), load_sem.at[0])
    own_input.start()

    def far_input(place):
        return remote(
            input_out, input_rows(place), core_send_sem.at[5], core_recv_sem.at[5], core_dev
        )

    far_input(core).start()

    row_of = lax.broadcasted_iota(jnp.int32, (width, HD), 0)
    head_of = lax.broadcasted_iota(jnp.int32, (width, HD), 1)
    shift = owned_heads.bit_length() - 1
    chosen = row_of == (head_of >> shift) * owned + (head_of & (owned_heads - 1))
    heads = jnp.concatenate([head_zero, head_one, jnp.zeros((6, HD), f32)], axis=0)
    spread = contract_columns(heads.astype(bf16), chosen.astype(f32).astype(bf16))
    small_rows[4:6] = spread[0:2]
    smalls = remote(
        small_rows.at[pl.ds(0, 8)], small_take, core_send_sem.at[4], core_recv_sem.at[4], core_dev
    )
    smalls.start()
    smalls.wait_recv()
    smalls.wait_send()
    small_rows[0:8] = small_rows[0:8] + small_take[...]
    attn_grads[0:width, 5 * HD : 5 * HD + 128] = small_rows[...].T

    for block in range(n_dp * 4):
        attn_blocks[block] = attn_grads[block * owned : (block + 1) * owned, :].astype(bf16)

    def attn_plane(k, place):
        index = (k - 1) * n_dp + place
        return remote(
            attn_blocks.at[place * 4 + plane[k][1]],
            attn_plane_take.at[index],
            attn_plane_send_sem.at[index],
            attn_plane_recv_sem.at[index],
            plane[k],
        )

    for place in range(n_dp):
        for k in (3, 1, 2):
            attn_plane(k, place).start()
    move(len(events) - 4)
    for place in range(n_dp):
        total = attn_blocks[place * 4 + ctx].astype(f32)
        for k in (1, 2, 3):
            attn_plane(k, place).wait_recv()
            total = total + attn_plane_take[(k - 1) * n_dp + place].astype(f32)
        attn_sums[place] = total.astype(bf16)

    def attn_hop(way, far, first):
        source = attn_sums.at[goal(way, far)] if first else attn_slots.at[way * line + far + 1]
        index = way * line + far
        return remote(
            source,
            attn_slots.at[index],
            attn_line_send_sem.at[index],
            attn_line_recv_sem.at[index],
            line_dev(way),
        )

    def attn_came(way, far):
        index = way * line + far
        block = attn_slots.at[index]
        remote(
            block, block, attn_line_send_sem.at[index], attn_line_recv_sem.at[index], line_dev(way)
        ).wait_recv()

    def attn_start(way):
        for far in range(last_dp, 0, -1):
            attn_hop(way, far, True).start()

    def attn_pass(way, far):
        attn_came(way, far + 1)
        index = way * line + far + 1
        total = attn_slots[index].astype(f32) + attn_sums[goal(way, far)].astype(f32)
        attn_slots[index] = total.astype(bf16)
        attn_hop(way, far, False).start()

    for way in range(2):
        if line > 1:
            pl.when(is_first(way))(functools.partial(attn_start, way))
    start_first([(1, k) for k in turn[2:]])
    for far in range(line - 2, 0, -1):
        for way in range(2):
            pl.when(not_first(way) & has_goal(way, far))(functools.partial(attn_pass, way, far))
    move(4)
    if line == 1:
        attn_reduced[...] = attn_sums[...]
    else:
        total = attn_sums[dp].astype(f32)
        for way in range(2):
            pl.when(not_first(way))(functools.partial(attn_came, way, 1))
            arrived = attn_slots[way * line + 1].astype(f32)
            total = total + jnp.where(not_first(way), arrived, 0.0)
        attn_reduced[0] = total.astype(bf16)
        columns = attn_reduced.at[0, :, pl.ds(2 * HD, HD)]
        own_keyval = pltpu.make_async_copy(columns, keyval_reduced.at[core], load_sem.at[1])
        own_keyval.start()

        def far_keyval(place):
            return remote(
                columns, keyval_reduced.at[place], core_send_sem.at[6], core_recv_sem.at[6], core_dev
            )

        far_keyval(core).start()
        far_keyval(core).wait_send()
        far_keyval(1 - core).wait_recv()
        own_keyval.wait()

    for k in (1, 2, 3):
        for copy in to_owner(k, True):
            copy.wait_recv()
        for copy in to_owner(k):
            copy.wait_send()
    for copy in own_done:
        copy.wait()
    own_input.wait()
    far_input(core).wait_send()
    far_input(1 - core).wait_recv()
    halves(False).wait_send()
    to_core.wait_send()
    pl.when(ctx > 0)(to_past.wait_send)
    exchange.wait_send()
    for place in range(n_dp):
        for k in (1, 2, 3):
            attn_plane(k, place).wait_send()

    def first_left(way):
        for far in range(last_dp, 0, -1):
            attn_hop(way, far, True).wait_send()
            for k in turn:
                first_hop(way, far, k).wait_send()

    def left(way, far):
        attn_hop(way, far, False).wait_send()
        for k in turn:
            next_hop(way, far, k).wait_send()

    for way in range(2):
        if line > 1:
            pl.when(is_first(way))(functools.partial(first_left, way))
        for far in range(line - 2, 0, -1):
            pl.when(not_first(way) & has_goal(way, far))(functools.partial(left, way, far))


def retreat_call(n_dp, line, owned_heads, *arrays):
    tokens, attn_full, keyval = arrays[4], arrays[11], arrays[15]
    mlp_grads = arrays[18]
    row_count, width = tokens.shape
    half = row_count // 2
    blocks = n_dp * 4
    owned, hid = mlp_grads.shape[1], mlp_grads.shape[2] // 3
    attn_cols = attn_full.shape[1]
    reach = keyval.shape[1]
    behind = reach - row_count
    f32, bf16 = jnp.float32, jnp.bfloat16
    vmem = pl.BlockSpec(memory_space=pltpu.VMEM)
    anywhere = pl.BlockSpec(memory_space=pl.ANY)
    dma = pltpu.SemaphoreType.DMA
    return pl.pallas_call(
        functools.partial(retreat_kernel, n_dp, line, owned_heads),
        out_shape=(
            jax.ShapeDtypeStruct((row_count, width), f32),
            jax.ShapeDtypeStruct((4, owned, 2 * hid), bf16),
            jax.ShapeDtypeStruct((4, owned, hid), bf16),
            jax.ShapeDtypeStruct((n_dp if line == 1 else 1, owned, attn_cols), bf16),
            jax.ShapeDtypeStruct((2, owned, HD), bf16),
        ),
        in_specs=[
            anywhere if index < 5 or 11 <= index <= 16 or index == 18 else vmem
            for index in range(len(arrays))
        ],
        out_specs=(anywhere, anywhere, anywhere, vmem, anywhere),
        scratch_shapes=[
            pltpu.VMEM((half, width), f32),
            pltpu.VMEM((max(8 * (line - 1), 4), owned, 3 * hid), bf16),
            pltpu.VMEM((max(width, 3 * half), attn_cols), f32),
            pltpu.VMEM((blocks, owned, attn_cols), bf16),
            pltpu.VMEM((3 * n_dp, owned, attn_cols), bf16),
            pltpu.VMEM((n_dp, owned, attn_cols), bf16),
            pltpu.VMEM((2 * line, owned, attn_cols), bf16),
            pltpu.VMEM((row_count, width), bf16),
            pltpu.VMEM((row_count, 2 * HD), bf16),
            pltpu.VMEM((row_count, 2 * HD), f32),
            pltpu.VMEM((row_count, 3 * HD), bf16),
            pltpu.VMEM((2, reach, HD), f32),
            pltpu.VMEM((2, reach, HD), bf16),
            pltpu.VMEM((reach, HD), bf16),
            pltpu.VMEM((behind, HD), bf16),
            pltpu.VMEM((half, width), f32),
            pltpu.VMEM((half, width), bf16),
            pltpu.VMEM((half, width), bf16),
            pltpu.VMEM((128, width), f32),
            pltpu.VMEM((8, width), f32),
            dma((8 * line,)),
            dma((8 * line,)),
            dma((8,)),
            dma((8,)),
            dma((4 * n_dp,)),
            dma((4 * n_dp,)),
            dma((2 * line,)),
            dma((2 * line,)),
            dma((7,)),
            dma((7,)),
            dma((12,)),
            pltpu.VMEM(mlp_grads.shape, bf16),
        ]
        + [
            pltpu.VMEM(arrays[index].shape, arrays[index].dtype)
            for index in (3, 4, 11, 12, 13, 14, 15, 16)
        ],
        compiler_params=pltpu.CompilerParams(
            collective_id=2, has_side_effects=True, vmem_limit_bytes=63 * 2**20
        ),
        cost_estimate=pl.CostEstimate(
            flops=10**10, bytes_accessed=40 * 2**20, transcendentals=2 * 10**6
        ),
        name="retreat",
    )(*arrays)


def update_call(wide, passed, small_grads, attn_grads, keyval_grads, gate_grads, down_grads, *states):
    owned = states[0].shape[0]
    cols = states[0].shape[1]
    blocks = down_grads.shape[0]

    def whole(array):
        return pl.BlockSpec(array.shape, lambda i: (0,) * array.ndim)

    def step(state, new, gradient, rate, decay=decay_rate):
        results = adam_step(
            state[0][...], gradient.astype(jnp.float32), state[1][...], state[2][...], rate, decay
        )
        for target, result in zip(new, results):
            target[...] = result

    def kernel(first_in, second_in, small_ref, attn_ref, keyval_ref, gate_ref, down_ref, *refs):
        olds, news, first_out, second_out = refs[:21], refs[21:42], *refs[42:]
        first_out[...] = first_in[...]
        second_out[...] = second_in[...]
        step(olds[9:12], news[9:12], gate_ref[...], D ** (-0.5))
        step(olds[12:15], news[12:15], down_ref[0], FF ** (-0.5))

        @pl.when(pl.program_id(0) == 0)
        def _():
            step(olds[0:3], news[0:3], attn_ref[0, :, 0:cols], D ** (-0.5))
            keyval = jnp.concatenate([keyval_ref[0], keyval_ref[1]], axis=1)
            step(olds[3:6], news[3:6], keyval, D ** (-0.5))
            output = attn_ref[0, :, cols + HD : 2 * cols + HD]
            step(olds[6:9], news[6:9], output, (HQ * HD) ** (-0.5))
            step(olds[15:18], news[15:18], small_ref[0:4], 0.5, 0.0)
            step(olds[18:21], news[18:21], small_ref[4:6, 0 : olds[18].shape[1]], 0.5, 0.0)

    gate_block = pl.BlockSpec((owned, 2, wide), lambda i: (0, 0, i))
    down_block = pl.BlockSpec((owned, wide), lambda i: (0, i))
    state_blocks = [whole(array) for array in states[:9]] + [gate_block] * 3 + [down_block] * 3
    state_blocks += [whole(array) for array in states[15:]]
    passed_blocks = [
        pl.BlockSpec((array.shape[0] // blocks, array.shape[1]), lambda i: (i, 0))
        for array in passed
    ]
    return pl.pallas_call(
        kernel,
        grid=(blocks,),
        in_specs=[
            *passed_blocks,
            whole(small_grads),
            whole(attn_grads),
            whole(keyval_grads),
            gate_block,
            pl.BlockSpec((1, owned, wide), lambda i: (i, 0, 0)),
        ]
        + state_blocks,
        out_specs=tuple(state_blocks + passed_blocks),
        out_shape=tuple(jax.ShapeDtypeStruct(array.shape, array.dtype) for array in states + passed),
        compiler_params=pltpu.CompilerParams(vmem_limit_bytes=63 * 2**20 + 900 * 2**10),
        name="update",
    )(*passed, small_grads, attn_grads, keyval_grads, gate_grads, down_grads, *states)


def on_device(
    tokens,
    out_cotangent,
    lengths,
    norm_gains,
    gain_first,
    gain_second,
    head_gains,
    head_first,
    head_second,
    query_weight,
    query_first,
    query_second,
    keyval_weight,
    keyval_first,
    keyval_second,
    output_weight,
    output_first,
    output_second,
    gate_up,
    gate_first,
    gate_second,
    down_weight,
    down_first,
    down_second,
):
    bf16, f32 = jnp.bfloat16, jnp.float32
    row_count = tokens.shape[0]
    owned = query_weight.shape[0]
    owned_heads = head_gains.shape[0]
    n_dp, n_ctx = lax.axis_size("dp"), lax.axis_size("ctx")
    half_ff = gate_up.shape[2]
    wide = -(-half_ff // (n_ctx * 128)) * 128
    behind = WIN
    ctx_place = lax.axis_index("ctx")
    core_first = lax.axis_index("tensor") == 0
    score_scale = HD ** (-0.5)

    head_columns = jnp.pad(head_gains, ((0, owned - owned_heads), (0, 0)))
    small = jnp.concatenate([norm_gains, head_columns], axis=1).astype(bf16)
    attn_pack = jnp.concatenate(
        [
            query_weight.astype(bf16),
            half_of(keyval_weight, 1).astype(bf16),
            output_weight.astype(bf16),
            jnp.pad(small, ((0, 0), (0, 122))),
        ],
        axis=1,
    )
    cols = query_weight.shape[1]

    def in_parts(array):
        padded = jnp.pad(array.astype(bf16), ((0, 0), (0, n_ctx * wide - half_ff)))
        return padded.reshape(owned, n_ctx, wide)

    mlp_pack = jnp.concatenate(
        [in_parts(gate_up[:, 0]), in_parts(gate_up[:, 1]), in_parts(down_weight)], axis=2
    )
    mlp_pack = jnp.moveaxis(mlp_pack, 1, 0)

    start_row = ctx_place * row_count
    row_index = jnp.arange(row_count, dtype=jnp.int32)
    query_position = token_layout(lengths[0], start_row + row_index)[1]
    query_cosine, query_sine = rope_tables(query_position)
    lowest = jnp.maximum(row_index - query_position + behind, row_index + 1)[:, None]
    (
        mlp_full,
        gain_rows,
        head_rows,
        log_total,
        attn_full,
        normed_one,
        lin,
        query_rot,
        keyval_all,
        attended_low,
        branch_raw,
        middle,
        group_rows,
    ) = attend_call(
        n_dp, owned_heads, behind, tokens, query_cosine, query_sine, lowest, attn_pack, mlp_pack
    )
    result, normed_two_grad, gain_three_part, mlp_grads = mlp_call(
        group_rows,
        middle,
        out_cotangent,
        gain_rows,
        mlp_full.reshape(n_dp * n_ctx * owned, 3 * wide),
    )

    line = n_dp if n_dp <= 4 else 1

    mlp_grads = mlp_grads.reshape(n_dp, n_ctx, owned, 3 * wide)
    if line == 1:
        mlp_grads = lax.psum_scatter(mlp_grads, "dp", scatter_dimension=0, tiled=True)
    mlp_grads = mlp_grads.reshape(line * n_ctx, owned, 3 * wide)
    input_grad, gate_arrived, down_arrived, attn_reduced, keyval_both = retreat_call(
        n_dp,
        line,
        owned_heads,
        normed_two_grad,
        middle,
        branch_raw,
        out_cotangent,
        tokens,
        query_cosine,
        query_sine,
        lowest,
        gain_rows,
        head_rows,
        gain_three_part,
        attn_full,
        normed_one,
        lin,
        query_rot,
        keyval_all,
        attended_low,
        log_total,
        mlp_grads,
    )
    if line == 1:
        attn_reduced = lax.psum_scatter(attn_reduced, "dp", scatter_dimension=0, tiled=True)
        keyval_half = attn_reduced[0, :, cols : cols + HD]
        first, second = jnp.where(core_first, 0, 1), jnp.where(core_first, 1, 0)
        keyval_both = jnp.stack([keyval_half, lax.ppermute(keyval_half, "tensor", [(0, 1), (1, 0)])])
        keyval_both = jnp.stack([keyval_both[first], keyval_both[second]])
    gate_reduced = gate_arrived.reshape(n_ctx, owned, 2, wide)
    gate_reduced = gate_reduced.transpose(1, 2, 0, 3).reshape(owned, 2, n_ctx * wide)
    gate_reduced = lax.optimization_barrier(gate_reduced)
    (
        query_new,
        query_first_new,
        query_second_new,
        keyval_new,
        keyval_first_new,
        keyval_second_new,
        output_new,
        output_first_new,
        output_second_new,
        gate_new,
        gate_first_new,
        gate_second_new,
        down_new,
        down_first_new,
        down_second_new,
        *gains_updated,
        result,
        input_grad,
    ) = update_call(
        wide,
        (result, input_grad),
        attn_reduced[0, :, 2 * cols + HD :].astype(f32).T,
        attn_reduced,
        keyval_both,
        gate_reduced,
        down_arrived,
        query_weight,
        query_first,
        query_second,
        keyval_weight,
        keyval_first,
        keyval_second,
        output_weight,
        output_first,
        output_second,
        gate_up,
        gate_first,
        gate_second,
        down_weight,
        down_first,
        down_second,
        norm_gains.T,
        gain_first.T,
        gain_second.T,
        head_gains.T,
        head_first.T,
        head_second.T,
    )
    (
        gains_new,
        gain_first_new,
        gain_second_new,
        heads_new,
        head_first_new,
        head_second_new,
    ) = (new.T for new in gains_updated)
    return (
        result,
        input_grad,
        gains_new,
        gain_first_new,
        gain_second_new,
        heads_new,
        head_first_new,
        head_second_new,
        query_new,
        query_first_new,
        query_second_new,
        keyval_new,
        keyval_first_new,
        keyval_second_new,
        output_new,
        output_first_new,
        output_second_new,
        gate_new,
        gate_first_new,
        gate_second_new,
        down_new,
        down_first_new,
        down_second_new,
    )


def solution(mesh):
    placed = (
        P(("dp", "ctx"), None),
        P(("dp", "ctx"), None),
        P("dp", None),
        P(("dp", "ctx"), None),
        P(("dp", "ctx"), None),
        P(("dp", "ctx"), None),
        P(("dp", "ctx"), None),
        P(("dp", "ctx"), None),
        P(("dp", "ctx"), None),
        P(("dp", "ctx"), "tensor"),
        P(("dp", "ctx"), "tensor"),
        P(("dp", "ctx"), "tensor"),
        P(("dp", "ctx"), None),
        P(("dp", "ctx"), None),
        P(("dp", "ctx"), None),
        P(("dp", "ctx"), "tensor"),
        P(("dp", "ctx"), "tensor"),
        P(("dp", "ctx"), "tensor"),
        P(("dp", "ctx"), None, "tensor"),
        P(("dp", "ctx"), None, "tensor"),
        P(("dp", "ctx"), None, "tensor"),
        P(("dp", "ctx"), "tensor"),
        P(("dp", "ctx"), "tensor"),
        P(("dp", "ctx"), "tensor"),
    )
    return jax.shard_map(
        on_device,
        mesh=mesh,
        in_specs=placed,
        out_specs=(
            P(("dp", "ctx"), None),
            P(("dp", "ctx"), None),
            P(("dp", "ctx"), None),
            P(("dp", "ctx"), None),
            P(("dp", "ctx"), None),
            P(("dp", "ctx"), None),
            P(("dp", "ctx"), None),
            P(("dp", "ctx"), None),
            P(("dp", "ctx"), "tensor"),
            P(("dp", "ctx"), "tensor"),
            P(("dp", "ctx"), "tensor"),
            P(("dp", "ctx"), None),
            P(("dp", "ctx"), None),
            P(("dp", "ctx"), None),
            P(("dp", "ctx"), "tensor"),
            P(("dp", "ctx"), "tensor"),
            P(("dp", "ctx"), "tensor"),
            P(("dp", "ctx"), None, "tensor"),
            P(("dp", "ctx"), None, "tensor"),
            P(("dp", "ctx"), None, "tensor"),
            P(("dp", "ctx"), "tensor"),
            P(("dp", "ctx"), "tensor"),
            P(("dp", "ctx"), "tensor"),
        ),
        check_vma=False,
    )
```

```python
import functools

import jax
import jax.numpy as jnp
import numpy as np
from jax import lax
from jax.experimental import pallas as pl
from jax.experimental.pallas import tpu as pltpu
from jax.sharding import PartitionSpec as P

D = 1152
HQ = 4
HD = 256
FF = 6912
WIN = 512
STEP = 10


norm_eps = 1e-06
beta_one = 0.9
beta_two = 0.95
adam_eps = 1e-08
decay_rate = 0.1
rope_base = 10000.0
GELU_SCALE = float(np.sqrt(2.0 / np.pi))
MESH = pl.DeviceIdType.MESH


def half_of(array, dim):
    size = array.shape[dim] // 2
    return lax.dynamic_slice_in_dim(array, lax.axis_index("tensor") * size, size, axis=dim)


def contract_rows(left_side, right_side):
    return lax.dot_general(
        left_side, right_side, (((0,), (0,)), ((), ())), preferred_element_type=jnp.float32
    )


def contract_columns(left_side, right_side):
    return lax.dot_general(
        left_side, right_side, (((1,), (1,)), ((), ())), preferred_element_type=jnp.float32
    )


def adam_step(weight_value, gradient, first_moment, second_moment, step_rate, decay_factor):
    first_moment = beta_one * first_moment + (1.0 - beta_one) * gradient
    second_moment = beta_two * second_moment + (1.0 - beta_two) * gradient * gradient
    first_hat = first_moment / (1.0 - beta_one**STEP)
    second_hat = second_moment / (1.0 - beta_two**STEP)
    update = first_hat / (jnp.sqrt(second_hat) + adam_eps)
    return (
        weight_value - step_rate * (update + decay_factor * weight_value),
        first_moment,
        second_moment,
    )


def places():
    return lax.axis_index("dp"), lax.axis_index("ctx"), lax.axis_index("tensor")


def plane_partners():
    dp, ctx, core = places()
    beside = ctx + 1 - 2 * lax.rem(ctx, 2)
    across = lax.rem(ctx + 2, 4)
    return (dp, beside, core), (dp, across, core), (dp, 3 - ctx, core), (dp, ctx, 1 - core)


def enter(n_dp, line):
    dp, ctx, core = places()
    barrier = pltpu.get_barrier_semaphore()

    def greet(device):
        pl.semaphore_signal(barrier, inc=1, device_id=device, device_id_type=MESH)

    for device in plane_partners():
        greet(device)
    if line:
        pl.when(dp < n_dp - 1)(lambda: greet((dp + 1, ctx, core)))
        pl.when(dp > 0)(lambda: greet((dp - 1, ctx, core)))
    ends = jnp.minimum(dp, 1) + jnp.minimum(n_dp - 1 - dp, 1) if line else 0
    pl.semaphore_wait(barrier, 4 + ends)


def in_columns(count, body):
    whole = count // 256

    def one(i, carry):
        body(pl.multiple_of(i * 256, 256), 256)
        return carry

    lax.fori_loop(0, whole, one, 0)
    if count % 256:
        body(whole * 256, count % 256)


def in_rows(count, body, start):
    size = 64

    def one(i, carry):
        return body(pl.multiple_of(i * size, size), size, carry)

    return lax.fori_loop(0, count // size, one, start)


def gather_copies(remote, buffer, base):
    x_dev, y_dev, _, core_dev = plane_partners()
    h = buffer.shape[2] // 2
    part_a, part_b = pl.ds(0, h), pl.ds(h, h)

    def piece(step, side):
        return buffer.at[step, 0, side]

    return [
        remote(piece(0, part_a), piece(1, part_a), base, x_dev),
        remote(piece(0, part_b), piece(1, part_b), base + 1, y_dev),
        remote(piece(0, part_b), piece(2, part_b), base + 2, x_dev),
        remote(piece(0, part_a), piece(2, part_a), base + 3, y_dev),
        remote(piece(1, part_a), piece(3, part_a), base + 4, y_dev),
        remote(piece(1, part_b), piece(3, part_b), base + 5, x_dev),
    ] + [
        remote(buffer.at[step, 0], buffer.at[step, 1], base + 6 + step, core_dev)
        for step in range(4)
    ]


def gather_step(copies, step):
    if step == 0:
        for copy in copies[:4]:
            copy.start()
    elif step == 1:
        copies[0].wait_recv()
        copies[1].wait_recv()
        copies[4].start()
        copies[5].start()
    else:
        copies[2 * step - 2].wait_recv()
        copies[2 * step - 1].wait_recv()
    copies[6 + step].start()
    copies[6 + step].wait_recv()


def turned(values, cosine, sine):
    half_dim = values.shape[-1] // 2
    lower, upper = values[:, :half_dim], values[:, half_dim:]
    return jnp.concatenate([lower * cosine - upper * sine, upper * cosine + lower * sine], axis=1)


def scale_of(values):
    return lax.rsqrt(jnp.mean(values * values, axis=1, keepdims=True) + norm_eps)


def attend_kernel(
    n_dp,
    owned_heads,
    tokens_in,
    lengths,
    inverse,
    attn_pack,
    mlp_pack,
    mlp_full,
    gain_rows,
    head_rows,
    log_total,
    cosine,
    sine,
    lowest,
    attn_full_out,
    normed_out_out,
    lin_out,
    query_out_out,
    keyval_out,
    attended_out,
    branch_out_out,
    middle_out_out,
    rows_out,
    slots,
    wide_slots,
    keyval,
    partial,
    core_send,
    core_take,
    own_sem,
    mlp_plane_send,
    mlp_plane_recv,
    mlp_line_send,
    mlp_line_recv,
    attn_line_send,
    attn_line_recv,
    attn_plane_send,
    attn_plane_recv,
    keyval_send,
    keyval_recv,
    rows,
    rows_send,
    rows_recv,
    rows_sem,
    attn_full,
    normed_out,
    lin,
    query_out,
    attended,
    branch_out,
    middle_out,
    out_sem,
    tokens,
):
    dp, ctx, core = places()
    x_dev, y_dev, far_dev, core_dev = plane_partners()
    plane = ((dp, ctx, core), x_dev, y_dev, far_dev)
    f32, bf16 = jnp.float32, jnp.bfloat16
    row_count, width = tokens.shape
    half = row_count // 2
    owned = attn_pack.shape[0]
    behind = keyval.shape[1] - row_count
    next_dev = (dp, ctx + 1, core)
    enter(n_dp, True)

    def remote(source, target, send, recv, device):
        return pltpu.make_async_remote_copy(
            src_ref=source, dst_ref=target, send_sem=send, recv_sem=recv, device_id=device,
            device_id_type=MESH,
        )

    def line_block(way, step, k):
        origin = dp - step if way == 0 else dp + step
        return origin * 4 + plane[k][1]

    def can_take(way, step):
        return dp >= step if way == 0 else dp <= n_dp - 1 - step

    def can_give(way):
        return dp < n_dp - 1 if way == 0 else dp > 0

    def line_dev(way):
        return (dp + 1, ctx, core) if way == 0 else (dp - 1, ctx, core)

    def mlp_hop(way, step, k):
        block = mlp_full.at[line_block(way, step, k)]
        index = (way * n_dp + step) * 4 + k
        return remote(block, block, mlp_line_send.at[index], mlp_line_recv.at[index], line_dev(way))

    def mlp_came(way, step, k):
        block = mlp_full.at[line_block(way, step, k)]
        index = (way * n_dp + step - 1) * 4 + k
        return remote(block, block, mlp_line_send.at[index], mlp_line_recv.at[index], line_dev(way))

    def attn_hop(way, step):
        block = slots.at[line_block(way, step, 0)]
        index = way * n_dp + step
        return remote(block, block, attn_line_send.at[index], attn_line_recv.at[index], line_dev(way))

    def attn_came(way, step):
        block = slots.at[line_block(way, step, 0)]
        index = way * n_dp + step - 1
        return remote(block, block, attn_line_send.at[index], attn_line_recv.at[index], line_dev(way))

    def each(step, act, give):
        for way in range(2):
            if give:
                fits = can_give(way) & can_take(way, step) if step else can_give(way)
            else:
                fits = can_take(way, step)
            pl.when(fits)(functools.partial(act, way))

    def attn_plane(way, step, side, came=False):
        from_k = {1: 0, 2: 0, 3: 1 if step % 2 == 0 else 2}[side]
        device = {1: x_dev, 2: y_dev, 3: y_dev if step % 2 == 0 else x_dev}[side]
        block = slots.at[line_block(way, step, side if came else from_k)]
        index = (way * n_dp + step) * 4 + side
        return remote(block, block, attn_plane_send.at[index], attn_plane_recv.at[index], device)

    pending = []

    def give(source, target):
        copy = pltpu.make_async_copy(source, target, out_sem.at[len(pending)])
        copy.start()
        pending.append(copy)

    def first_hop(way, source, blocks, send, recv):
        return remote(source, blocks.at[dp * 4 + ctx], send, recv, line_dev(way))

    def attn_first(way):
        index = way * n_dp
        return first_hop(
            way, attn_pack, slots, attn_line_send.at[index], attn_line_recv.at[index]
        )

    def mlp_own(way):
        index = way * n_dp * 4
        return first_hop(
            way, mlp_pack.at[ctx], mlp_full, mlp_line_send.at[index], mlp_line_recv.at[index]
        )

    def attn_near(side):
        return remote(
            attn_pack,
            slots.at[dp * 4 + ctx],
            attn_plane_send.at[side],
            attn_plane_recv.at[side],
            plane[side],
        )

    own_attn = pltpu.make_async_copy(attn_pack, slots.at[dp * 4 + ctx], own_sem.at[0])
    own_tokens = pltpu.make_async_copy(tokens_in, tokens, own_sem.at[2])
    own_mlp = pltpu.make_async_copy(mlp_pack.at[ctx], mlp_full.at[dp * 4 + ctx], own_sem.at[1])
    own_attn.start()
    own_mlp.start()
    each(0, lambda way: attn_first(way).start(), True)
    for side in (1, 2):
        attn_near(side).start()
    each(0, lambda way: mlp_own(way).start(), True)

    def mlp_plane(k, came=False):
        return remote(
            mlp_pack.at[plane[k][1]],
            mlp_full.at[dp * 4 + (plane[k][1] if came else ctx)],
            mlp_plane_send.at[k],
            mlp_plane_recv.at[k],
            plane[k],
        )

    for k in (1, 2):
        mlp_plane(k).start()

    own_tokens.start()

    def place_rows(first, size, carry):
        at = pl.ds(first, size)
        row = first + lax.broadcasted_iota(jnp.int32, (size, 1), 0)
        position = ctx * row_count + row
        stop, begin = 0, jnp.zeros((size, 1), jnp.int32)
        for index in range(lengths.shape[1]):
            stop = stop + lengths[0, index]
            begin = begin + jnp.where(position >= stop, lengths[0, index], 0)
        position = position - begin
        lowest[at] = jnp.maximum(row - position + behind, row + 1)
        angles = position.astype(f32) * inverse[...]
        cosine[at] = jnp.cos(angles)
        sine[at] = jnp.sin(angles)
        return carry

    in_rows(row_count, place_rows, 0)

    def came(way, step):
        attn_came(way, step).wait_recv()

    def hand_on(way, step):
        for side in (1, 2):
            attn_plane(way, step, side).start()

    order = [(0, 0)] + [(way, step) for step in range(1, n_dp) for way in range(2)]

    def relay(way, step):
        for side in (1, 2):
            attn_plane(way, step, side, True).wait_recv()
        attn_plane(way, step, 3).start()

    def relayed(way, step):
        attn_plane(way, step, 3, True).wait_recv()

    def where_held(way, step, act):
        if step:
            pl.when(can_take(way, step))(lambda: act(way, step))
        else:
            act(way, step)

    def mlp_first(k):
        mlp_plane(k, True).wait_recv()
        each(0, lambda way: mlp_hop(way, 0, k).start(), True)

    def mlp_next(step, k):
        each(step, lambda way: mlp_came(way, step, k).wait_recv(), False)
        if step < n_dp - 1:
            each(step, lambda way: mlp_hop(way, step, k).start(), True)

    events = [functools.partial(mlp_first, k) for k in (1, 2, 3)] + [
        functools.partial(mlp_next, step, k) for step in range(1, n_dp) for k in range(4)
    ]
    events.reverse()

    def move(count):
        for _ in range(min(count, len(events))):
            events.pop()()

    own_attn.wait()
    for step in range(1, n_dp):
        each(step, lambda way: came(way, step), False)
        each(step, lambda way: attn_hop(way, step).start(), True)
        each(step, lambda way: hand_on(way, step), False)
        if step == 1:
            mlp_plane(3).start()
        if step <= 3:
            move(1)
    if n_dp == 1:
        mlp_plane(3).start()
    move(max(0, 4 - n_dp) + 2)
    for way, step in order:
        where_held(way, step, relay)
    move(1)
    for way, step in order:
        where_held(way, step, relayed)
    move(1)

    for block in range(n_dp * 4):
        wide_slots[block * owned : (block + 1) * owned, :] = slots[block].astype(f32)

    def narrow(first, size, carry):
        at = pl.ds(first, size)
        attn_full[at] = wide_slots[at].astype(bf16)
        return carry

    in_rows(width, narrow, 0)
    give(attn_full, attn_full_out)
    pick = lax.broadcasted_iota(jnp.int32, (8, 128), 0) == lax.broadcasted_iota(
        jnp.int32, (8, 128), 1
    )
    small = contract_columns(pick.astype(f32).astype(bf16), attn_full[:, 1280:1408])
    gain_rows[...] = small
    row_of = lax.broadcasted_iota(jnp.int32, (width, HD), 0)
    head_of = lax.broadcasted_iota(jnp.int32, (width, HD), 1)
    shift = owned_heads.bit_length() - 1
    chosen = row_of == (head_of >> shift) * owned + (head_of & (owned_heads - 1))
    heads = jnp.dot(
        small.astype(bf16), chosen.astype(f32).astype(bf16), preferred_element_type=f32
    )
    head_rows[...] = heads

    def normalize(first, size, carry):
        at = pl.ds(first, size)
        values = tokens[at].astype(f32)
        normed_out[at] = (values * scale_of(values) * gain_rows[0:1]).astype(bf16)
        return carry

    own_tokens.wait()
    in_rows(row_count, normalize, 0)

    def project(start, size):
        lin[:, pl.ds(start, size)] = jnp.dot(
            normed_out[...], attn_full[:, pl.ds(start, size)], preferred_element_type=f32
        )

    in_columns(3 * HD, project)
    give(normed_out, normed_out_out)
    give(lin, lin_out)

    def turn_keyval(first, size, carry):
        at = pl.ds(first, size)
        values = lin[at, 2 * HD : 3 * HD]
        keys = turned(values * scale_of(values) * head_rows[5:6], cosine[at], sine[at])
        mine = jnp.where(core == 0, keys, values).astype(bf16)
        keyval[core, pl.ds(pl.multiple_of(first + behind, 64), size)] = mine
        return carry

    in_rows(row_count, turn_keyval, 0)
    own_rows, last_rows = pl.ds(behind, row_count), pl.ds(row_count, behind)
    past_rows = pl.ds(0, behind)

    def to_core(came=False):
        block = keyval.at[1 - core if came else core, own_rows]
        return remote(block, block, keyval_send.at[0], keyval_recv.at[0], core_dev)

    def past_to_core(came=False):
        block = keyval.at[1 - core if came else core, past_rows]
        return remote(block, block, keyval_send.at[2], keyval_recv.at[2], core_dev)

    to_next = remote(
        keyval.at[core, last_rows],
        keyval.at[core, past_rows],
        keyval_send.at[1],
        keyval_recv.at[1],
        next_dev,
    )
    pl.when(ctx < 3)(to_next.start)
    to_core().start()

    def turn_query(first, size, carry):
        at = pl.ds(first, size)
        for head in range(2):
            values = lin[at, head * HD : (head + 1) * HD]
            normal = values * scale_of(values) * head_rows[4:5]
            query_out[head, at] = turned(normal, cosine[at], sine[at]).astype(bf16)
        return carry

    in_rows(row_count, turn_query, 0)
    give(query_out, query_out_out)

    @pl.when(ctx > 0)
    def _():
        to_next.wait_recv()
        past_to_core().start()
        past_to_core(True).wait_recv()

    @pl.when(ctx == 0)
    def _():
        keyval[:, 0:behind] = jnp.zeros((2, behind, HD), bf16)

    to_core(True).wait_recv()

    block_rows = 256
    reach = block_rows + behind

    def attend(first, head):
        at = pl.ds(first, block_rows)
        near = pl.ds(first, reach)
        scores = contract_columns(query_out[head, at], keyval[0, near]) * HD ** (-0.5)
        key_at = first + lax.broadcasted_iota(jnp.int32, (block_rows, reach), 1)
        query_at = first + behind + lax.broadcasted_iota(jnp.int32, (block_rows, reach), 0)
        scores = jnp.where((key_at >= lowest[at]) & (key_at <= query_at), scores, -1e30)
        row_max = jnp.max(scores, axis=1, keepdims=True)
        values = jnp.exp(scores - row_max)
        row_total = jnp.sum(values, axis=1, keepdims=True)
        probs = (values / row_total).astype(bf16)
        log_total[head, at] = row_max + jnp.log(row_total)
        out = jnp.dot(probs, keyval[1, near], preferred_element_type=f32)
        attended[at, head * HD : (head + 1) * HD] = out.astype(bf16)

    for block in range(row_count // block_rows):
        for head in range(2):
            attend(block * block_rows, head)
    give(attended, attended_out)
    give(keyval, keyval_out)
    move(2)

    def outward(start, size):
        partial[:, pl.ds(start, size)] = contract_columns(
            attended[...], attn_full[pl.ds(start, size), 3 * HD : 5 * HD]
        )

    in_columns(width, outward)

    def give_half(first, size, carry):
        at = pl.ds(pl.multiple_of((1 - core) * half + first, 64), size)
        core_send[pl.ds(first, size)] = partial[at].astype(bf16)
        return carry

    in_rows(half, give_half, 0)
    exchange = remote(core_send, core_take, keyval_send.at[3], keyval_recv.at[3], core_dev)
    exchange.start()
    move(1)
    exchange.wait_recv()

    def finish(first, size, carry):
        at = pl.ds(first, size)
        whole_at = pl.ds(pl.multiple_of(core * half + first, 64), size)
        branch = partial[whole_at] + core_take[at].astype(f32)
        branch_out[at] = branch
        middle = tokens[whole_at].astype(f32) + branch * scale_of(branch) * gain_rows[1:2]
        middle_out[at] = middle
        rows[0, 0, at] = (middle * scale_of(middle) * gain_rows[2:3]).astype(bf16)
        return carry

    in_rows(half, finish, 0)

    give(branch_out, branch_out_out)
    give(middle_out, middle_out_out)

    def remote_rows(source, target, index, device):
        return remote(source, target, rows_send.at[index], rows_recv.at[index], device)

    gather = gather_copies(remote_rows, rows, 0)
    outs = [
        pltpu.make_async_copy(rows.at[step], rows_out.at[step], rows_sem.at[step])
        for step in range(4)
    ]
    for step in range(4):
        gather_step(gather, step)
        outs[step].start()
        if step == 0:
            move(1)
    move(len(events))
    for copy in gather:
        copy.wait_send()
    for copy in outs + pending + [own_mlp]:
        copy.wait()

    exchange.wait_send()
    to_core().wait_send()
    pl.when(ctx < 3)(to_next.wait_send)
    pl.when(ctx > 0)(past_to_core().wait_send)
    for k in (1, 2, 3):
        mlp_plane(k).wait_send()
    each(0, lambda way: attn_first(way).wait_send(), True)
    each(0, lambda way: mlp_own(way).wait_send(), True)
    for step in range(n_dp - 1):
        if step:
            each(step, lambda way: attn_hop(way, step).wait_send(), True)
        for k in range(4):
            if step or k:
                each(step, lambda way: mlp_hop(way, step, k).wait_send(), True)

    def left(way, step):
        for side in (1, 2, 3):
            if step or side == 3:
                attn_plane(way, step, side).wait_send()
            else:
                attn_near(side).wait_send()

    for way, step in order:
        where_held(way, step, left)


def attend_call(n_dp, owned_heads, behind, tokens, lengths, inverse, attn_pack, mlp_pack):
    row_count, width = tokens.shape
    half = row_count // 2
    owned, attn_cols = attn_pack.shape
    blocks = n_dp * 4
    f32, bf16 = jnp.float32, jnp.bfloat16
    vmem = pl.BlockSpec(memory_space=pltpu.VMEM)
    anywhere = pl.BlockSpec(memory_space=pl.ANY)

    def array(dtype, *shape):
        return jax.ShapeDtypeStruct(shape, dtype)

    dma = pltpu.SemaphoreType.DMA
    return pl.pallas_call(
        functools.partial(attend_kernel, n_dp, owned_heads),
        out_shape=(
            array(bf16, blocks, owned, mlp_pack.shape[2]),
            array(f32, 8, width),
            array(f32, 8, HD),
            array(f32, 2, row_count, 1),
            array(f32, row_count, HD // 2),
            array(f32, row_count, HD // 2),
            array(jnp.int32, row_count, 1),
            array(bf16, width, attn_cols),
            array(bf16, row_count, width),
            array(f32, row_count, 3 * HD),
            array(bf16, 2, row_count, HD),
            array(bf16, 2, behind + row_count, HD),
            array(bf16, row_count, 2 * HD),
            array(f32, half, width),
            array(f32, half, width),
            array(bf16, 4, 2, half, width),
        ),
        in_specs=[
            anywhere,
            pl.BlockSpec(memory_space=pltpu.SMEM),
            vmem,
            anywhere,
            anywhere,
        ],
        out_specs=(anywhere,) + (vmem,) * 6 + (anywhere,) * 9,
        scratch_shapes=[
            pltpu.VMEM((blocks, owned, attn_cols), bf16),
            pltpu.VMEM((width, attn_cols), f32),
            pltpu.VMEM((2, behind + row_count, HD), bf16),
            pltpu.VMEM((row_count, width), f32),
            pltpu.VMEM((half, width), bf16),
            pltpu.VMEM((half, width), bf16),
            dma((3,)),
            dma((4,)),
            dma((4,)),
            dma((8 * n_dp,)),
            dma((8 * n_dp,)),
            dma((2 * n_dp,)),
            dma((2 * n_dp,)),
            dma((8 * n_dp,)),
            dma((8 * n_dp,)),
            dma((4,)),
            dma((4,)),
            pltpu.VMEM((4, 2, half, width), bf16),
            dma((10,)),
            dma((10,)),
            dma((4,)),
            pltpu.VMEM((width, attn_cols), bf16),
            pltpu.VMEM((row_count, width), bf16),
            pltpu.VMEM((row_count, 3 * HD), f32),
            pltpu.VMEM((2, row_count, HD), bf16),
            pltpu.VMEM((row_count, 2 * HD), bf16),
            pltpu.VMEM((half, width), f32),
            pltpu.VMEM((half, width), f32),
            dma((8,)),
            pltpu.VMEM((row_count, width), bf16),
        ],
        compiler_params=pltpu.CompilerParams(
            collective_id=1, has_side_effects=True, vmem_limit_bytes=60 * 2**20
        ),
        cost_estimate=pl.CostEstimate(
            flops=4 * 10**9, bytes_accessed=30 * 2**20, transcendentals=2 * 10**6
        ),
        name="attend",
    )(tokens, lengths, inverse, attn_pack, mlp_pack)


def mlp_kernel(
    n_dp,
    line,
    rows_in,
    middle_in,
    cotangent_in,
    gain_rows,
    weights_in,
    result_out,
    back_sum,
    gain_sum,
    weights_out,
    early,
    result,
    rows,
    grads,
    hidden,
    pair,
    weights,
    total,
    waiting,
    core_send,
    core_take,
    plane_send,
    plane_take,
    send_sem,
    recv_sem,
    load_sem,
    out_sem,
    middle,
    cotangent,
):
    half, width = middle.shape
    h = half // 2
    hid = hidden.shape[2]
    step_rows = 2 * half
    part_a, part_b = pl.ds(0, h), pl.ds(h, h)
    x_dev, y_dev, _, core_dev = plane_partners()
    core = lax.axis_index("tensor")
    gain = gain_rows.at[pl.ds(3, 1)]
    f32, bf16 = jnp.float32, jnp.bfloat16

    loads = [pltpu.make_async_copy(weights_in, weights, load_sem.at[4])] + [
        pltpu.make_async_copy(rows_in.at[step], rows.at[step], load_sem.at[step])
        for step in range(4)
    ]
    norm_loads = [
        pltpu.make_async_copy(middle_in, middle, load_sem.at[5]),
        pltpu.make_async_copy(cotangent_in, cotangent, load_sem.at[6]),
    ]
    for load in [loads[0], loads[4], loads[3], loads[2], loads[1]] + norm_loads:
        load.start()
    enter(n_dp, line > 1)

    def remote(source, target, index, device):
        return pltpu.make_async_remote_copy(
            src_ref=source,
            dst_ref=target,
            send_sem=send_sem.at[index],
            recv_sem=recv_sem.at[index],
            device_id=device,
            device_id_type=MESH,
        )

    def scatter_copies(base):
        return [
            remote(plane_send.at[0, part_a], plane_take.at[0, part_a], base, y_dev),
            remote(plane_send.at[0, part_b], plane_take.at[0, part_b], base + 1, x_dev),
            remote(plane_send.at[1, part_a], plane_take.at[1, part_a], base + 2, y_dev),
            remote(plane_send.at[1, part_b], plane_take.at[1, part_b], base + 3, x_dev),
            remote(plane_send.at[2, part_a], plane_take.at[2, part_a], base + 4, x_dev),
            remote(plane_send.at[2, part_b], plane_take.at[2, part_b], base + 5, y_dev),
        ] + [
            remote(core_send.at[step % 2], core_take.at[step], base + 6 + step, core_dev)
            for step in range(4)
        ]

    def scatter_step(copies, step, before, left, first):
        kept = (total, waiting, back_sum, back_sum)[step]
        slot = core_send.at[step % 2]
        if before is not None:
            copies[6 + before].wait_send()

        def part(rows, start, size):
            right = weights[pl.ds(start, size), first : first + left.shape[2]]
            return contract_columns(left[step, rows], right)

        def give(start, size):
            slot[:, pl.ds(start, size)] = part(pl.ds(half, half), start, size).astype(bf16)

        def keep(start, size):
            kept[:, pl.ds(start, size)] = part(pl.ds(0, half), start, size)

        in_columns(width, give)
        copies[6 + step].start()
        in_columns(width, keep)

    def scatter_rest(copies, step):
        kept = (total, waiting, back_sum, back_sum)[step]
        copies[6 + step].wait_recv()
        summed = kept[...] + core_take[step].astype(f32)
        if step < 2:
            kept[...] = summed
        else:
            plane_send[step - 2] = summed.astype(bf16)
            copies[2 * step - 4].start()
            copies[2 * step - 3].start()

    def scatter_end(copies):
        copies[2].wait_recv()
        copies[3].wait_recv()
        plane_send[2] = (waiting[...] + plane_take[1].astype(f32)).astype(bf16)
        copies[4].start()
        copies[5].start()

    def scatter_total(at):
        return total[at] + plane_take[0, at].astype(f32) + plane_take[2, at].astype(f32)

    def scatter_wait(copies):
        for index in (0, 1, 4, 5):
            copies[index].wait_recv()

    def sent(copies):
        for copy in copies:
            copy.wait_send()

    scatter = scatter_copies(0)
    loads[0].wait()
    for step in (3, 2, 1, 0):
        loads[1 + step].wait()

        def activate(start, size):
            def lin(first):
                return jnp.dot(
                    rows[step].reshape(step_rows, width),
                    weights[:, pl.ds(pl.multiple_of(first + start, 128), size)],
                    preferred_element_type=f32,
                )

            gate, up = lin(0), lin(hid)
            square = gate * gate
            chance = 0.5 + 0.5 * jnp.tanh(gate * (GELU_SCALE + GELU_SCALE * 0.044715 * square))
            gelu = gate * chance
            slope = chance + gelu * (1.0 - chance) * (
                2 * GELU_SCALE + 6 * GELU_SCALE * 0.044715 * square
            )
            hidden[step, :, pl.ds(start, size)] = (gelu * up).astype(bf16)
            pair[step, :, pl.ds(start, size)] = (slope * up).astype(bf16)
            pair[step, :, pl.ds(pl.multiple_of(hid + start, 128), size)] = gelu.astype(bf16)

        in_columns(hid, activate)
        scatter_step(scatter, step, step + 2 if step < 2 else None, hidden, 2 * hid)
        scatter_rest(scatter, step)
        if step == 1:
            scatter_end(scatter)
    scatter_wait(scatter)
    sent(scatter[:8])
    for load in norm_loads:
        load.wait()

    def norm_rows(first, size, gain_total):
        at = pl.ds(first, size)
        raw = scatter_total(at)
        scale = lax.rsqrt(jnp.mean(raw * raw, axis=1, keepdims=True) + norm_eps)
        normal = raw * scale
        result[at] = (middle[at] + normal * gain[...]).astype(bf16)
        cotangents = cotangent[pl.ds(pl.multiple_of(core * half + first, 64), size)].astype(f32)
        scaled = cotangents * gain[...]
        inner = jnp.mean(raw * scaled, axis=1, keepdims=True)
        back = scale * scaled - raw * (scale * scale * scale * inner)
        grads[0, 0, at] = back.astype(bf16)
        return gain_total + jnp.sum(cotangents * normal, axis=0, keepdims=True)

    gain_sum[...] = in_rows(half, norm_rows, jnp.zeros((1, width), f32))

    def result_rows(place):
        return result_out.at[pl.ds(pl.multiple_of(place * half, 64), half)]

    own_result = pltpu.make_async_copy(result, result_rows(core), out_sem.at[2])
    far_result = remote(result, result_rows(core), 30, core_dev)
    own_result.start()
    far_result.start()

    gather = gather_copies(remote, grads, 10)
    scatter = scatter_copies(20)
    for step in range(4):
        gather_step(gather, step)

        def unfold(start, size):
            hidden_grad = jnp.dot(
                grads[step].reshape(step_rows, width),
                weights[:, pl.ds(pl.multiple_of(2 * hid + start, 128), size)],
                preferred_element_type=f32,
            )
            hidden_grad = hidden_grad.astype(bf16)
            for first in (0, hid):
                at = pl.ds(pl.multiple_of(first + start, 128), size)
                pair[step, :, at] = pair[step, :, at] * hidden_grad

        in_columns(hid, unfold)
        if step:
            scatter_rest(scatter, step - 1)
        scatter_step(scatter, step, step - 2 if step >= 2 else None, pair, 0)
    scatter_rest(scatter, 3)
    sent(gather)

    def weigh(first, right):
        def one(i, carry):
            at = pl.ds(pl.multiple_of(i * 384, 128), 384)
            left = (rows if right is pair else grads)[:, :, :, at].reshape(8 * half, 384)
            product = contract_rows(left, right[...].reshape(8 * half, right.shape[2]))
            weights[at, first : first + right.shape[2]] = product.astype(bf16)
            return carry

        lax.fori_loop(0, width // 384, one, 0)
        columns = pl.ds(first, right.shape[2])
        copy = pltpu.make_async_copy(
            weights.at[:, columns], weights_out.at[:, columns], out_sem.at[first // (2 * hid)]
        )
        copy.start()
        return copy

    down_out = weigh(2 * hid, hidden)

    dp, ctx, _ = places()
    last_dp = line - 1
    group = width // line

    def early_copy(way, index):
        place = last_dp - index if way == 0 else index
        first = pl.multiple_of(place * group, 8)
        device = (dp + 1, ctx, core) if way == 0 else (dp - 1, ctx, core)
        source = weights.at[pl.ds(first, group), pl.ds(2 * hid, hid)]
        item = 2 * index + way
        return remote(source, early.at[item], 31 + item, device)

    def sends_early(way):
        return dp == 0 if way == 0 else dp == last_dp

    if line > 1:
        for way, index in early_items(line):
            pl.when(sends_early(way))(early_copy(way, index).start)
    scatter_end(scatter)
    gate_out = weigh(0, pair)
    scatter_wait(scatter)

    def finish_rows(first, size, carry):
        at = pl.ds(first, size)
        back_sum[at] = scatter_total(at)
        return carry

    in_rows(half, finish_rows, 0)
    sent(scatter[:6] + scatter[8:])
    if line > 1:
        for way, index in early_items(line):
            pl.when(sends_early(way))(early_copy(way, index).wait_send)
            pl.when(takes_early(way, dp, last_dp))(early_copy(way, index).wait_recv)
    down_out.wait()
    gate_out.wait()
    own_result.wait()
    far_result.wait_send()
    remote(result, result_rows(1 - core), 30, core_dev).wait_recv()


def early_items(line):
    return [(way, index) for index in range(min(2, line - 1)) for way in range(2)]


def takes_early(way, dp, last_dp):
    return dp == 1 if way == 0 else dp == last_dp - 1


def mlp_call(n_dp, line, rows, middle, cotangent, gain_rows, weights):
    half, width = middle.shape
    hid = weights.shape[1] // 3
    count = 8 * half
    f32, bf16 = jnp.float32, jnp.bfloat16
    vmem = pl.BlockSpec(memory_space=pltpu.VMEM)
    anywhere = pl.BlockSpec(memory_space=pl.ANY)
    return pl.pallas_call(
        functools.partial(mlp_kernel, n_dp, line),
        out_shape=(
            jax.ShapeDtypeStruct(cotangent.shape, bf16),
            jax.ShapeDtypeStruct((half, width), f32),
            jax.ShapeDtypeStruct((1, width), f32),
            jax.ShapeDtypeStruct((width, 3 * hid), bf16),
            jax.ShapeDtypeStruct((max(2, len(early_items(line))), width // line, hid), bf16),
        ),
        in_specs=[anywhere, anywhere, anywhere, vmem, anywhere],
        out_specs=(anywhere, vmem, vmem, anywhere, anywhere),
        scratch_shapes=[
            pltpu.VMEM((half, width), bf16),
            pltpu.VMEM((4, 2, half, width), bf16),
            pltpu.VMEM((4, 2, half, width), bf16),
            pltpu.VMEM((4, 2 * half, hid), bf16),
            pltpu.VMEM((4, 2 * half, 2 * hid), bf16),
            pltpu.VMEM((width, 3 * hid), bf16),
            pltpu.VMEM((half, width), f32),
            pltpu.VMEM((half, width), f32),
            pltpu.VMEM((2, half, width), bf16),
            pltpu.VMEM((4, half, width), bf16),
            pltpu.VMEM((3, half, width), bf16),
            pltpu.VMEM((3, half, width), bf16),
            pltpu.SemaphoreType.DMA((35,)),
            pltpu.SemaphoreType.DMA((35,)),
            pltpu.SemaphoreType.DMA((7,)),
            pltpu.SemaphoreType.DMA((3,)),
            pltpu.VMEM((half, width), f32),
            pltpu.VMEM(cotangent.shape, bf16),
        ],
        compiler_params=pltpu.CompilerParams(
            collective_id=0, has_side_effects=True, vmem_limit_bytes=63 * 2**20
        ),
        cost_estimate=pl.CostEstimate(
            flops=2 * count * width * hid * 9, bytes_accessed=30 * 2**20, transcendentals=count * hid
        ),
        name="feed_forward",
    )(rows, middle, cotangent, gain_rows, weights)


def norm_back(values, gains, grads):
    scale = scale_of(values)
    normal = values * scale
    scaled = grads * gains
    inner = jnp.mean(values * scaled, axis=1, keepdims=True)
    return scale * scaled - values * (scale * scale * scale * inner), grads * normal


def retreat_kernel(
    n_dp,
    line,
    owned_heads,
    back_sum,
    middle,
    branch,
    cotangent_in,
    tokens_in,
    cosine,
    sine,
    lowest,
    gain_rows,
    head_rows,
    gain_three,
    attn_full_in,
    normed_one_in,
    lin_in,
    query_in,
    keyval_in,
    attended_in,
    log_total,
    mlp_grads,
    early,
    input_whole,
    gate_reduced,
    down_reduced,
    attn_reduced,
    keyval_reduced,
    input_out,
    line_slots,
    attn_grads,
    attn_blocks,
    attn_plane_take,
    attn_sums,
    attn_slots,
    branch_low,
    attended_grad,
    query_grad,
    lin_grad,
    keyval_grad,
    keyval_send,
    keyval_take,
    past_take,
    partial,
    core_send,
    core_take,
    small_rows,
    small_take,
    line_send_sem,
    line_recv_sem,
    plane_send_sem,
    plane_recv_sem,
    attn_plane_send_sem,
    attn_plane_recv_sem,
    attn_line_send_sem,
    attn_line_recv_sem,
    core_send_sem,
    core_recv_sem,
    load_sem,
    early_sem,
    mlp_own,
    cotangent,
    tokens,
    attn_full,
    normed_one,
    lin,
    query,
    keyval,
    attended,
):
    dp, ctx, core = places()
    x_dev, y_dev, far_dev, core_dev = plane_partners()
    plane = ((dp, ctx, core), x_dev, y_dev, far_dev)
    f32, bf16 = jnp.float32, jnp.bfloat16
    row_count, width = tokens.shape
    half = row_count // 2
    owned, hid = mlp_grads.shape[1], mlp_grads.shape[2] // 3
    behind = keyval.shape[1] - row_count
    last_dp = line - 1
    here_dp = dp if line > 1 else 0
    early_count = len(early_items(line)) // 2
    sources = (
        (cotangent_in, cotangent),
        (attn_full_in, attn_full),
        (query_in, query),
        (keyval_in, keyval),
        (mlp_grads, mlp_own),
        (lin_in, lin),
        (attended_in, attended),
        (normed_one_in, normed_one),
        (tokens_in, tokens),
    )
    held = [
        pltpu.make_async_copy(source, target, load_sem.at[3 + index])
        for index, (source, target) in enumerate(sources)
    ]
    loads = [
        pltpu.make_async_copy(
            source,
            attn_grads.at[pl.ds(index * half, half), pl.ds(0, width)],
            load_sem.at[index],
        )
        for index, source in enumerate((middle, branch, back_sum))
    ]
    for load in loads + held:
        load.start()
    enter(n_dp, line > 1)

    def remote(source, target, send, recv, device):
        return pltpu.make_async_remote_copy(
            src_ref=source,
            dst_ref=target,
            send_sem=send,
            recv_sem=recv,
            device_id=device,
            device_id_type=MESH,
        )

    def goal(way, far):
        return dp + far if way == 0 else dp - far

    def has_goal(way, far):
        return dp + far <= last_dp if way == 0 else dp >= far

    def is_first(way):
        return dp == 0 if way == 0 else dp == last_dp

    def not_first(way):
        return dp > 0 if way == 0 else dp < last_dp

    def line_dev(way):
        return (dp + 1, ctx, core) if way == 0 else (dp - 1, ctx, core)

    def slot_of(way, far, k):
        return (way * last_dp + far - 1) * 4 + k

    def own_mlp(place, k):
        return mlp_own[place * 4 + plane[k][1]].astype(f32)

    def first_hop(way, far, k):
        slot = slot_of(way, far, k)
        columns = pl.ds(0, 2 * hid if last_dp - far < early_count else 3 * hid)
        return remote(
            mlp_grads.at[goal(way, far) * 4 + plane[k][1], :, columns],
            line_slots.at[slot, :, columns],
            line_send_sem.at[slot],
            line_recv_sem.at[slot],
            line_dev(way),
        )

    def next_hop(way, far, k):
        slot = slot_of(way, far, k)
        return remote(
            line_slots.at[slot_of(way, far + 1, k)],
            line_slots.at[slot],
            line_send_sem.at[slot],
            line_recv_sem.at[slot],
            line_dev(way),
        )

    def came(way, far, k):
        slot = slot_of(way, far, k)

        def wait(count):
            block = line_slots.at[slot, :, pl.ds(0, count)]
            remote(
                block, block, line_send_sem.at[slot], line_recv_sem.at[slot], line_dev(way)
            ).wait_recv()

        def wait_both():
            wait(2 * hid)
            early_load(way, last_dp - far, k).wait()

        if far == last_dp:
            wait_both()
        elif last_dp - far < early_count:
            beside_first = takes_early(way, dp, last_dp)
            pl.when(beside_first)(wait_both)
            pl.when(jnp.logical_not(beside_first))(functools.partial(wait, 3 * hid))
        else:
            wait(3 * hid)

    def early_load(way, index, k):
        return pltpu.make_async_copy(
            early.at[2 * index + way, plane[k][1]],
            line_slots.at[slot_of(way, last_dp - index, k), :, pl.ds(2 * hid, hid)],
            early_sem.at[(2 * index + way) * 4 + k],
        )

    def load_early(way):
        for index in range(early_count):
            for k in range(4):
                early_load(way, index, k).start()

    if line > 1:
        for way in range(2):
            pl.when(takes_early(way, dp, last_dp))(functools.partial(load_early, way))

    turn = (3, 1, 2, 0)

    def start_first(blocks):
        def start(way):
            for far, k in blocks:
                first_hop(way, far, k).start()

        for way in range(2):
            if line > 1:
                pl.when(is_first(way))(functools.partial(start, way))

    start_first([(far, k) for far in range(last_dp, 1, -1) for k in turn])

    def pass_on(way, far, k):
        came(way, far + 1, k)
        slot = slot_of(way, far + 1, k)
        line_slots[slot] = (line_slots[slot].astype(f32) + own_mlp(goal(way, far), k)).astype(bf16)
        next_hop(way, far, k).start()

    def mlp_step(far, k):
        for way in range(2):
            pl.when(not_first(way) & has_goal(way, far))(functools.partial(pass_on, way, far, k))

    parts = ((gate_reduced, pl.ds(0, 2 * hid)), (down_reduced, pl.ds(2 * hid, hid)))

    def to_owner(k, came=False):
        place = plane[k][1] if came else ctx
        return [
            remote(
                line_slots.at[k, :, columns],
                target.at[place],
                plane_send_sem.at[2 * k + index],
                plane_recv_sem.at[2 * k + index],
                plane[k],
            )
            for index, (target, columns) in enumerate(parts)
        ]

    own_done = [
        pltpu.make_async_copy(line_slots.at[0, :, columns], target.at[ctx], plane_send_sem.at[index])
        for index, (target, columns) in enumerate(parts)
    ]

    def mlp_last(k):
        if line > 1:
            for way in range(2):
                pl.when(not_first(way))(functools.partial(came, way, 1, k))
        total = own_mlp(here_dp, k)
        for way in range(2):
            if line > 1:
                arrived = line_slots[slot_of(way, 1, k)].astype(f32)
                total = total + jnp.where(not_first(way), arrived, 0.0)
        line_slots[k] = total.astype(bf16)
        for copy in to_owner(k) if k else own_done:
            copy.start()

    events = [
        functools.partial(mlp_step, far, k) for far in range(line - 2, 0, -1) for k in turn
    ] + [functools.partial(mlp_last, k) for k in turn]
    events.reverse()

    def move(count):
        for _ in range(min(count, len(events))):
            events.pop()()

    for load in loads + held[:1]:
        load.wait()

    def loaded(index, first, size):
        return attn_grads[pl.ds(pl.multiple_of(first + index * half, 64), size), 0:width]

    def norms(first, size, carry):
        at = pl.ds(first, size)
        part, gain_two = norm_back(loaded(0, first, size), gain_rows[2:3], loaded(2, first, size))
        whole_at = pl.ds(pl.multiple_of(core * half + first, 64), size)
        middle_grad = cotangent[whole_at].astype(f32) + part
        input_out[at] = middle_grad
        grad, gain_one = norm_back(loaded(1, first, size), gain_rows[1:2], middle_grad)
        branch_low[whole_at] = grad.astype(bf16)
        return (
            carry[0] + jnp.sum(gain_one, axis=0, keepdims=True),
            carry[1] + jnp.sum(gain_two, axis=0, keepdims=True),
        )

    nothing = jnp.zeros((1, width), f32)
    small_rows[...] = jnp.zeros_like(small_rows)
    gain_one, gain_two = in_rows(half, norms, (nothing, nothing))
    small_rows[1:2] = gain_one
    small_rows[2:3] = gain_two
    small_rows[3:4] = gain_three[...]

    def halves(came):
        rows = pl.ds(pl.multiple_of((1 - core if came else core) * half, 64), half)
        return remote(
            branch_low.at[rows], branch_low.at[rows], core_send_sem.at[0], core_recv_sem.at[0], core_dev
        )

    halves(False).start()
    halves(True).wait_recv()

    def inward(start, size):
        grad = jnp.dot(
            branch_low[...],
            attn_full[:, pl.ds(pl.multiple_of(3 * HD + start, 128), size)],
            preferred_element_type=f32,
        )
        attended_grad[:, pl.ds(start, size)] = grad.astype(bf16)

    held[1].wait()
    in_columns(2 * HD, inward)

    block_rows = 256
    reach = block_rows + behind
    keyval_grad[...] = jnp.zeros_like(keyval_grad)
    for load in held[2:5]:
        load.wait()

    def retreat(first, head):
        at = pl.ds(first, block_rows)
        near = pl.ds(first, reach)
        columns = slice(head * HD, (head + 1) * HD)
        scores = contract_columns(query[head, at], keyval[0, near]) * HD ** (-0.5)
        key_at = first + lax.broadcasted_iota(jnp.int32, (block_rows, reach), 1)
        query_at = first + behind + lax.broadcasted_iota(jnp.int32, (block_rows, reach), 0)
        scores = jnp.where((key_at >= lowest[at]) & (key_at <= query_at), scores, -1e30)
        probs = jnp.exp(scores - log_total[head, at])
        grads = attended_grad[at, columns]
        probs_grad = contract_columns(grads, keyval[1, near])
        delta = jnp.sum(probs * probs_grad, axis=1, keepdims=True)
        score_grad = (probs * (probs_grad - delta)).astype(bf16)
        query_grad[at, columns] = (
            jnp.dot(score_grad, keyval[0, near], preferred_element_type=f32) * HD ** (-0.5)
        )
        keyval_grad[0, near] += contract_rows(score_grad, query[head, at]) * HD ** (-0.5)
        keyval_grad[1, near] += contract_rows(probs.astype(bf16), grads)

    for block in range(row_count // block_rows):
        for head in range(2):
            retreat(block * block_rows, head)
    move(2)

    keyval_send[0] = keyval_grad[1 - core].astype(bf16)
    to_core = remote(
        keyval_send.at[0], keyval_take, core_send_sem.at[1], core_recv_sem.at[1], core_dev
    )
    to_core.start()

    def query_rows(first, size, carry):
        at = pl.ds(first, size)
        total = carry
        for head in range(2):
            columns = slice(head * HD, (head + 1) * HD)
            grads = turned(query_grad[at, columns], cosine[at], -sine[at])
            grad, gain = norm_back(lin[at, columns], head_rows[4:5], grads)
            lin_grad[at, columns] = grad.astype(bf16)
            total = total + jnp.sum(gain, axis=0, keepdims=True)
        return total

    for load in held[5:]:
        load.wait()
    head_zero = in_rows(row_count, query_rows, jnp.zeros((1, HD), f32))
    move(1)
    to_core.wait_recv()
    keyval_grad[core] = keyval_grad[core] + keyval_take[...].astype(f32)
    keyval_send[1, 0:behind] = keyval_grad[core, 0:behind].astype(bf16)
    to_past = remote(
        keyval_send.at[1, pl.ds(0, behind)],
        past_take,
        core_send_sem.at[2],
        core_recv_sem.at[2],
        (dp, ctx - 1, core),
    )
    pl.when(ctx > 0)(to_past.start)

    def outward(start, size):
        attn_grads[0:width, pl.ds(pl.multiple_of(3 * HD + start, 128), size)] = contract_rows(
            branch_low[...], attended[:, pl.ds(start, size)]
        )

    in_columns(2 * HD, outward)

    @pl.when(ctx < 3)
    def _():
        to_past.wait_recv()
        late = pl.ds(row_count, behind)
        keyval_grad[core, late] = keyval_grad[core, late] + past_take[...].astype(f32)

    def keyval_rows(first, size, carry):
        at = pl.ds(first, size)
        values = keyval_grad[core, pl.ds(pl.multiple_of(first + behind, 64), size)]
        grads = turned(values, cosine[at], -sine[at])
        grad, gain = norm_back(lin[at, 2 * HD : 3 * HD], head_rows[5:6], grads)
        lin_grad[at, 2 * HD : 3 * HD] = jnp.where(core == 0, grad, values).astype(bf16)
        return carry + jnp.sum(gain, axis=0, keepdims=True)

    head_one = in_rows(row_count, keyval_rows, jnp.zeros((1, HD), f32))
    head_one = jnp.where(core == 0, head_one, 0.0)

    def weigh(start, size):
        attn_grads[0:width, pl.ds(start, size)] = contract_rows(
            normed_one[...], lin_grad[:, pl.ds(start, size)]
        )

    in_columns(3 * HD, weigh)

    attn_parts = ((0, 5 * HD), (5 * HD, 128))

    def attn_plane(k, place, part):
        index = (k - 1) * n_dp + place
        columns = pl.ds(*attn_parts[part])
        return remote(
            attn_blocks.at[place * 4 + plane[k][1], :, columns],
            attn_plane_take.at[index, :, columns],
            attn_plane_send_sem.at[2 * index + part],
            attn_plane_recv_sem.at[2 * index + part],
            plane[k],
        )

    def give_attn(part):
        first, count = attn_parts[part]
        for block in range(n_dp * 4):
            attn_blocks[block, :, first : first + count] = attn_grads[
                block * owned : (block + 1) * owned, first : first + count
            ].astype(bf16)
        for place in range(n_dp):
            for k in (3, 1, 2):
                attn_plane(k, place, part).start()

    give_attn(0)
    move(1)
    start_first([(1, k) for k in turn])

    def back(start, size):
        columns = pl.ds(start, size)
        product = contract_columns(lin_grad[...], attn_full[columns, 0 : 3 * HD])
        first, second = product[:half], product[half:]
        partial[:, columns] = jnp.where(core == 0, first, second)
        core_send[:, columns] = jnp.where(core == 0, second, first).astype(bf16)

    in_columns(width, back)
    exchange = remote(core_send, core_take, core_send_sem.at[3], core_recv_sem.at[3], core_dev)
    exchange.start()
    exchange.wait_recv()

    def finish(first, size, carry):
        at = pl.ds(first, size)
        whole_at = pl.ds(pl.multiple_of(core * half + first, 64), size)
        grads = partial[at] + core_take[at].astype(f32)
        part, gain = norm_back(tokens[whole_at].astype(f32), gain_rows[0:1], grads)
        input_out[at] = input_out[at] + part
        return carry + jnp.sum(gain, axis=0, keepdims=True)

    small_rows[0:1] = in_rows(half, finish, nothing)

    def input_rows(place):
        return input_whole.at[pl.ds(pl.multiple_of(place * half, 64), half)]

    own_input = pltpu.make_async_copy(input_out, input_rows(core), load_sem.at[0])
    own_input.start()

    def far_input(place):
        return remote(
            input_out, input_rows(place), core_send_sem.at[5], core_recv_sem.at[5], core_dev
        )

    far_input(core).start()

    row_of = lax.broadcasted_iota(jnp.int32, (width, HD), 0)
    head_of = lax.broadcasted_iota(jnp.int32, (width, HD), 1)
    shift = owned_heads.bit_length() - 1
    chosen = row_of == (head_of >> shift) * owned + (head_of & (owned_heads - 1))
    heads = jnp.concatenate([head_zero, head_one, jnp.zeros((6, HD), f32)], axis=0)
    spread = contract_columns(heads.astype(bf16), chosen.astype(f32).astype(bf16))
    small_rows[4:6] = spread[0:2]
    smalls = remote(
        small_rows.at[pl.ds(0, 8)], small_take, core_send_sem.at[4], core_recv_sem.at[4], core_dev
    )
    smalls.start()
    smalls.wait_recv()
    smalls.wait_send()
    small_rows[0:8] = small_rows[0:8] + small_take[...]
    attn_grads[0:width, 5 * HD : 5 * HD + 128] = small_rows[...].T

    give_attn(1)
    move(len(events) - 4)
    for place in range(n_dp):
        total = attn_blocks[place * 4 + ctx].astype(f32)
        for k in (1, 2, 3):
            attn_plane(k, place, 0).wait_recv()
            attn_plane(k, place, 1).wait_recv()
            total = total + attn_plane_take[(k - 1) * n_dp + place].astype(f32)
        attn_sums[place] = total.astype(bf16)

    def attn_hop(way, far, first):
        source = attn_sums.at[goal(way, far)] if first else attn_slots.at[way * line + far + 1]
        index = way * line + far
        return remote(
            source,
            attn_slots.at[index],
            attn_line_send_sem.at[index],
            attn_line_recv_sem.at[index],
            line_dev(way),
        )

    def attn_came(way, far):
        index = way * line + far
        block = attn_slots.at[index]
        remote(
            block, block, attn_line_send_sem.at[index], attn_line_recv_sem.at[index], line_dev(way)
        ).wait_recv()

    def attn_start(way):
        for far in range(last_dp, 0, -1):
            attn_hop(way, far, True).start()

    def attn_pass(way, far):
        attn_came(way, far + 1)
        index = way * line + far + 1
        total = attn_slots[index].astype(f32) + attn_sums[goal(way, far)].astype(f32)
        attn_slots[index] = total.astype(bf16)
        attn_hop(way, far, False).start()

    for way in range(2):
        if line > 1:
            pl.when(is_first(way))(functools.partial(attn_start, way))
    move(4)
    for far in range(line - 2, 0, -1):
        for way in range(2):
            pl.when(not_first(way) & has_goal(way, far))(functools.partial(attn_pass, way, far))
    if line == 1:
        attn_reduced[...] = attn_sums[...]
    else:
        total = attn_sums[dp].astype(f32)
        for way in range(2):
            pl.when(not_first(way))(functools.partial(attn_came, way, 1))
            arrived = attn_slots[way * line + 1].astype(f32)
            total = total + jnp.where(not_first(way), arrived, 0.0)
        attn_reduced[0] = total.astype(bf16)
        columns = attn_reduced.at[0, :, pl.ds(2 * HD, HD)]
        own_keyval = pltpu.make_async_copy(columns, keyval_reduced.at[core], load_sem.at[1])
        own_keyval.start()

        def far_keyval(place):
            return remote(
                columns, keyval_reduced.at[place], core_send_sem.at[6], core_recv_sem.at[6], core_dev
            )

        far_keyval(core).start()
        far_keyval(core).wait_send()
        far_keyval(1 - core).wait_recv()
        own_keyval.wait()

    for k in (1, 2, 3):
        for copy in to_owner(k, True):
            copy.wait_recv()
        for copy in to_owner(k):
            copy.wait_send()
    for copy in own_done:
        copy.wait()
    own_input.wait()
    far_input(core).wait_send()
    far_input(1 - core).wait_recv()
    halves(False).wait_send()
    to_core.wait_send()
    pl.when(ctx > 0)(to_past.wait_send)
    exchange.wait_send()
    for place in range(n_dp):
        for k in (1, 2, 3):
            attn_plane(k, place, 0).wait_send()
            attn_plane(k, place, 1).wait_send()

    def first_left(way):
        for far in range(last_dp, 0, -1):
            attn_hop(way, far, True).wait_send()
            for k in turn:
                first_hop(way, far, k).wait_send()

    def left(way, far):
        attn_hop(way, far, False).wait_send()
        for k in turn:
            next_hop(way, far, k).wait_send()

    for way in range(2):
        if line > 1:
            pl.when(is_first(way))(functools.partial(first_left, way))
        for far in range(line - 2, 0, -1):
            pl.when(not_first(way) & has_goal(way, far))(functools.partial(left, way, far))


def retreat_call(n_dp, line, owned_heads, *arrays):
    tokens, attn_full, keyval = arrays[4], arrays[11], arrays[15]
    mlp_grads = arrays[18]
    row_count, width = tokens.shape
    half = row_count // 2
    blocks = n_dp * 4
    owned, hid = mlp_grads.shape[1], mlp_grads.shape[2] // 3
    attn_cols = attn_full.shape[1]
    reach = keyval.shape[1]
    behind = reach - row_count
    f32, bf16 = jnp.float32, jnp.bfloat16
    vmem = pl.BlockSpec(memory_space=pltpu.VMEM)
    anywhere = pl.BlockSpec(memory_space=pl.ANY)
    dma = pltpu.SemaphoreType.DMA
    return pl.pallas_call(
        functools.partial(retreat_kernel, n_dp, line, owned_heads),
        out_shape=(
            jax.ShapeDtypeStruct((row_count, width), f32),
            jax.ShapeDtypeStruct((4, owned, 2 * hid), bf16),
            jax.ShapeDtypeStruct((4, owned, hid), bf16),
            jax.ShapeDtypeStruct((n_dp if line == 1 else 1, owned, attn_cols), bf16),
            jax.ShapeDtypeStruct((2, owned, HD), bf16),
        ),
        in_specs=[
            anywhere if index < 5 or 11 <= index <= 16 or index >= 18 else vmem
            for index in range(len(arrays))
        ],
        out_specs=(anywhere, anywhere, anywhere, vmem, anywhere),
        scratch_shapes=[
            pltpu.VMEM((half, width), f32),
            pltpu.VMEM((max(8 * (line - 1), 4), owned, 3 * hid), bf16),
            pltpu.VMEM((max(width, 3 * half), attn_cols), f32),
            pltpu.VMEM((blocks, owned, attn_cols), bf16),
            pltpu.VMEM((3 * n_dp, owned, attn_cols), bf16),
            pltpu.VMEM((n_dp, owned, attn_cols), bf16),
            pltpu.VMEM((2 * line, owned, attn_cols), bf16),
            pltpu.VMEM((row_count, width), bf16),
            pltpu.VMEM((row_count, 2 * HD), bf16),
            pltpu.VMEM((row_count, 2 * HD), f32),
            pltpu.VMEM((row_count, 3 * HD), bf16),
            pltpu.VMEM((2, reach, HD), f32),
            pltpu.VMEM((2, reach, HD), bf16),
            pltpu.VMEM((reach, HD), bf16),
            pltpu.VMEM((behind, HD), bf16),
            pltpu.VMEM((half, width), f32),
            pltpu.VMEM((half, width), bf16),
            pltpu.VMEM((half, width), bf16),
            pltpu.VMEM((128, width), f32),
            pltpu.VMEM((8, width), f32),
            dma((8 * line,)),
            dma((8 * line,)),
            dma((8,)),
            dma((8,)),
            dma((6 * n_dp,)),
            dma((6 * n_dp,)),
            dma((2 * line,)),
            dma((2 * line,)),
            dma((7,)),
            dma((7,)),
            dma((12,)),
            dma((16,)),
            pltpu.VMEM(mlp_grads.shape, bf16),
        ]
        + [
            pltpu.VMEM(arrays[index].shape, arrays[index].dtype)
            for index in (3, 4, 11, 12, 13, 14, 15, 16)
        ],
        compiler_params=pltpu.CompilerParams(
            collective_id=2, has_side_effects=True, vmem_limit_bytes=63 * 2**20
        ),
        cost_estimate=pl.CostEstimate(
            flops=10**10, bytes_accessed=40 * 2**20, transcendentals=2 * 10**6
        ),
        name="retreat",
    )(*arrays)


def update_call(wide, passed, small_grads, attn_grads, keyval_grads, gate_grads, down_grads, *states):
    owned = states[0].shape[0]
    cols = states[0].shape[1]
    blocks = down_grads.shape[0]

    def whole(array):
        return pl.BlockSpec(array.shape, lambda i: (0,) * array.ndim)

    def step(state, new, gradient, rate, decay=decay_rate):
        results = adam_step(
            state[0][...], gradient.astype(jnp.float32), state[1][...], state[2][...], rate, decay
        )
        for target, result in zip(new, results):
            target[...] = result

    def kernel(first_in, second_in, small_ref, attn_ref, keyval_ref, gate_ref, down_ref, *refs):
        olds, news, first_out, second_out = refs[:21], refs[21:42], *refs[42:]
        first_out[...] = first_in[...]
        second_out[...] = second_in[...]
        step(olds[9:12], news[9:12], gate_ref[...], D ** (-0.5))
        step(olds[12:15], news[12:15], down_ref[0], FF ** (-0.5))

        @pl.when(pl.program_id(0) == 0)
        def _():
            step(olds[0:3], news[0:3], attn_ref[0, :, 0:cols], D ** (-0.5))
            keyval = jnp.concatenate([keyval_ref[0], keyval_ref[1]], axis=1)
            step(olds[3:6], news[3:6], keyval, D ** (-0.5))
            output = attn_ref[0, :, cols + HD : 2 * cols + HD]
            step(olds[6:9], news[6:9], output, (HQ * HD) ** (-0.5))
            step(olds[15:18], news[15:18], small_ref[0:4], 0.5, 0.0)
            step(olds[18:21], news[18:21], small_ref[4:6, 0 : olds[18].shape[1]], 0.5, 0.0)

    gate_block = pl.BlockSpec((owned, 2, wide), lambda i: (0, 0, i))
    down_block = pl.BlockSpec((owned, wide), lambda i: (0, i))
    state_blocks = [whole(array) for array in states[:9]] + [gate_block] * 3 + [down_block] * 3
    state_blocks += [whole(array) for array in states[15:]]
    passed_blocks = [
        pl.BlockSpec((array.shape[0] // blocks, array.shape[1]), lambda i: (i, 0))
        for array in passed
    ]
    return pl.pallas_call(
        kernel,
        grid=(blocks,),
        in_specs=[
            *passed_blocks,
            whole(small_grads),
            whole(attn_grads),
            whole(keyval_grads),
            gate_block,
            pl.BlockSpec((1, owned, wide), lambda i: (i, 0, 0)),
        ]
        + state_blocks,
        out_specs=tuple(state_blocks + passed_blocks),
        out_shape=tuple(jax.ShapeDtypeStruct(array.shape, array.dtype) for array in states + passed),
        compiler_params=pltpu.CompilerParams(vmem_limit_bytes=63 * 2**20 + 900 * 2**10),
        name="update",
    )(*passed, small_grads, attn_grads, keyval_grads, gate_grads, down_grads, *states)


def on_device(
    tokens,
    out_cotangent,
    lengths,
    norm_gains,
    gain_first,
    gain_second,
    head_gains,
    head_first,
    head_second,
    query_weight,
    query_first,
    query_second,
    keyval_weight,
    keyval_first,
    keyval_second,
    output_weight,
    output_first,
    output_second,
    gate_up,
    gate_first,
    gate_second,
    down_weight,
    down_first,
    down_second,
):
    bf16, f32 = jnp.bfloat16, jnp.float32
    row_count = tokens.shape[0]
    owned = query_weight.shape[0]
    owned_heads = head_gains.shape[0]
    n_dp, n_ctx = lax.axis_size("dp"), lax.axis_size("ctx")
    half_ff = gate_up.shape[2]
    wide = -(-half_ff // (n_ctx * 128)) * 128
    behind = WIN
    line = n_dp if n_dp <= 4 else 1
    ctx_place = lax.axis_index("ctx")
    core_first = lax.axis_index("tensor") == 0
    score_scale = HD ** (-0.5)

    head_columns = jnp.pad(head_gains, ((0, owned - owned_heads), (0, 0)))
    small = jnp.concatenate([norm_gains, head_columns], axis=1).astype(bf16)
    attn_pack = jnp.concatenate(
        [
            query_weight.astype(bf16),
            half_of(keyval_weight, 1).astype(bf16),
            output_weight.astype(bf16),
            jnp.pad(small, ((0, 0), (0, 122))),
        ],
        axis=1,
    )
    cols = query_weight.shape[1]

    def in_parts(array):
        padded = jnp.pad(array.astype(bf16), ((0, 0), (0, n_ctx * wide - half_ff)))
        return padded.reshape(owned, n_ctx, wide)

    mlp_pack = jnp.concatenate(
        [in_parts(gate_up[:, 0]), in_parts(gate_up[:, 1]), in_parts(down_weight)], axis=2
    )
    mlp_pack = jnp.moveaxis(mlp_pack, 1, 0)

    exponent = np.arange(HD // 2, dtype=np.float32) * np.float32(2.0 / HD)
    inverse = jnp.power(jnp.float32(rope_base), -jnp.asarray(exponent))[None]
    (
        mlp_full,
        gain_rows,
        head_rows,
        log_total,
        query_cosine,
        query_sine,
        lowest,
        attn_full,
        normed_one,
        lin,
        query_rot,
        keyval_all,
        attended_low,
        branch_raw,
        middle,
        group_rows,
    ) = attend_call(n_dp, owned_heads, behind, tokens, lengths, inverse, attn_pack, mlp_pack)
    result, normed_two_grad, gain_three_part, mlp_grads, early = mlp_call(
        n_dp,
        line,
        group_rows,
        middle,
        out_cotangent,
        gain_rows,
        mlp_full.reshape(n_dp * n_ctx * owned, 3 * wide),
    )


    mlp_grads = mlp_grads.reshape(n_dp, n_ctx, owned, 3 * wide)
    if line == 1:
        mlp_grads = lax.psum_scatter(mlp_grads, "dp", scatter_dimension=0, tiled=True)
    mlp_grads = mlp_grads.reshape(line * n_ctx, owned, 3 * wide)
    input_grad, gate_arrived, down_arrived, attn_reduced, keyval_both = retreat_call(
        n_dp,
        line,
        owned_heads,
        normed_two_grad,
        middle,
        branch_raw,
        out_cotangent,
        tokens,
        query_cosine,
        query_sine,
        lowest,
        gain_rows,
        head_rows,
        gain_three_part,
        attn_full,
        normed_one,
        lin,
        query_rot,
        keyval_all,
        attended_low,
        log_total,
        mlp_grads,
        early.reshape(early.shape[0], -1, owned, wide),
    )
    if line == 1:
        attn_reduced = lax.psum_scatter(attn_reduced, "dp", scatter_dimension=0, tiled=True)
        keyval_half = attn_reduced[0, :, cols : cols + HD]
        first, second = jnp.where(core_first, 0, 1), jnp.where(core_first, 1, 0)
        keyval_both = jnp.stack([keyval_half, lax.ppermute(keyval_half, "tensor", [(0, 1), (1, 0)])])
        keyval_both = jnp.stack([keyval_both[first], keyval_both[second]])
    gate_reduced = gate_arrived.reshape(n_ctx, owned, 2, wide)
    gate_reduced = gate_reduced.transpose(1, 2, 0, 3).reshape(owned, 2, n_ctx * wide)
    gate_reduced = lax.optimization_barrier(gate_reduced)
    (
        query_new,
        query_first_new,
        query_second_new,
        keyval_new,
        keyval_first_new,
        keyval_second_new,
        output_new,
        output_first_new,
        output_second_new,
        gate_new,
        gate_first_new,
        gate_second_new,
        down_new,
        down_first_new,
        down_second_new,
        *gains_updated,
        result,
        input_grad,
    ) = update_call(
        wide,
        (result, input_grad),
        attn_reduced[0, :, 2 * cols + HD :].astype(f32).T,
        attn_reduced,
        keyval_both,
        gate_reduced,
        down_arrived,
        query_weight,
        query_first,
        query_second,
        keyval_weight,
        keyval_first,
        keyval_second,
        output_weight,
        output_first,
        output_second,
        gate_up,
        gate_first,
        gate_second,
        down_weight,
        down_first,
        down_second,
        norm_gains.T,
        gain_first.T,
        gain_second.T,
        head_gains.T,
        head_first.T,
        head_second.T,
    )
    (
        gains_new,
        gain_first_new,
        gain_second_new,
        heads_new,
        head_first_new,
        head_second_new,
    ) = (new.T for new in gains_updated)
    return (
        result,
        input_grad,
        gains_new,
        gain_first_new,
        gain_second_new,
        heads_new,
        head_first_new,
        head_second_new,
        query_new,
        query_first_new,
        query_second_new,
        keyval_new,
        keyval_first_new,
        keyval_second_new,
        output_new,
        output_first_new,
        output_second_new,
        gate_new,
        gate_first_new,
        gate_second_new,
        down_new,
        down_first_new,
        down_second_new,
    )


def solution(mesh):
    placed = (
        P(("dp", "ctx"), None),
        P(("dp", "ctx"), None),
        P("dp", None),
        P(("dp", "ctx"), None),
        P(("dp", "ctx"), None),
        P(("dp", "ctx"), None),
        P(("dp", "ctx"), None),
        P(("dp", "ctx"), None),
        P(("dp", "ctx"), None),
        P(("dp", "ctx"), "tensor"),
        P(("dp", "ctx"), "tensor"),
        P(("dp", "ctx"), "tensor"),
        P(("dp", "ctx"), None),
        P(("dp", "ctx"), None),
        P(("dp", "ctx"), None),
        P(("dp", "ctx"), "tensor"),
        P(("dp", "ctx"), "tensor"),
        P(("dp", "ctx"), "tensor"),
        P(("dp", "ctx"), None, "tensor"),
        P(("dp", "ctx"), None, "tensor"),
        P(("dp", "ctx"), None, "tensor"),
        P(("dp", "ctx"), "tensor"),
        P(("dp", "ctx"), "tensor"),
        P(("dp", "ctx"), "tensor"),
    )
    return jax.shard_map(
        on_device,
        mesh=mesh,
        in_specs=placed,
        out_specs=(
            P(("dp", "ctx"), None),
            P(("dp", "ctx"), None),
            P(("dp", "ctx"), None),
            P(("dp", "ctx"), None),
            P(("dp", "ctx"), None),
            P(("dp", "ctx"), None),
            P(("dp", "ctx"), None),
            P(("dp", "ctx"), None),
            P(("dp", "ctx"), "tensor"),
            P(("dp", "ctx"), "tensor"),
            P(("dp", "ctx"), "tensor"),
            P(("dp", "ctx"), None),
            P(("dp", "ctx"), None),
            P(("dp", "ctx"), None),
            P(("dp", "ctx"), "tensor"),
            P(("dp", "ctx"), "tensor"),
            P(("dp", "ctx"), "tensor"),
            P(("dp", "ctx"), None, "tensor"),
            P(("dp", "ctx"), None, "tensor"),
            P(("dp", "ctx"), None, "tensor"),
            P(("dp", "ctx"), "tensor"),
            P(("dp", "ctx"), "tensor"),
            P(("dp", "ctx"), "tensor"),
        ),
        check_vma=False,
    )
```

```python
import functools

import jax
import jax.numpy as jnp
import numpy as np
from jax import lax
from jax.experimental import pallas as pl
from jax.experimental.pallas import tpu as pltpu
from jax.sharding import PartitionSpec as P

D = 1152
HQ = 4
HD = 256
FF = 6912
WIN = 512
STEP = 10


norm_eps = 1e-06
beta_one = 0.9
beta_two = 0.95
adam_eps = 1e-08
decay_rate = 0.1
rope_base = 10000.0
GELU_SCALE = float(np.sqrt(2.0 / np.pi))
MESH = pl.DeviceIdType.MESH


def half_of(array, dim):
    size = array.shape[dim] // 2
    return lax.dynamic_slice_in_dim(array, lax.axis_index("tensor") * size, size, axis=dim)


def contract_rows(left_side, right_side):
    return lax.dot_general(
        left_side, right_side, (((0,), (0,)), ((), ())), preferred_element_type=jnp.float32
    )


def contract_columns(left_side, right_side):
    return lax.dot_general(
        left_side, right_side, (((1,), (1,)), ((), ())), preferred_element_type=jnp.float32
    )


def adam_step(weight_value, gradient, first_moment, second_moment, step_rate, decay_factor):
    first_moment = beta_one * first_moment + (1.0 - beta_one) * gradient
    second_moment = beta_two * second_moment + (1.0 - beta_two) * gradient * gradient
    first_hat = first_moment / (1.0 - beta_one**STEP)
    second_hat = second_moment / (1.0 - beta_two**STEP)
    update = first_hat / (jnp.sqrt(second_hat) + adam_eps)
    return (
        weight_value - step_rate * (update + decay_factor * weight_value),
        first_moment,
        second_moment,
    )


def places():
    return lax.axis_index("dp"), lax.axis_index("ctx"), lax.axis_index("tensor")


def plane_partners():
    dp, ctx, core = places()
    beside = ctx + 1 - 2 * lax.rem(ctx, 2)
    across = lax.rem(ctx + 2, 4)
    return (dp, beside, core), (dp, across, core), (dp, 3 - ctx, core), (dp, ctx, 1 - core)


def enter(n_dp, line):
    dp, ctx, core = places()
    barrier = pltpu.get_barrier_semaphore()

    def greet(device):
        pl.semaphore_signal(barrier, inc=1, device_id=device, device_id_type=MESH)

    for device in plane_partners():
        greet(device)
    if line:
        pl.when(dp < n_dp - 1)(lambda: greet((dp + 1, ctx, core)))
        pl.when(dp > 0)(lambda: greet((dp - 1, ctx, core)))
    ends = jnp.minimum(dp, 1) + jnp.minimum(n_dp - 1 - dp, 1) if line else 0
    pl.semaphore_wait(barrier, 4 + ends)


def in_columns(count, body):
    whole = count // 256

    def one(i, carry):
        body(pl.multiple_of(i * 256, 256), 256)
        return carry

    lax.fori_loop(0, whole, one, 0)
    if count % 256:
        body(whole * 256, count % 256)


def in_rows(count, body, start):
    size = 64

    def one(i, carry):
        return body(pl.multiple_of(i * size, size), size, carry)

    return lax.fori_loop(0, count // size, one, start)


def gather_copies(remote, buffer, base):
    x_dev, y_dev, _, core_dev = plane_partners()
    h = buffer.shape[2] // 2
    part_a, part_b = pl.ds(0, h), pl.ds(h, h)

    def piece(step, side):
        return buffer.at[step, 0, side]

    return [
        remote(piece(0, part_a), piece(1, part_a), base, x_dev),
        remote(piece(0, part_b), piece(1, part_b), base + 1, y_dev),
        remote(piece(0, part_b), piece(2, part_b), base + 2, x_dev),
        remote(piece(0, part_a), piece(2, part_a), base + 3, y_dev),
        remote(piece(1, part_a), piece(3, part_a), base + 4, y_dev),
        remote(piece(1, part_b), piece(3, part_b), base + 5, x_dev),
    ] + [
        remote(buffer.at[step, 0], buffer.at[step, 1], base + 6 + step, core_dev)
        for step in range(4)
    ]


def gather_step(copies, step):
    if step == 0:
        for copy in copies[:4]:
            copy.start()
    elif step == 1:
        copies[0].wait_recv()
        copies[1].wait_recv()
        copies[4].start()
        copies[5].start()
    else:
        copies[2 * step - 2].wait_recv()
        copies[2 * step - 1].wait_recv()
    copies[6 + step].start()
    copies[6 + step].wait_recv()


def turned(values, cosine, sine):
    half_dim = values.shape[-1] // 2
    lower, upper = values[:, :half_dim], values[:, half_dim:]
    return jnp.concatenate([lower * cosine - upper * sine, upper * cosine + lower * sine], axis=1)


def scale_of(values):
    return lax.rsqrt(jnp.mean(values * values, axis=1, keepdims=True) + norm_eps)


def attend_kernel(
    n_dp,
    owned_heads,
    tokens_in,
    lengths,
    inverse,
    attn_pack,
    mlp_pack,
    mlp_full,
    gain_rows,
    head_rows,
    log_total,
    cosine,
    sine,
    lowest,
    attn_full_out,
    normed_out_out,
    lin_out,
    query_out_out,
    keyval_out,
    attended_out,
    branch_out_out,
    middle_out_out,
    rows_out,
    slots,
    wide_slots,
    keyval,
    partial,
    core_send,
    core_take,
    own_sem,
    mlp_plane_send,
    mlp_plane_recv,
    mlp_line_send,
    mlp_line_recv,
    attn_line_send,
    attn_line_recv,
    attn_plane_send,
    attn_plane_recv,
    keyval_send,
    keyval_recv,
    rows,
    rows_send,
    rows_recv,
    rows_sem,
    attn_full,
    normed_out,
    lin,
    query_out,
    attended,
    branch_out,
    middle_out,
    out_sem,
    tokens,
):
    dp, ctx, core = places()
    x_dev, y_dev, far_dev, core_dev = plane_partners()
    plane = ((dp, ctx, core), x_dev, y_dev, far_dev)
    f32, bf16 = jnp.float32, jnp.bfloat16
    row_count, width = tokens.shape
    half = row_count // 2
    owned = attn_pack.shape[0]
    behind = keyval.shape[1] - row_count
    next_dev = (dp, ctx + 1, core)
    enter(n_dp, True)

    def remote(source, target, send, recv, device):
        return pltpu.make_async_remote_copy(
            src_ref=source, dst_ref=target, send_sem=send, recv_sem=recv, device_id=device,
            device_id_type=MESH,
        )

    def line_block(way, step, k):
        origin = dp - step if way == 0 else dp + step
        return origin * 4 + plane[k][1]

    def can_take(way, step):
        return dp >= step if way == 0 else dp <= n_dp - 1 - step

    def can_give(way):
        return dp < n_dp - 1 if way == 0 else dp > 0

    def line_dev(way):
        return (dp + 1, ctx, core) if way == 0 else (dp - 1, ctx, core)

    def mlp_hop(way, step, k):
        block = mlp_full.at[line_block(way, step, k)]
        index = (way * n_dp + step) * 4 + k
        return remote(block, block, mlp_line_send.at[index], mlp_line_recv.at[index], line_dev(way))

    def mlp_came(way, step, k):
        block = mlp_full.at[line_block(way, step, k)]
        index = (way * n_dp + step - 1) * 4 + k
        return remote(block, block, mlp_line_send.at[index], mlp_line_recv.at[index], line_dev(way))

    def attn_hop(way, step):
        block = slots.at[line_block(way, step, 0)]
        index = way * n_dp + step
        return remote(block, block, attn_line_send.at[index], attn_line_recv.at[index], line_dev(way))

    def attn_came(way, step):
        block = slots.at[line_block(way, step, 0)]
        index = way * n_dp + step - 1
        return remote(block, block, attn_line_send.at[index], attn_line_recv.at[index], line_dev(way))

    def each(step, act, give):
        for way in range(2):
            if give:
                fits = can_give(way) & can_take(way, step) if step else can_give(way)
            else:
                fits = can_take(way, step)
            pl.when(fits)(functools.partial(act, way))

    def attn_plane(way, step, side, came=False):
        from_k = {1: 0, 2: 0, 3: 1 if step % 2 == 0 else 2}[side]
        device = {1: x_dev, 2: y_dev, 3: y_dev if step % 2 == 0 else x_dev}[side]
        block = slots.at[line_block(way, step, side if came else from_k)]
        index = (way * n_dp + step) * 4 + side
        return remote(block, block, attn_plane_send.at[index], attn_plane_recv.at[index], device)

    pending = []

    def give(source, target):
        copy = pltpu.make_async_copy(source, target, out_sem.at[len(pending)])
        copy.start()
        pending.append(copy)

    def first_hop(way, source, blocks, send, recv):
        return remote(source, blocks.at[dp * 4 + ctx], send, recv, line_dev(way))

    def attn_first(way):
        index = way * n_dp
        return first_hop(
            way, attn_pack, slots, attn_line_send.at[index], attn_line_recv.at[index]
        )

    def mlp_own(way):
        index = way * n_dp * 4
        return first_hop(
            way, mlp_pack.at[ctx], mlp_full, mlp_line_send.at[index], mlp_line_recv.at[index]
        )

    def attn_near(side):
        return remote(
            attn_pack,
            slots.at[dp * 4 + ctx],
            attn_plane_send.at[side],
            attn_plane_recv.at[side],
            plane[side],
        )

    own_attn = pltpu.make_async_copy(attn_pack, slots.at[dp * 4 + ctx], own_sem.at[0])
    own_tokens = pltpu.make_async_copy(tokens_in, tokens, own_sem.at[2])
    own_mlp = pltpu.make_async_copy(mlp_pack.at[ctx], mlp_full.at[dp * 4 + ctx], own_sem.at[1])
    own_attn.start()
    own_mlp.start()
    each(0, lambda way: attn_first(way).start(), True)
    for side in (1, 2):
        attn_near(side).start()
    each(0, lambda way: mlp_own(way).start(), True)

    def mlp_plane(k, came=False):
        return remote(
            mlp_pack.at[plane[k][1]],
            mlp_full.at[dp * 4 + (plane[k][1] if came else ctx)],
            mlp_plane_send.at[k],
            mlp_plane_recv.at[k],
            plane[k],
        )

    for k in (1, 2):
        mlp_plane(k).start()

    own_tokens.start()

    def place_rows(first, size, carry):
        at = pl.ds(first, size)
        row = first + lax.broadcasted_iota(jnp.int32, (size, 1), 0)
        position = ctx * row_count + row
        stop, begin = 0, jnp.zeros((size, 1), jnp.int32)
        for index in range(lengths.shape[1]):
            stop = stop + lengths[0, index]
            begin = begin + jnp.where(position >= stop, lengths[0, index], 0)
        position = position - begin
        lowest[at] = jnp.maximum(row - position + behind, row + 1)
        angles = position.astype(f32) * inverse[...]
        cosine[at] = jnp.cos(angles)
        sine[at] = jnp.sin(angles)
        return carry

    in_rows(row_count, place_rows, 0)

    def came(way, step):
        attn_came(way, step).wait_recv()

    def hand_on(way, step):
        for side in (1, 2):
            attn_plane(way, step, side).start()

    order = [(0, 0)] + [(way, step) for step in range(1, n_dp) for way in range(2)]

    def relay(way, step):
        for side in (1, 2):
            attn_plane(way, step, side, True).wait_recv()
        attn_plane(way, step, 3).start()

    def relayed(way, step):
        attn_plane(way, step, 3, True).wait_recv()

    def where_held(way, step, act):
        if step:
            pl.when(can_take(way, step))(lambda: act(way, step))
        else:
            act(way, step)

    def mlp_first(k):
        mlp_plane(k, True).wait_recv()
        each(0, lambda way: mlp_hop(way, 0, k).start(), True)

    def mlp_next(step, k):
        each(step, lambda way: mlp_came(way, step, k).wait_recv(), False)
        if step < n_dp - 1:
            each(step, lambda way: mlp_hop(way, step, k).start(), True)

    events = [functools.partial(mlp_first, k) for k in (1, 2, 3)] + [
        functools.partial(mlp_next, step, k) for step in range(1, n_dp) for k in range(4)
    ]
    events.reverse()

    def move(count):
        for _ in range(min(count, len(events))):
            events.pop()()

    own_attn.wait()
    for step in range(1, n_dp):
        each(step, lambda way: came(way, step), False)
        each(step, lambda way: attn_hop(way, step).start(), True)
        each(step, lambda way: hand_on(way, step), False)
        if step == 1:
            mlp_plane(3).start()
        if step <= 3:
            move(1)
    if n_dp == 1:
        mlp_plane(3).start()
    move(max(0, 4 - n_dp) + 2)
    for way, step in order:
        where_held(way, step, relay)
    move(1)
    for way, step in order:
        where_held(way, step, relayed)
    move(1)

    for block in range(n_dp * 4):
        wide_slots[block * owned : (block + 1) * owned, :] = slots[block].astype(f32)

    def narrow(first, size, carry):
        at = pl.ds(first, size)
        attn_full[at] = wide_slots[at].astype(bf16)
        return carry

    in_rows(width, narrow, 0)
    give(attn_full, attn_full_out)
    pick = lax.broadcasted_iota(jnp.int32, (8, 128), 0) == lax.broadcasted_iota(
        jnp.int32, (8, 128), 1
    )
    small = contract_columns(pick.astype(f32).astype(bf16), attn_full[:, 1280:1408])
    gain_rows[...] = small
    row_of = lax.broadcasted_iota(jnp.int32, (width, HD), 0)
    head_of = lax.broadcasted_iota(jnp.int32, (width, HD), 1)
    shift = owned_heads.bit_length() - 1
    chosen = row_of == (head_of >> shift) * owned + (head_of & (owned_heads - 1))
    heads = jnp.dot(
        small.astype(bf16), chosen.astype(f32).astype(bf16), preferred_element_type=f32
    )
    head_rows[...] = heads

    def normalize(first, size, carry):
        at = pl.ds(first, size)
        values = tokens[at].astype(f32)
        normed_out[at] = (values * scale_of(values) * gain_rows[0:1]).astype(bf16)
        return carry

    own_tokens.wait()
    in_rows(row_count, normalize, 0)

    def project(start, size):
        lin[:, pl.ds(start, size)] = jnp.dot(
            normed_out[...], attn_full[:, pl.ds(start, size)], preferred_element_type=f32
        )

    in_columns(3 * HD, project)
    give(normed_out, normed_out_out)
    give(lin, lin_out)

    def turn_keyval(first, size, carry):
        at = pl.ds(first, size)
        values = lin[at, 2 * HD : 3 * HD]
        keys = turned(values * scale_of(values) * head_rows[5:6], cosine[at], sine[at])
        mine = jnp.where(core == 0, keys, values).astype(bf16)
        keyval[core, pl.ds(pl.multiple_of(first + behind, 64), size)] = mine
        return carry

    in_rows(row_count, turn_keyval, 0)
    own_rows, last_rows = pl.ds(behind, row_count), pl.ds(row_count, behind)
    past_rows = pl.ds(0, behind)

    def to_core(came=False):
        block = keyval.at[1 - core if came else core, own_rows]
        return remote(block, block, keyval_send.at[0], keyval_recv.at[0], core_dev)

    def past_to_core(came=False):
        block = keyval.at[1 - core if came else core, past_rows]
        return remote(block, block, keyval_send.at[2], keyval_recv.at[2], core_dev)

    to_next = remote(
        keyval.at[core, last_rows],
        keyval.at[core, past_rows],
        keyval_send.at[1],
        keyval_recv.at[1],
        next_dev,
    )
    pl.when(ctx < 3)(to_next.start)
    to_core().start()

    def turn_query(first, size, carry):
        at = pl.ds(first, size)
        for head in range(2):
            values = lin[at, head * HD : (head + 1) * HD]
            normal = values * scale_of(values) * head_rows[4:5]
            query_out[head, at] = turned(normal, cosine[at], sine[at]).astype(bf16)
        return carry

    in_rows(row_count, turn_query, 0)
    give(query_out, query_out_out)

    @pl.when(ctx > 0)
    def _():
        to_next.wait_recv()
        past_to_core().start()
        past_to_core(True).wait_recv()

    @pl.when(ctx == 0)
    def _():
        keyval[:, 0:behind] = jnp.zeros((2, behind, HD), bf16)

    to_core(True).wait_recv()

    block_rows = 256
    reach = block_rows + behind

    def attend(first, head):
        at = pl.ds(first, block_rows)
        near = pl.ds(first, reach)
        scores = contract_columns(query_out[head, at], keyval[0, near]) * HD ** (-0.5)
        key_at = first + lax.broadcasted_iota(jnp.int32, (block_rows, reach), 1)
        query_at = first + behind + lax.broadcasted_iota(jnp.int32, (block_rows, reach), 0)
        scores = jnp.where((key_at >= lowest[at]) & (key_at <= query_at), scores, -1e30)
        row_max = jnp.max(scores, axis=1, keepdims=True)
        values = jnp.exp(scores - row_max)
        row_total = jnp.sum(values, axis=1, keepdims=True)
        probs = (values / row_total).astype(bf16)
        log_total[head, at] = row_max + jnp.log(row_total)
        out = jnp.dot(probs, keyval[1, near], preferred_element_type=f32)
        attended[at, head * HD : (head + 1) * HD] = out.astype(bf16)

    for block in range(row_count // block_rows):
        for head in range(2):
            attend(block * block_rows, head)
    give(attended, attended_out)
    give(keyval, keyval_out)
    move(2)

    def outward(start, size):
        partial[:, pl.ds(start, size)] = contract_columns(
            attended[...], attn_full[pl.ds(start, size), 3 * HD : 5 * HD]
        )

    in_columns(width, outward)

    def give_half(first, size, carry):
        at = pl.ds(pl.multiple_of((1 - core) * half + first, 64), size)
        core_send[pl.ds(first, size)] = partial[at].astype(bf16)
        return carry

    in_rows(half, give_half, 0)
    exchange = remote(core_send, core_take, keyval_send.at[3], keyval_recv.at[3], core_dev)
    exchange.start()
    move(1)
    exchange.wait_recv()

    def finish(first, size, carry):
        at = pl.ds(first, size)
        whole_at = pl.ds(pl.multiple_of(core * half + first, 64), size)
        branch = partial[whole_at] + core_take[at].astype(f32)
        branch_out[at] = branch
        middle = tokens[whole_at].astype(f32) + branch * scale_of(branch) * gain_rows[1:2]
        middle_out[at] = middle
        rows[0, 0, at] = (middle * scale_of(middle) * gain_rows[2:3]).astype(bf16)
        return carry

    in_rows(half, finish, 0)

    give(branch_out, branch_out_out)
    give(middle_out, middle_out_out)

    def remote_rows(source, target, index, device):
        return remote(source, target, rows_send.at[index], rows_recv.at[index], device)

    gather = gather_copies(remote_rows, rows, 0)
    outs = [
        pltpu.make_async_copy(rows.at[step], rows_out.at[step], rows_sem.at[step])
        for step in range(4)
    ]
    for step in range(4):
        gather_step(gather, step)
        outs[step].start()
        if step == 0:
            move(1)
    move(len(events))
    for copy in gather:
        copy.wait_send()
    for copy in outs + pending + [own_mlp]:
        copy.wait()

    exchange.wait_send()
    to_core().wait_send()
    pl.when(ctx < 3)(to_next.wait_send)
    pl.when(ctx > 0)(past_to_core().wait_send)
    for k in (1, 2, 3):
        mlp_plane(k).wait_send()
    each(0, lambda way: attn_first(way).wait_send(), True)
    each(0, lambda way: mlp_own(way).wait_send(), True)
    for step in range(n_dp - 1):
        if step:
            each(step, lambda way: attn_hop(way, step).wait_send(), True)
        for k in range(4):
            if step or k:
                each(step, lambda way: mlp_hop(way, step, k).wait_send(), True)

    def left(way, step):
        for side in (1, 2, 3):
            if step or side == 3:
                attn_plane(way, step, side).wait_send()
            else:
                attn_near(side).wait_send()

    for way, step in order:
        where_held(way, step, left)


def attend_call(n_dp, owned_heads, behind, tokens, lengths, inverse, attn_pack, mlp_pack):
    row_count, width = tokens.shape
    half = row_count // 2
    owned, attn_cols = attn_pack.shape
    blocks = n_dp * 4
    f32, bf16 = jnp.float32, jnp.bfloat16
    vmem = pl.BlockSpec(memory_space=pltpu.VMEM)
    anywhere = pl.BlockSpec(memory_space=pl.ANY)

    def array(dtype, *shape):
        return jax.ShapeDtypeStruct(shape, dtype)

    dma = pltpu.SemaphoreType.DMA
    return pl.pallas_call(
        functools.partial(attend_kernel, n_dp, owned_heads),
        out_shape=(
            array(bf16, blocks, owned, mlp_pack.shape[2]),
            array(f32, 8, width),
            array(f32, 8, HD),
            array(f32, 2, row_count, 1),
            array(f32, row_count, HD // 2),
            array(f32, row_count, HD // 2),
            array(jnp.int32, row_count, 1),
            array(bf16, width, attn_cols),
            array(bf16, row_count, width),
            array(f32, row_count, 3 * HD),
            array(bf16, 2, row_count, HD),
            array(bf16, 2, behind + row_count, HD),
            array(bf16, row_count, 2 * HD),
            array(f32, half, width),
            array(f32, half, width),
            array(bf16, 4, 2, half, width),
        ),
        in_specs=[
            anywhere,
            pl.BlockSpec(memory_space=pltpu.SMEM),
            vmem,
            anywhere,
            anywhere,
        ],
        out_specs=(anywhere,) + (vmem,) * 6 + (anywhere,) * 9,
        scratch_shapes=[
            pltpu.VMEM((blocks, owned, attn_cols), bf16),
            pltpu.VMEM((width, attn_cols), f32),
            pltpu.VMEM((2, behind + row_count, HD), bf16),
            pltpu.VMEM((row_count, width), f32),
            pltpu.VMEM((half, width), bf16),
            pltpu.VMEM((half, width), bf16),
            dma((3,)),
            dma((4,)),
            dma((4,)),
            dma((8 * n_dp,)),
            dma((8 * n_dp,)),
            dma((2 * n_dp,)),
            dma((2 * n_dp,)),
            dma((8 * n_dp,)),
            dma((8 * n_dp,)),
            dma((4,)),
            dma((4,)),
            pltpu.VMEM((4, 2, half, width), bf16),
            dma((10,)),
            dma((10,)),
            dma((4,)),
            pltpu.VMEM((width, attn_cols), bf16),
            pltpu.VMEM((row_count, width), bf16),
            pltpu.VMEM((row_count, 3 * HD), f32),
            pltpu.VMEM((2, row_count, HD), bf16),
            pltpu.VMEM((row_count, 2 * HD), bf16),
            pltpu.VMEM((half, width), f32),
            pltpu.VMEM((half, width), f32),
            dma((8,)),
            pltpu.VMEM((row_count, width), bf16),
        ],
        compiler_params=pltpu.CompilerParams(
            collective_id=1, has_side_effects=True, vmem_limit_bytes=60 * 2**20
        ),
        cost_estimate=pl.CostEstimate(
            flops=4 * 10**9, bytes_accessed=30 * 2**20, transcendentals=2 * 10**6
        ),
        name="attend",
    )(tokens, lengths, inverse, attn_pack, mlp_pack)


def mlp_kernel(
    n_dp,
    line,
    rows_in,
    middle_in,
    cotangent_in,
    gain_rows,
    weights_in,
    result_out,
    back_sum,
    gain_sum,
    weights_out,
    early,
    result,
    rows,
    grads,
    hidden,
    pair,
    weights,
    total,
    waiting,
    core_send,
    core_take,
    plane_send,
    plane_take,
    send_sem,
    recv_sem,
    load_sem,
    out_sem,
    middle,
    cotangent,
):
    half, width = middle.shape
    h = half // 2
    hid = hidden.shape[2]
    step_rows = 2 * half
    part_a, part_b = pl.ds(0, h), pl.ds(h, h)
    x_dev, y_dev, _, core_dev = plane_partners()
    core = lax.axis_index("tensor")
    gain = gain_rows.at[pl.ds(3, 1)]
    f32, bf16 = jnp.float32, jnp.bfloat16

    loads = [pltpu.make_async_copy(weights_in, weights, load_sem.at[4])] + [
        pltpu.make_async_copy(rows_in.at[step], rows.at[step], load_sem.at[step])
        for step in range(4)
    ]
    norm_loads = [
        pltpu.make_async_copy(middle_in, middle, load_sem.at[5]),
        pltpu.make_async_copy(cotangent_in, cotangent, load_sem.at[6]),
    ]
    for load in [loads[0], loads[4], loads[3], loads[2], loads[1]] + norm_loads:
        load.start()
    enter(n_dp, line > 1)

    def remote(source, target, index, device):
        return pltpu.make_async_remote_copy(
            src_ref=source,
            dst_ref=target,
            send_sem=send_sem.at[index],
            recv_sem=recv_sem.at[index],
            device_id=device,
            device_id_type=MESH,
        )

    def scatter_copies(base):
        return [
            remote(plane_send.at[0, part_a], plane_take.at[0, part_a], base, y_dev),
            remote(plane_send.at[0, part_b], plane_take.at[0, part_b], base + 1, x_dev),
            remote(plane_send.at[1, part_a], plane_take.at[1, part_a], base + 2, y_dev),
            remote(plane_send.at[1, part_b], plane_take.at[1, part_b], base + 3, x_dev),
            remote(plane_send.at[2, part_a], plane_take.at[2, part_a], base + 4, x_dev),
            remote(plane_send.at[2, part_b], plane_take.at[2, part_b], base + 5, y_dev),
        ] + [
            remote(core_send.at[step % 2], core_take.at[step], base + 6 + step, core_dev)
            for step in range(4)
        ]

    def scatter_step(copies, step, before, left, first):
        kept = (total, waiting, back_sum, back_sum)[step]
        slot = core_send.at[step % 2]
        if before is not None:
            copies[6 + before].wait_send()

        def part(rows, start, size):
            right = weights[pl.ds(start, size), first : first + left.shape[2]]
            return contract_columns(left[step, rows], right)

        def give(start, size):
            slot[:, pl.ds(start, size)] = part(pl.ds(half, half), start, size).astype(bf16)

        def keep(start, size):
            kept[:, pl.ds(start, size)] = part(pl.ds(0, half), start, size)

        in_columns(width, give)
        copies[6 + step].start()
        in_columns(width, keep)

    def scatter_rest(copies, step):
        kept = (total, waiting, back_sum, back_sum)[step]
        copies[6 + step].wait_recv()
        summed = kept[...] + core_take[step].astype(f32)
        if step < 2:
            kept[...] = summed
        else:
            plane_send[step - 2] = summed.astype(bf16)
            copies[2 * step - 4].start()
            copies[2 * step - 3].start()

    def scatter_end(copies):
        copies[2].wait_recv()
        copies[3].wait_recv()
        plane_send[2] = (waiting[...] + plane_take[1].astype(f32)).astype(bf16)
        copies[4].start()
        copies[5].start()

    def scatter_total(at):
        return total[at] + plane_take[0, at].astype(f32) + plane_take[2, at].astype(f32)

    def scatter_wait(copies):
        for index in (0, 1, 4, 5):
            copies[index].wait_recv()

    def sent(copies):
        for copy in copies:
            copy.wait_send()

    scatter = scatter_copies(0)
    loads[0].wait()
    for step in (3, 2, 1, 0):
        loads[1 + step].wait()

        def activate(start, size):
            def lin(first):
                return jnp.dot(
                    rows[step].reshape(step_rows, width),
                    weights[:, pl.ds(pl.multiple_of(first + start, 128), size)],
                    preferred_element_type=f32,
                )

            gate, up = lin(0), lin(hid)
            square = gate * gate
            chance = 0.5 + 0.5 * jnp.tanh(gate * (GELU_SCALE + GELU_SCALE * 0.044715 * square))
            gelu = gate * chance
            slope = chance + gelu * (1.0 - chance) * (
                2 * GELU_SCALE + 6 * GELU_SCALE * 0.044715 * square
            )
            hidden[step, :, pl.ds(start, size)] = (gelu * up).astype(bf16)
            pair[step, :, pl.ds(start, size)] = (slope * up).astype(bf16)
            pair[step, :, pl.ds(pl.multiple_of(hid + start, 128), size)] = gelu.astype(bf16)

        in_columns(hid, activate)
        scatter_step(scatter, step, step + 2 if step < 2 else None, hidden, 2 * hid)
        scatter_rest(scatter, step)
        if step == 1:
            scatter_end(scatter)
    scatter_wait(scatter)
    sent(scatter[:8])
    for load in norm_loads:
        load.wait()

    def norm_rows(first, size, gain_total):
        at = pl.ds(first, size)
        raw = scatter_total(at)
        scale = lax.rsqrt(jnp.mean(raw * raw, axis=1, keepdims=True) + norm_eps)
        normal = raw * scale
        result[at] = (middle[at] + normal * gain[...]).astype(bf16)
        cotangents = cotangent[pl.ds(pl.multiple_of(core * half + first, 64), size)].astype(f32)
        scaled = cotangents * gain[...]
        inner = jnp.mean(raw * scaled, axis=1, keepdims=True)
        back = scale * scaled - raw * (scale * scale * scale * inner)
        grads[0, 0, at] = back.astype(bf16)
        return gain_total + jnp.sum(cotangents * normal, axis=0, keepdims=True)

    gain_sum[...] = in_rows(half, norm_rows, jnp.zeros((1, width), f32))

    def result_rows(place):
        return result_out.at[pl.ds(pl.multiple_of(place * half, 64), half)]

    own_result = pltpu.make_async_copy(result, result_rows(core), out_sem.at[2])
    far_result = remote(result, result_rows(core), 30, core_dev)
    own_result.start()
    far_result.start()

    gather = gather_copies(remote, grads, 10)
    scatter = scatter_copies(20)
    for step in range(4):
        gather_step(gather, step)

        def unfold(start, size):
            hidden_grad = jnp.dot(
                grads[step].reshape(step_rows, width),
                weights[:, pl.ds(pl.multiple_of(2 * hid + start, 128), size)],
                preferred_element_type=f32,
            )
            hidden_grad = hidden_grad.astype(bf16)
            for first in (0, hid):
                at = pl.ds(pl.multiple_of(first + start, 128), size)
                pair[step, :, at] = pair[step, :, at] * hidden_grad

        in_columns(hid, unfold)
        if step:
            scatter_rest(scatter, step - 1)
        scatter_step(scatter, step, step - 2 if step >= 2 else None, pair, 0)
    scatter_rest(scatter, 3)
    sent(gather)

    dp, ctx, _ = places()
    last_dp = line - 1
    group = width // line
    chunk_rows = 384
    chunks = width // chunk_rows

    def weigh(first, left, right, i):
        chunk = jnp.where(2 * dp < n_dp, chunks - 1 - i, i)
        at = pl.ds(pl.multiple_of(chunk * chunk_rows, 128), chunk_rows)
        product = contract_rows(
            left[:, :, :, at].reshape(8 * half, chunk_rows),
            right[...].reshape(8 * half, right.shape[2]),
        )
        weights[at, first : first + right.shape[2]] = product.astype(bf16)

    def leave(first, count, index):
        columns = pl.ds(first, count)
        copy = pltpu.make_async_copy(
            weights.at[:, columns], weights_out.at[:, columns], out_sem.at[index]
        )
        copy.start()
        return copy

    def early_copy(way, index):
        place = last_dp - index if way == 0 else index
        first = pl.multiple_of(place * group, 8)
        device = (dp + 1, ctx, core) if way == 0 else (dp - 1, ctx, core)
        source = weights.at[pl.ds(first, group), pl.ds(2 * hid, hid)]
        item = 2 * index + way
        return remote(source, early.at[item], 31 + item, device)

    def sends_early(way):
        return dp == 0 if way == 0 else dp == last_dp

    for i in range(chunks):
        weigh(2 * hid, grads, hidden, i)
        for way, index in early_items(line):
            if i * chunk_rows < (index + 1) * group <= (i + 1) * chunk_rows:
                pl.when(sends_early(way))(early_copy(way, index).start)
    down_out = leave(2 * hid, hid, 1)
    weigh(0, rows, pair, 0)
    scatter_end(scatter)
    for i in range(1, chunks):
        weigh(0, rows, pair, i)
    gate_out = leave(0, 2 * hid, 0)
    scatter_wait(scatter)

    def finish_rows(first, size, carry):
        at = pl.ds(first, size)
        back_sum[at] = scatter_total(at)
        return carry

    in_rows(half, finish_rows, 0)
    sent(scatter[:6] + scatter[8:])
    if line > 1:
        for way, index in early_items(line):
            pl.when(sends_early(way))(early_copy(way, index).wait_send)
            pl.when(takes_early(way, dp, last_dp))(early_copy(way, index).wait_recv)
    down_out.wait()
    gate_out.wait()
    own_result.wait()
    far_result.wait_send()
    remote(result, result_rows(1 - core), 30, core_dev).wait_recv()


def early_items(line):
    return [(way, index) for index in range(min(2, line - 1)) for way in range(2)]


def takes_early(way, dp, last_dp):
    return dp == 1 if way == 0 else dp == last_dp - 1


def mlp_call(n_dp, line, rows, middle, cotangent, gain_rows, weights):
    half, width = middle.shape
    hid = weights.shape[1] // 3
    count = 8 * half
    f32, bf16 = jnp.float32, jnp.bfloat16
    vmem = pl.BlockSpec(memory_space=pltpu.VMEM)
    anywhere = pl.BlockSpec(memory_space=pl.ANY)
    return pl.pallas_call(
        functools.partial(mlp_kernel, n_dp, line),
        out_shape=(
            jax.ShapeDtypeStruct(cotangent.shape, bf16),
            jax.ShapeDtypeStruct((half, width), f32),
            jax.ShapeDtypeStruct((1, width), f32),
            jax.ShapeDtypeStruct((width, 3 * hid), bf16),
            jax.ShapeDtypeStruct((max(2, len(early_items(line))), width // line, hid), bf16),
        ),
        in_specs=[anywhere, anywhere, anywhere, vmem, anywhere],
        out_specs=(anywhere, vmem, vmem, anywhere, anywhere),
        scratch_shapes=[
            pltpu.VMEM((half, width), bf16),
            pltpu.VMEM((4, 2, half, width), bf16),
            pltpu.VMEM((4, 2, half, width), bf16),
            pltpu.VMEM((4, 2 * half, hid), bf16),
            pltpu.VMEM((4, 2 * half, 2 * hid), bf16),
            pltpu.VMEM((width, 3 * hid), bf16),
            pltpu.VMEM((half, width), f32),
            pltpu.VMEM((half, width), f32),
            pltpu.VMEM((2, half, width), bf16),
            pltpu.VMEM((4, half, width), bf16),
            pltpu.VMEM((3, half, width), bf16),
            pltpu.VMEM((3, half, width), bf16),
            pltpu.SemaphoreType.DMA((35,)),
            pltpu.SemaphoreType.DMA((35,)),
            pltpu.SemaphoreType.DMA((7,)),
            pltpu.SemaphoreType.DMA((3,)),
            pltpu.VMEM((half, width), f32),
            pltpu.VMEM(cotangent.shape, bf16),
        ],
        compiler_params=pltpu.CompilerParams(
            collective_id=0, has_side_effects=True, vmem_limit_bytes=63 * 2**20
        ),
        cost_estimate=pl.CostEstimate(
            flops=2 * count * width * hid * 9, bytes_accessed=30 * 2**20, transcendentals=count * hid
        ),
        name="feed_forward",
    )(rows, middle, cotangent, gain_rows, weights)


def norm_back(values, gains, grads):
    scale = scale_of(values)
    normal = values * scale
    scaled = grads * gains
    inner = jnp.mean(values * scaled, axis=1, keepdims=True)
    return scale * scaled - values * (scale * scale * scale * inner), grads * normal


def retreat_kernel(
    n_dp,
    line,
    owned_heads,
    back_sum,
    middle,
    branch,
    cotangent_in,
    tokens_in,
    cosine,
    sine,
    lowest,
    gain_rows,
    head_rows,
    gain_three,
    attn_full_in,
    normed_one_in,
    lin_in,
    query_in,
    keyval_in,
    attended_in,
    log_total,
    mlp_grads,
    early,
    input_whole,
    gate_reduced,
    down_reduced,
    attn_reduced,
    keyval_reduced,
    input_out,
    line_slots,
    attn_grads,
    attn_blocks,
    attn_plane_take,
    attn_sums,
    attn_slots,
    branch_low,
    attended_grad,
    query_grad,
    lin_grad,
    keyval_grad,
    keyval_send,
    keyval_take,
    past_take,
    partial,
    core_send,
    core_take,
    small_rows,
    small_take,
    line_send_sem,
    line_recv_sem,
    plane_send_sem,
    plane_recv_sem,
    attn_plane_send_sem,
    attn_plane_recv_sem,
    attn_line_send_sem,
    attn_line_recv_sem,
    core_send_sem,
    core_recv_sem,
    load_sem,
    early_sem,
    mlp_own,
    cotangent,
    tokens,
    attn_full,
    normed_one,
    lin,
    query,
    keyval,
    attended,
):
    dp, ctx, core = places()
    x_dev, y_dev, far_dev, core_dev = plane_partners()
    plane = ((dp, ctx, core), x_dev, y_dev, far_dev)
    f32, bf16 = jnp.float32, jnp.bfloat16
    row_count, width = tokens.shape
    half = row_count // 2
    owned, hid = mlp_grads.shape[1], mlp_grads.shape[2] // 3
    behind = keyval.shape[1] - row_count
    last_dp = line - 1
    here_dp = dp if line > 1 else 0
    early_count = len(early_items(line)) // 2
    sources = (
        (cotangent_in, cotangent),
        (attn_full_in, attn_full),
        (query_in, query),
        (keyval_in, keyval),
        (mlp_grads, mlp_own),
        (lin_in, lin),
        (attended_in, attended),
        (normed_one_in, normed_one),
        (tokens_in, tokens),
    )
    held = [
        pltpu.make_async_copy(source, target, load_sem.at[3 + index])
        for index, (source, target) in enumerate(sources)
    ]
    loads = [
        pltpu.make_async_copy(
            source,
            attn_grads.at[pl.ds(index * half, half), pl.ds(0, width)],
            load_sem.at[index],
        )
        for index, source in enumerate((middle, branch, back_sum))
    ]
    for load in loads + held:
        load.start()
    enter(n_dp, line > 1)

    def remote(source, target, send, recv, device):
        return pltpu.make_async_remote_copy(
            src_ref=source,
            dst_ref=target,
            send_sem=send,
            recv_sem=recv,
            device_id=device,
            device_id_type=MESH,
        )

    def goal(way, far):
        return dp + far if way == 0 else dp - far

    def has_goal(way, far):
        return dp + far <= last_dp if way == 0 else dp >= far

    def is_first(way):
        return dp == 0 if way == 0 else dp == last_dp

    def not_first(way):
        return dp > 0 if way == 0 else dp < last_dp

    def line_dev(way):
        return (dp + 1, ctx, core) if way == 0 else (dp - 1, ctx, core)

    def slot_of(way, far, k):
        return (way * last_dp + far - 1) * 4 + k

    def own_mlp(place, k):
        return mlp_own[place * 4 + plane[k][1]].astype(f32)

    def first_hop(way, far, k):
        slot = slot_of(way, far, k)
        columns = pl.ds(0, 2 * hid if last_dp - far < early_count else 3 * hid)
        return remote(
            mlp_grads.at[goal(way, far) * 4 + plane[k][1], :, columns],
            line_slots.at[slot, :, columns],
            line_send_sem.at[slot],
            line_recv_sem.at[slot],
            line_dev(way),
        )

    def next_hop(way, far, k):
        slot = slot_of(way, far, k)
        return remote(
            line_slots.at[slot_of(way, far + 1, k)],
            line_slots.at[slot],
            line_send_sem.at[slot],
            line_recv_sem.at[slot],
            line_dev(way),
        )

    def came(way, far, k):
        slot = slot_of(way, far, k)

        def wait(count):
            block = line_slots.at[slot, :, pl.ds(0, count)]
            remote(
                block, block, line_send_sem.at[slot], line_recv_sem.at[slot], line_dev(way)
            ).wait_recv()

        def wait_both():
            wait(2 * hid)
            early_load(way, last_dp - far, k).wait()

        if far == last_dp:
            wait_both()
        elif last_dp - far < early_count:
            beside_first = takes_early(way, dp, last_dp)
            pl.when(beside_first)(wait_both)
            pl.when(jnp.logical_not(beside_first))(functools.partial(wait, 3 * hid))
        else:
            wait(3 * hid)

    def early_load(way, index, k):
        return pltpu.make_async_copy(
            early.at[2 * index + way, plane[k][1]],
            line_slots.at[slot_of(way, last_dp - index, k), :, pl.ds(2 * hid, hid)],
            early_sem.at[(2 * index + way) * 4 + k],
        )

    def load_early(way):
        for index in range(early_count):
            for k in range(4):
                early_load(way, index, k).start()

    if line > 1:
        for way in range(2):
            pl.when(takes_early(way, dp, last_dp))(functools.partial(load_early, way))

    turn = (3, 1, 2, 0)

    def start_first(blocks):
        def start(way):
            for far, k in blocks:
                first_hop(way, far, k).start()

        for way in range(2):
            if line > 1:
                pl.when(is_first(way))(functools.partial(start, way))

    start_first([(far, k) for far in range(last_dp, 1, -1) for k in turn])

    def pass_on(way, far, k):
        came(way, far + 1, k)
        slot = slot_of(way, far + 1, k)
        line_slots[slot] = (line_slots[slot].astype(f32) + own_mlp(goal(way, far), k)).astype(bf16)
        next_hop(way, far, k).start()

    def mlp_step(far, k):
        for way in range(2):
            pl.when(not_first(way) & has_goal(way, far))(functools.partial(pass_on, way, far, k))

    parts = ((gate_reduced, pl.ds(0, 2 * hid)), (down_reduced, pl.ds(2 * hid, hid)))

    def to_owner(k, came=False):
        place = plane[k][1] if came else ctx
        return [
            remote(
                line_slots.at[k, :, columns],
                target.at[place],
                plane_send_sem.at[2 * k + index],
                plane_recv_sem.at[2 * k + index],
                plane[k],
            )
            for index, (target, columns) in enumerate(parts)
        ]

    own_done = [
        pltpu.make_async_copy(line_slots.at[0, :, columns], target.at[ctx], plane_send_sem.at[index])
        for index, (target, columns) in enumerate(parts)
    ]

    def mlp_last(k):
        if line > 1:
            for way in range(2):
                pl.when(not_first(way))(functools.partial(came, way, 1, k))
        total = own_mlp(here_dp, k)
        for way in range(2):
            if line > 1:
                arrived = line_slots[slot_of(way, 1, k)].astype(f32)
                total = total + jnp.where(not_first(way), arrived, 0.0)
        line_slots[k] = total.astype(bf16)
        for copy in to_owner(k) if k else own_done:
            copy.start()

    events = [
        functools.partial(mlp_step, far, k) for far in range(line - 2, 0, -1) for k in turn
    ] + [functools.partial(mlp_last, k) for k in turn]
    events.reverse()

    def move(count):
        for _ in range(min(count, len(events))):
            events.pop()()

    for load in loads + held[:1]:
        load.wait()

    def loaded(index, first, size):
        return attn_grads[pl.ds(pl.multiple_of(first + index * half, 64), size), 0:width]

    def norms(first, size, carry):
        at = pl.ds(first, size)
        part, gain_two = norm_back(loaded(0, first, size), gain_rows[2:3], loaded(2, first, size))
        whole_at = pl.ds(pl.multiple_of(core * half + first, 64), size)
        middle_grad = cotangent[whole_at].astype(f32) + part
        input_out[at] = middle_grad
        grad, gain_one = norm_back(loaded(1, first, size), gain_rows[1:2], middle_grad)
        branch_low[whole_at] = grad.astype(bf16)
        return (
            carry[0] + jnp.sum(gain_one, axis=0, keepdims=True),
            carry[1] + jnp.sum(gain_two, axis=0, keepdims=True),
        )

    nothing = jnp.zeros((1, width), f32)
    small_rows[...] = jnp.zeros_like(small_rows)
    gain_one, gain_two = in_rows(half, norms, (nothing, nothing))
    small_rows[1:2] = gain_one
    small_rows[2:3] = gain_two
    small_rows[3:4] = gain_three[...]

    def halves(came):
        rows = pl.ds(pl.multiple_of((1 - core if came else core) * half, 64), half)
        return remote(
            branch_low.at[rows], branch_low.at[rows], core_send_sem.at[0], core_recv_sem.at[0], core_dev
        )

    halves(False).start()
    halves(True).wait_recv()

    def inward(start, size):
        grad = jnp.dot(
            branch_low[...],
            attn_full[:, pl.ds(pl.multiple_of(3 * HD + start, 128), size)],
            preferred_element_type=f32,
        )
        attended_grad[:, pl.ds(start, size)] = grad.astype(bf16)

    held[1].wait()
    in_columns(2 * HD, inward)

    block_rows = 256
    reach = block_rows + behind
    keyval_grad[...] = jnp.zeros_like(keyval_grad)
    for load in held[2:5]:
        load.wait()

    def retreat(first, head):
        at = pl.ds(first, block_rows)
        near = pl.ds(first, reach)
        columns = slice(head * HD, (head + 1) * HD)
        scores = contract_columns(query[head, at], keyval[0, near]) * HD ** (-0.5)
        key_at = first + lax.broadcasted_iota(jnp.int32, (block_rows, reach), 1)
        query_at = first + behind + lax.broadcasted_iota(jnp.int32, (block_rows, reach), 0)
        scores = jnp.where((key_at >= lowest[at]) & (key_at <= query_at), scores, -1e30)
        probs = jnp.exp(scores - log_total[head, at])
        grads = attended_grad[at, columns]
        probs_grad = contract_columns(grads, keyval[1, near])
        delta = jnp.sum(probs * probs_grad, axis=1, keepdims=True)
        score_grad = (probs * (probs_grad - delta)).astype(bf16)
        query_grad[at, columns] = (
            jnp.dot(score_grad, keyval[0, near], preferred_element_type=f32) * HD ** (-0.5)
        )
        keyval_grad[0, near] += contract_rows(score_grad, query[head, at]) * HD ** (-0.5)
        keyval_grad[1, near] += contract_rows(probs.astype(bf16), grads)

    for block in range(row_count // block_rows):
        for head in range(2):
            retreat(block * block_rows, head)
    move(2)

    keyval_send[0] = keyval_grad[1 - core].astype(bf16)
    to_core = remote(
        keyval_send.at[0], keyval_take, core_send_sem.at[1], core_recv_sem.at[1], core_dev
    )
    to_core.start()

    def query_rows(first, size, carry):
        at = pl.ds(first, size)
        total = carry
        for head in range(2):
            columns = slice(head * HD, (head + 1) * HD)
            grads = turned(query_grad[at, columns], cosine[at], -sine[at])
            grad, gain = norm_back(lin[at, columns], head_rows[4:5], grads)
            lin_grad[at, columns] = grad.astype(bf16)
            total = total + jnp.sum(gain, axis=0, keepdims=True)
        return total

    for load in held[5:]:
        load.wait()
    head_zero = in_rows(row_count, query_rows, jnp.zeros((1, HD), f32))
    move(1)
    to_core.wait_recv()
    keyval_grad[core] = keyval_grad[core] + keyval_take[...].astype(f32)
    keyval_send[1, 0:behind] = keyval_grad[core, 0:behind].astype(bf16)
    to_past = remote(
        keyval_send.at[1, pl.ds(0, behind)],
        past_take,
        core_send_sem.at[2],
        core_recv_sem.at[2],
        (dp, ctx - 1, core),
    )
    pl.when(ctx > 0)(to_past.start)

    def outward(start, size):
        attn_grads[0:width, pl.ds(pl.multiple_of(3 * HD + start, 128), size)] = contract_rows(
            branch_low[...], attended[:, pl.ds(start, size)]
        )

    in_columns(2 * HD, outward)

    @pl.when(ctx < 3)
    def _():
        to_past.wait_recv()
        late = pl.ds(row_count, behind)
        keyval_grad[core, late] = keyval_grad[core, late] + past_take[...].astype(f32)

    def keyval_rows(first, size, carry):
        at = pl.ds(first, size)
        values = keyval_grad[core, pl.ds(pl.multiple_of(first + behind, 64), size)]
        grads = turned(values, cosine[at], -sine[at])
        grad, gain = norm_back(lin[at, 2 * HD : 3 * HD], head_rows[5:6], grads)
        lin_grad[at, 2 * HD : 3 * HD] = jnp.where(core == 0, grad, values).astype(bf16)
        return carry + jnp.sum(gain, axis=0, keepdims=True)

    head_one = in_rows(row_count, keyval_rows, jnp.zeros((1, HD), f32))
    head_one = jnp.where(core == 0, head_one, 0.0)

    def weigh(start, size):
        attn_grads[0:width, pl.ds(start, size)] = contract_rows(
            normed_one[...], lin_grad[:, pl.ds(start, size)]
        )

    in_columns(3 * HD, weigh)

    attn_parts = ((0, 5 * HD), (5 * HD, 128))

    def attn_plane(k, place, part):
        index = (k - 1) * n_dp + place
        columns = pl.ds(*attn_parts[part])
        return remote(
            attn_blocks.at[place * 4 + plane[k][1], :, columns],
            attn_plane_take.at[index, :, columns],
            attn_plane_send_sem.at[2 * index + part],
            attn_plane_recv_sem.at[2 * index + part],
            plane[k],
        )

    def give_attn(part):
        first, count = attn_parts[part]
        for block in range(n_dp * 4):
            attn_blocks[block, :, first : first + count] = attn_grads[
                block * owned : (block + 1) * owned, first : first + count
            ].astype(bf16)
        for place in range(n_dp):
            for k in (3, 1, 2):
                attn_plane(k, place, part).start()

    give_attn(0)
    move(1)
    start_first([(1, k) for k in turn])

    def back(start, size):
        columns = pl.ds(start, size)
        product = contract_columns(lin_grad[...], attn_full[columns, 0 : 3 * HD])
        first, second = product[:half], product[half:]
        partial[:, columns] = jnp.where(core == 0, first, second)
        core_send[:, columns] = jnp.where(core == 0, second, first).astype(bf16)

    in_columns(width, back)
    exchange = remote(core_send, core_take, core_send_sem.at[3], core_recv_sem.at[3], core_dev)
    exchange.start()
    exchange.wait_recv()

    def finish(first, size, carry):
        at = pl.ds(first, size)
        whole_at = pl.ds(pl.multiple_of(core * half + first, 64), size)
        grads = partial[at] + core_take[at].astype(f32)
        part, gain = norm_back(tokens[whole_at].astype(f32), gain_rows[0:1], grads)
        input_out[at] = input_out[at] + part
        return carry + jnp.sum(gain, axis=0, keepdims=True)

    small_rows[0:1] = in_rows(half, finish, nothing)

    def input_rows(place):
        return input_whole.at[pl.ds(pl.multiple_of(place * half, 64), half)]

    own_input = pltpu.make_async_copy(input_out, input_rows(core), load_sem.at[0])
    own_input.start()

    def far_input(place):
        return remote(
            input_out, input_rows(place), core_send_sem.at[5], core_recv_sem.at[5], core_dev
        )

    far_input(core).start()

    row_of = lax.broadcasted_iota(jnp.int32, (width, HD), 0)
    head_of = lax.broadcasted_iota(jnp.int32, (width, HD), 1)
    shift = owned_heads.bit_length() - 1
    chosen = row_of == (head_of >> shift) * owned + (head_of & (owned_heads - 1))
    heads = jnp.concatenate([head_zero, head_one, jnp.zeros((6, HD), f32)], axis=0)
    spread = contract_columns(heads.astype(bf16), chosen.astype(f32).astype(bf16))
    small_rows[4:6] = spread[0:2]
    smalls = remote(
        small_rows.at[pl.ds(0, 8)], small_take, core_send_sem.at[4], core_recv_sem.at[4], core_dev
    )
    smalls.start()
    smalls.wait_recv()
    smalls.wait_send()
    small_rows[0:8] = small_rows[0:8] + small_take[...]
    attn_grads[0:width, 5 * HD : 5 * HD + 128] = small_rows[...].T

    give_attn(1)
    move(len(events) - 4)
    for place in range(n_dp):
        total = attn_blocks[place * 4 + ctx].astype(f32)
        for k in (1, 2, 3):
            attn_plane(k, place, 0).wait_recv()
            attn_plane(k, place, 1).wait_recv()
            total = total + attn_plane_take[(k - 1) * n_dp + place].astype(f32)
        attn_sums[place] = total.astype(bf16)

    def attn_hop(way, far, first):
        source = attn_sums.at[goal(way, far)] if first else attn_slots.at[way * line + far + 1]
        index = way * line + far
        return remote(
            source,
            attn_slots.at[index],
            attn_line_send_sem.at[index],
            attn_line_recv_sem.at[index],
            line_dev(way),
        )

    def attn_came(way, far):
        index = way * line + far
        block = attn_slots.at[index]
        remote(
            block, block, attn_line_send_sem.at[index], attn_line_recv_sem.at[index], line_dev(way)
        ).wait_recv()

    def attn_start(way):
        for far in range(last_dp, 0, -1):
            attn_hop(way, far, True).start()

    def attn_pass(way, far):
        attn_came(way, far + 1)
        index = way * line + far + 1
        total = attn_slots[index].astype(f32) + attn_sums[goal(way, far)].astype(f32)
        attn_slots[index] = total.astype(bf16)
        attn_hop(way, far, False).start()

    for way in range(2):
        if line > 1:
            pl.when(is_first(way))(functools.partial(attn_start, way))
    move(4)
    for far in range(line - 2, 0, -1):
        for way in range(2):
            pl.when(not_first(way) & has_goal(way, far))(functools.partial(attn_pass, way, far))
    if line == 1:
        attn_reduced[...] = attn_sums[...]
    else:
        total = attn_sums[dp].astype(f32)
        for way in range(2):
            pl.when(not_first(way))(functools.partial(attn_came, way, 1))
            arrived = attn_slots[way * line + 1].astype(f32)
            total = total + jnp.where(not_first(way), arrived, 0.0)
        attn_reduced[0] = total.astype(bf16)
        columns = attn_reduced.at[0, :, pl.ds(2 * HD, HD)]
        own_keyval = pltpu.make_async_copy(columns, keyval_reduced.at[core], load_sem.at[1])
        own_keyval.start()

        def far_keyval(place):
            return remote(
                columns, keyval_reduced.at[place], core_send_sem.at[6], core_recv_sem.at[6], core_dev
            )

        far_keyval(core).start()
        far_keyval(core).wait_send()
        far_keyval(1 - core).wait_recv()
        own_keyval.wait()

    for k in (1, 2, 3):
        for copy in to_owner(k, True):
            copy.wait_recv()
        for copy in to_owner(k):
            copy.wait_send()
    for copy in own_done:
        copy.wait()
    own_input.wait()
    far_input(core).wait_send()
    far_input(1 - core).wait_recv()
    halves(False).wait_send()
    to_core.wait_send()
    pl.when(ctx > 0)(to_past.wait_send)
    exchange.wait_send()
    for place in range(n_dp):
        for k in (1, 2, 3):
            attn_plane(k, place, 0).wait_send()
            attn_plane(k, place, 1).wait_send()

    def first_left(way):
        for far in range(last_dp, 0, -1):
            attn_hop(way, far, True).wait_send()
            for k in turn:
                first_hop(way, far, k).wait_send()

    def left(way, far):
        attn_hop(way, far, False).wait_send()
        for k in turn:
            next_hop(way, far, k).wait_send()

    for way in range(2):
        if line > 1:
            pl.when(is_first(way))(functools.partial(first_left, way))
        for far in range(line - 2, 0, -1):
            pl.when(not_first(way) & has_goal(way, far))(functools.partial(left, way, far))


def retreat_call(n_dp, line, owned_heads, *arrays):
    tokens, attn_full, keyval = arrays[4], arrays[11], arrays[15]
    mlp_grads = arrays[18]
    row_count, width = tokens.shape
    half = row_count // 2
    blocks = n_dp * 4
    owned, hid = mlp_grads.shape[1], mlp_grads.shape[2] // 3
    attn_cols = attn_full.shape[1]
    reach = keyval.shape[1]
    behind = reach - row_count
    f32, bf16 = jnp.float32, jnp.bfloat16
    vmem = pl.BlockSpec(memory_space=pltpu.VMEM)
    anywhere = pl.BlockSpec(memory_space=pl.ANY)
    dma = pltpu.SemaphoreType.DMA
    return pl.pallas_call(
        functools.partial(retreat_kernel, n_dp, line, owned_heads),
        out_shape=(
            jax.ShapeDtypeStruct((row_count, width), f32),
            jax.ShapeDtypeStruct((4, owned, 2 * hid), bf16),
            jax.ShapeDtypeStruct((4, owned, hid), bf16),
            jax.ShapeDtypeStruct((n_dp if line == 1 else 1, owned, attn_cols), bf16),
            jax.ShapeDtypeStruct((2, owned, HD), bf16),
        ),
        in_specs=[
            anywhere if index < 5 or 11 <= index <= 16 or index >= 18 else vmem
            for index in range(len(arrays))
        ],
        out_specs=(anywhere, anywhere, anywhere, vmem, anywhere),
        scratch_shapes=[
            pltpu.VMEM((half, width), f32),
            pltpu.VMEM((max(8 * (line - 1), 4), owned, 3 * hid), bf16),
            pltpu.VMEM((max(width, 3 * half), attn_cols), f32),
            pltpu.VMEM((blocks, owned, attn_cols), bf16),
            pltpu.VMEM((3 * n_dp, owned, attn_cols), bf16),
            pltpu.VMEM((n_dp, owned, attn_cols), bf16),
            pltpu.VMEM((2 * line, owned, attn_cols), bf16),
            pltpu.VMEM((row_count, width), bf16),
            pltpu.VMEM((row_count, 2 * HD), bf16),
            pltpu.VMEM((row_count, 2 * HD), f32),
            pltpu.VMEM((row_count, 3 * HD), bf16),
            pltpu.VMEM((2, reach, HD), f32),
            pltpu.VMEM((2, reach, HD), bf16),
            pltpu.VMEM((reach, HD), bf16),
            pltpu.VMEM((behind, HD), bf16),
            pltpu.VMEM((half, width), f32),
            pltpu.VMEM((half, width), bf16),
            pltpu.VMEM((half, width), bf16),
            pltpu.VMEM((128, width), f32),
            pltpu.VMEM((8, width), f32),
            dma((8 * line,)),
            dma((8 * line,)),
            dma((8,)),
            dma((8,)),
            dma((6 * n_dp,)),
            dma((6 * n_dp,)),
            dma((2 * line,)),
            dma((2 * line,)),
            dma((7,)),
            dma((7,)),
            dma((12,)),
            dma((16,)),
            pltpu.VMEM(mlp_grads.shape, bf16),
        ]
        + [
            pltpu.VMEM(arrays[index].shape, arrays[index].dtype)
            for index in (3, 4, 11, 12, 13, 14, 15, 16)
        ],
        compiler_params=pltpu.CompilerParams(
            collective_id=2, has_side_effects=True, vmem_limit_bytes=63 * 2**20
        ),
        cost_estimate=pl.CostEstimate(
            flops=10**10, bytes_accessed=40 * 2**20, transcendentals=2 * 10**6
        ),
        name="retreat",
    )(*arrays)


def update_call(wide, passed, small_grads, attn_grads, keyval_grads, gate_grads, down_grads, *states):
    owned = states[0].shape[0]
    cols = states[0].shape[1]
    blocks = down_grads.shape[0]

    def whole(array):
        return pl.BlockSpec(array.shape, lambda i: (0,) * array.ndim)

    def step(state, new, gradient, rate, decay=decay_rate):
        results = adam_step(
            state[0][...], gradient.astype(jnp.float32), state[1][...], state[2][...], rate, decay
        )
        for target, result in zip(new, results):
            target[...] = result

    def kernel(first_in, second_in, small_ref, attn_ref, keyval_ref, gate_ref, down_ref, *refs):
        olds, news, first_out, second_out = refs[:21], refs[21:42], *refs[42:]
        first_out[...] = first_in[...]
        second_out[...] = second_in[...]
        step(olds[9:12], news[9:12], gate_ref[...], D ** (-0.5))
        step(olds[12:15], news[12:15], down_ref[0], FF ** (-0.5))

        @pl.when(pl.program_id(0) == 0)
        def _():
            step(olds[0:3], news[0:3], attn_ref[0, :, 0:cols], D ** (-0.5))
            keyval = jnp.concatenate([keyval_ref[0], keyval_ref[1]], axis=1)
            step(olds[3:6], news[3:6], keyval, D ** (-0.5))
            output = attn_ref[0, :, cols + HD : 2 * cols + HD]
            step(olds[6:9], news[6:9], output, (HQ * HD) ** (-0.5))
            step(olds[15:18], news[15:18], small_ref[0:4], 0.5, 0.0)
            step(olds[18:21], news[18:21], small_ref[4:6, 0 : olds[18].shape[1]], 0.5, 0.0)

    gate_block = pl.BlockSpec((owned, 2, wide), lambda i: (0, 0, i))
    down_block = pl.BlockSpec((owned, wide), lambda i: (0, i))
    state_blocks = [whole(array) for array in states[:9]] + [gate_block] * 3 + [down_block] * 3
    state_blocks += [whole(array) for array in states[15:]]
    passed_blocks = [
        pl.BlockSpec((array.shape[0] // blocks, array.shape[1]), lambda i: (i, 0))
        for array in passed
    ]
    return pl.pallas_call(
        kernel,
        grid=(blocks,),
        in_specs=[
            *passed_blocks,
            whole(small_grads),
            whole(attn_grads),
            whole(keyval_grads),
            gate_block,
            pl.BlockSpec((1, owned, wide), lambda i: (i, 0, 0)),
        ]
        + state_blocks,
        out_specs=tuple(state_blocks + passed_blocks),
        out_shape=tuple(jax.ShapeDtypeStruct(array.shape, array.dtype) for array in states + passed),
        compiler_params=pltpu.CompilerParams(vmem_limit_bytes=63 * 2**20 + 900 * 2**10),
        name="update",
    )(*passed, small_grads, attn_grads, keyval_grads, gate_grads, down_grads, *states)


def on_device(
    tokens,
    out_cotangent,
    lengths,
    norm_gains,
    gain_first,
    gain_second,
    head_gains,
    head_first,
    head_second,
    query_weight,
    query_first,
    query_second,
    keyval_weight,
    keyval_first,
    keyval_second,
    output_weight,
    output_first,
    output_second,
    gate_up,
    gate_first,
    gate_second,
    down_weight,
    down_first,
    down_second,
):
    bf16, f32 = jnp.bfloat16, jnp.float32
    row_count = tokens.shape[0]
    owned = query_weight.shape[0]
    owned_heads = head_gains.shape[0]
    n_dp, n_ctx = lax.axis_size("dp"), lax.axis_size("ctx")
    half_ff = gate_up.shape[2]
    wide = -(-half_ff // (n_ctx * 128)) * 128
    behind = WIN
    line = n_dp if n_dp <= 4 else 1
    ctx_place = lax.axis_index("ctx")
    core_first = lax.axis_index("tensor") == 0
    score_scale = HD ** (-0.5)

    head_columns = jnp.pad(head_gains, ((0, owned - owned_heads), (0, 0)))
    small = jnp.concatenate([norm_gains, head_columns], axis=1).astype(bf16)
    attn_pack = jnp.concatenate(
        [
            query_weight.astype(bf16),
            half_of(keyval_weight, 1).astype(bf16),
            output_weight.astype(bf16),
            jnp.pad(small, ((0, 0), (0, 122))),
        ],
        axis=1,
    )
    cols = query_weight.shape[1]

    def in_parts(array):
        padded = jnp.pad(array.astype(bf16), ((0, 0), (0, n_ctx * wide - half_ff)))
        return padded.reshape(owned, n_ctx, wide)

    mlp_pack = jnp.concatenate(
        [in_parts(gate_up[:, 0]), in_parts(gate_up[:, 1]), in_parts(down_weight)], axis=2
    )
    mlp_pack = jnp.moveaxis(mlp_pack, 1, 0)

    exponent = np.arange(HD // 2, dtype=np.float32) * np.float32(2.0 / HD)
    inverse = jnp.power(jnp.float32(rope_base), -jnp.asarray(exponent))[None]
    (
        mlp_full,
        gain_rows,
        head_rows,
        log_total,
        query_cosine,
        query_sine,
        lowest,
        attn_full,
        normed_one,
        lin,
        query_rot,
        keyval_all,
        attended_low,
        branch_raw,
        middle,
        group_rows,
    ) = attend_call(n_dp, owned_heads, behind, tokens, lengths, inverse, attn_pack, mlp_pack)
    result, normed_two_grad, gain_three_part, mlp_grads, early = mlp_call(
        n_dp,
        line,
        group_rows,
        middle,
        out_cotangent,
        gain_rows,
        mlp_full.reshape(n_dp * n_ctx * owned, 3 * wide),
    )


    mlp_grads = mlp_grads.reshape(n_dp, n_ctx, owned, 3 * wide)
    if line == 1:
        mlp_grads = lax.psum_scatter(mlp_grads, "dp", scatter_dimension=0, tiled=True)
    mlp_grads = mlp_grads.reshape(line * n_ctx, owned, 3 * wide)
    input_grad, gate_arrived, down_arrived, attn_reduced, keyval_both = retreat_call(
        n_dp,
        line,
        owned_heads,
        normed_two_grad,
        middle,
        branch_raw,
        out_cotangent,
        tokens,
        query_cosine,
        query_sine,
        lowest,
        gain_rows,
        head_rows,
        gain_three_part,
        attn_full,
        normed_one,
        lin,
        query_rot,
        keyval_all,
        attended_low,
        log_total,
        mlp_grads,
        early.reshape(early.shape[0], -1, owned, wide),
    )
    if line == 1:
        attn_reduced = lax.psum_scatter(attn_reduced, "dp", scatter_dimension=0, tiled=True)
        keyval_half = attn_reduced[0, :, cols : cols + HD]
        first, second = jnp.where(core_first, 0, 1), jnp.where(core_first, 1, 0)
        keyval_both = jnp.stack([keyval_half, lax.ppermute(keyval_half, "tensor", [(0, 1), (1, 0)])])
        keyval_both = jnp.stack([keyval_both[first], keyval_both[second]])
    gate_reduced = gate_arrived.reshape(n_ctx, owned, 2, wide)
    gate_reduced = gate_reduced.transpose(1, 2, 0, 3).reshape(owned, 2, n_ctx * wide)
    gate_reduced = lax.optimization_barrier(gate_reduced)
    (
        query_new,
        query_first_new,
        query_second_new,
        keyval_new,
        keyval_first_new,
        keyval_second_new,
        output_new,
        output_first_new,
        output_second_new,
        gate_new,
        gate_first_new,
        gate_second_new,
        down_new,
        down_first_new,
        down_second_new,
        *gains_updated,
        result,
        input_grad,
    ) = update_call(
        wide,
        (result, input_grad),
        attn_reduced[0, :, 2 * cols + HD :].astype(f32).T,
        attn_reduced,
        keyval_both,
        gate_reduced,
        down_arrived,
        query_weight,
        query_first,
        query_second,
        keyval_weight,
        keyval_first,
        keyval_second,
        output_weight,
        output_first,
        output_second,
        gate_up,
        gate_first,
        gate_second,
        down_weight,
        down_first,
        down_second,
        norm_gains.T,
        gain_first.T,
        gain_second.T,
        head_gains.T,
        head_first.T,
        head_second.T,
    )
    (
        gains_new,
        gain_first_new,
        gain_second_new,
        heads_new,
        head_first_new,
        head_second_new,
    ) = (new.T for new in gains_updated)
    return (
        result,
        input_grad,
        gains_new,
        gain_first_new,
        gain_second_new,
        heads_new,
        head_first_new,
        head_second_new,
        query_new,
        query_first_new,
        query_second_new,
        keyval_new,
        keyval_first_new,
        keyval_second_new,
        output_new,
        output_first_new,
        output_second_new,
        gate_new,
        gate_first_new,
        gate_second_new,
        down_new,
        down_first_new,
        down_second_new,
    )


def solution(mesh):
    placed = (
        P(("dp", "ctx"), None),
        P(("dp", "ctx"), None),
        P("dp", None),
        P(("dp", "ctx"), None),
        P(("dp", "ctx"), None),
        P(("dp", "ctx"), None),
        P(("dp", "ctx"), None),
        P(("dp", "ctx"), None),
        P(("dp", "ctx"), None),
        P(("dp", "ctx"), "tensor"),
        P(("dp", "ctx"), "tensor"),
        P(("dp", "ctx"), "tensor"),
        P(("dp", "ctx"), None),
        P(("dp", "ctx"), None),
        P(("dp", "ctx"), None),
        P(("dp", "ctx"), "tensor"),
        P(("dp", "ctx"), "tensor"),
        P(("dp", "ctx"), "tensor"),
        P(("dp", "ctx"), None, "tensor"),
        P(("dp", "ctx"), None, "tensor"),
        P(("dp", "ctx"), None, "tensor"),
        P(("dp", "ctx"), "tensor"),
        P(("dp", "ctx"), "tensor"),
        P(("dp", "ctx"), "tensor"),
    )
    return jax.shard_map(
        on_device,
        mesh=mesh,
        in_specs=placed,
        out_specs=(
            P(("dp", "ctx"), None),
            P(("dp", "ctx"), None),
            P(("dp", "ctx"), None),
            P(("dp", "ctx"), None),
            P(("dp", "ctx"), None),
            P(("dp", "ctx"), None),
            P(("dp", "ctx"), None),
            P(("dp", "ctx"), None),
            P(("dp", "ctx"), "tensor"),
            P(("dp", "ctx"), "tensor"),
            P(("dp", "ctx"), "tensor"),
            P(("dp", "ctx"), None),
            P(("dp", "ctx"), None),
            P(("dp", "ctx"), None),
            P(("dp", "ctx"), "tensor"),
            P(("dp", "ctx"), "tensor"),
            P(("dp", "ctx"), "tensor"),
            P(("dp", "ctx"), None, "tensor"),
            P(("dp", "ctx"), None, "tensor"),
            P(("dp", "ctx"), None, "tensor"),
            P(("dp", "ctx"), "tensor"),
            P(("dp", "ctx"), "tensor"),
            P(("dp", "ctx"), "tensor"),
        ),
        check_vma=False,
    )
```

```python
import functools

import jax
import jax.numpy as jnp
import numpy as np
from jax import lax
from jax.experimental import pallas as pl
from jax.experimental.pallas import tpu as pltpu
from jax.sharding import PartitionSpec as P

D = 1152
HQ = 4
HD = 256
FF = 6912
WIN = 512
STEP = 10


norm_eps = 1e-06
beta_one = 0.9
beta_two = 0.95
adam_eps = 1e-08
decay_rate = 0.1
rope_base = 10000.0
GELU_SCALE = float(np.sqrt(2.0 / np.pi))
MESH = pl.DeviceIdType.MESH


def half_of(array, dim):
    size = array.shape[dim] // 2
    return lax.dynamic_slice_in_dim(array, lax.axis_index("tensor") * size, size, axis=dim)


def contract_rows(left_side, right_side):
    return lax.dot_general(
        left_side, right_side, (((0,), (0,)), ((), ())), preferred_element_type=jnp.float32
    )


def contract_columns(left_side, right_side):
    return lax.dot_general(
        left_side, right_side, (((1,), (1,)), ((), ())), preferred_element_type=jnp.float32
    )


def adam_step(weight_value, gradient, first_moment, second_moment, step_rate, decay_factor):
    first_moment = beta_one * first_moment + (1.0 - beta_one) * gradient
    second_moment = beta_two * second_moment + (1.0 - beta_two) * gradient * gradient
    first_hat = first_moment / (1.0 - beta_one**STEP)
    second_hat = second_moment / (1.0 - beta_two**STEP)
    update = first_hat / (jnp.sqrt(second_hat) + adam_eps)
    return (
        weight_value - step_rate * (update + decay_factor * weight_value),
        first_moment,
        second_moment,
    )


def places():
    return lax.axis_index("dp"), lax.axis_index("ctx"), lax.axis_index("tensor")


def plane_partners():
    dp, ctx, core = places()
    beside = ctx + 1 - 2 * lax.rem(ctx, 2)
    across = lax.rem(ctx + 2, 4)
    return (dp, beside, core), (dp, across, core), (dp, 3 - ctx, core), (dp, ctx, 1 - core)


def enter(n_dp, line):
    dp, ctx, core = places()
    barrier = pltpu.get_barrier_semaphore()

    def greet(device):
        pl.semaphore_signal(barrier, inc=1, device_id=device, device_id_type=MESH)

    for device in plane_partners():
        greet(device)
    if line:
        pl.when(dp < n_dp - 1)(lambda: greet((dp + 1, ctx, core)))
        pl.when(dp > 0)(lambda: greet((dp - 1, ctx, core)))
    ends = jnp.minimum(dp, 1) + jnp.minimum(n_dp - 1 - dp, 1) if line else 0
    pl.semaphore_wait(barrier, 4 + ends)


def in_columns(count, body):
    whole = count // 256

    def one(i, carry):
        body(pl.multiple_of(i * 256, 256), 256)
        return carry

    lax.fori_loop(0, whole, one, 0)
    if count % 256:
        body(whole * 256, count % 256)


def in_rows(count, body, start):
    size = 64

    def one(i, carry):
        return body(pl.multiple_of(i * size, size), size, carry)

    return lax.fori_loop(0, count // size, one, start)


def gather_copies(remote, buffer, base):
    x_dev, y_dev, _, core_dev = plane_partners()
    h = buffer.shape[2] // 2
    part_a, part_b = pl.ds(0, h), pl.ds(h, h)

    def piece(step, side):
        return buffer.at[step, 0, side]

    return [
        remote(piece(0, part_a), piece(1, part_a), base, x_dev),
        remote(piece(0, part_b), piece(1, part_b), base + 1, y_dev),
        remote(piece(0, part_b), piece(2, part_b), base + 2, x_dev),
        remote(piece(0, part_a), piece(2, part_a), base + 3, y_dev),
        remote(piece(1, part_a), piece(3, part_a), base + 4, y_dev),
        remote(piece(1, part_b), piece(3, part_b), base + 5, x_dev),
    ] + [
        remote(buffer.at[step, 0], buffer.at[step, 1], base + 6 + step, core_dev)
        for step in range(4)
    ]


def gather_step(copies, step):
    if step == 0:
        for copy in copies[:4]:
            copy.start()
    elif step == 1:
        copies[0].wait_recv()
        copies[1].wait_recv()
        copies[4].start()
        copies[5].start()
    else:
        copies[2 * step - 2].wait_recv()
        copies[2 * step - 1].wait_recv()
    copies[6 + step].start()
    copies[6 + step].wait_recv()


def turned(values, cosine, sine):
    half_dim = values.shape[-1] // 2
    lower, upper = values[:, :half_dim], values[:, half_dim:]
    return jnp.concatenate([lower * cosine - upper * sine, upper * cosine + lower * sine], axis=1)


def scale_of(values):
    return lax.rsqrt(jnp.mean(values * values, axis=1, keepdims=True) + norm_eps)


def attend_kernel(
    n_dp,
    owned_heads,
    tokens_in,
    lengths,
    inverse,
    attn_pack,
    mlp_pack,
    mlp_full,
    gain_rows,
    head_rows,
    log_total,
    cosine,
    sine,
    lowest,
    attn_full_out,
    normed_out_out,
    lin_out,
    query_out_out,
    keyval_out,
    attended_out,
    branch_out_out,
    middle_out_out,
    rows_out,
    slots,
    wide_slots,
    keyval,
    partial,
    core_send,
    core_take,
    own_sem,
    mlp_plane_send,
    mlp_plane_recv,
    mlp_line_send,
    mlp_line_recv,
    attn_line_send,
    attn_line_recv,
    attn_plane_send,
    attn_plane_recv,
    keyval_send,
    keyval_recv,
    rows,
    rows_send,
    rows_recv,
    rows_sem,
    attn_full,
    normed_out,
    lin,
    query_out,
    attended,
    branch_out,
    middle_out,
    out_sem,
    tokens,
):
    dp, ctx, core = places()
    x_dev, y_dev, far_dev, core_dev = plane_partners()
    plane = ((dp, ctx, core), x_dev, y_dev, far_dev)
    f32, bf16 = jnp.float32, jnp.bfloat16
    row_count, width = tokens.shape
    half = row_count // 2
    owned = attn_pack.shape[0]
    behind = keyval.shape[1] - row_count
    next_dev = (dp, ctx + 1, core)
    enter(n_dp, True)

    def remote(source, target, send, recv, device):
        return pltpu.make_async_remote_copy(
            src_ref=source, dst_ref=target, send_sem=send, recv_sem=recv, device_id=device,
            device_id_type=MESH,
        )

    def line_block(way, step, k):
        origin = dp - step if way == 0 else dp + step
        return origin * 4 + plane[k][1]

    def can_take(way, step):
        return dp >= step if way == 0 else dp <= n_dp - 1 - step

    def can_give(way):
        return dp < n_dp - 1 if way == 0 else dp > 0

    def line_dev(way):
        return (dp + 1, ctx, core) if way == 0 else (dp - 1, ctx, core)

    def mlp_hop(way, step, k):
        block = mlp_full.at[line_block(way, step, k)]
        index = (way * n_dp + step) * 4 + k
        return remote(block, block, mlp_line_send.at[index], mlp_line_recv.at[index], line_dev(way))

    def mlp_came(way, step, k):
        block = mlp_full.at[line_block(way, step, k)]
        index = (way * n_dp + step - 1) * 4 + k
        return remote(block, block, mlp_line_send.at[index], mlp_line_recv.at[index], line_dev(way))

    def attn_hop(way, step):
        block = slots.at[line_block(way, step, 0)]
        index = way * n_dp + step
        return remote(block, block, attn_line_send.at[index], attn_line_recv.at[index], line_dev(way))

    def attn_came(way, step):
        block = slots.at[line_block(way, step, 0)]
        index = way * n_dp + step - 1
        return remote(block, block, attn_line_send.at[index], attn_line_recv.at[index], line_dev(way))

    def each(step, act, give):
        for way in range(2):
            if give:
                fits = can_give(way) & can_take(way, step) if step else can_give(way)
            else:
                fits = can_take(way, step)
            pl.when(fits)(functools.partial(act, way))

    def attn_plane(way, step, side, came=False):
        from_k = {1: 0, 2: 0, 3: 1 if step % 2 == 0 else 2}[side]
        device = {1: x_dev, 2: y_dev, 3: y_dev if step % 2 == 0 else x_dev}[side]
        block = slots.at[line_block(way, step, side if came else from_k)]
        index = (way * n_dp + step) * 4 + side
        return remote(block, block, attn_plane_send.at[index], attn_plane_recv.at[index], device)

    pending = []

    def give(source, target):
        copy = pltpu.make_async_copy(source, target, out_sem.at[len(pending)])
        copy.start()
        pending.append(copy)

    def first_hop(way, source, blocks, send, recv):
        return remote(source, blocks.at[dp * 4 + ctx], send, recv, line_dev(way))

    def attn_first(way):
        index = way * n_dp
        return first_hop(
            way, attn_pack, slots, attn_line_send.at[index], attn_line_recv.at[index]
        )

    def mlp_own(way):
        index = way * n_dp * 4
        return first_hop(
            way, mlp_pack.at[ctx], mlp_full, mlp_line_send.at[index], mlp_line_recv.at[index]
        )

    def attn_near(side):
        return remote(
            attn_pack,
            slots.at[dp * 4 + ctx],
            attn_plane_send.at[side],
            attn_plane_recv.at[side],
            plane[side],
        )

    own_attn = pltpu.make_async_copy(attn_pack, slots.at[dp * 4 + ctx], own_sem.at[0])
    own_tokens = pltpu.make_async_copy(tokens_in, tokens, own_sem.at[2])
    own_mlp = pltpu.make_async_copy(mlp_pack.at[ctx], mlp_full.at[dp * 4 + ctx], own_sem.at[1])
    own_attn.start()
    own_mlp.start()
    each(0, lambda way: attn_first(way).start(), True)
    for side in (1, 2):
        attn_near(side).start()
    each(0, lambda way: mlp_own(way).start(), True)

    def mlp_plane(k, came=False):
        return remote(
            mlp_pack.at[plane[k][1]],
            mlp_full.at[dp * 4 + (plane[k][1] if came else ctx)],
            mlp_plane_send.at[k],
            mlp_plane_recv.at[k],
            plane[k],
        )

    for k in (1, 2):
        mlp_plane(k).start()

    own_tokens.start()

    def place_rows(first, size, carry):
        at = pl.ds(first, size)
        row = first + lax.broadcasted_iota(jnp.int32, (size, 1), 0)
        position = ctx * row_count + row
        stop, begin = 0, jnp.zeros((size, 1), jnp.int32)
        for index in range(lengths.shape[1]):
            stop = stop + lengths[0, index]
            begin = begin + jnp.where(position >= stop, lengths[0, index], 0)
        position = position - begin
        lowest[at] = jnp.maximum(row - position + behind, row + 1)
        angles = position.astype(f32) * inverse[...]
        cosine[at] = jnp.cos(angles)
        sine[at] = jnp.sin(angles)
        return carry

    in_rows(row_count, place_rows, 0)

    def came(way, step):
        attn_came(way, step).wait_recv()

    def hand_on(way, step):
        for side in (1, 2):
            attn_plane(way, step, side).start()

    order = [(0, 0)] + [(way, step) for step in range(1, n_dp) for way in range(2)]

    def relay(way, step):
        for side in (1, 2):
            attn_plane(way, step, side, True).wait_recv()
        attn_plane(way, step, 3).start()

    def relayed(way, step):
        attn_plane(way, step, 3, True).wait_recv()

    def where_held(way, step, act):
        if step:
            pl.when(can_take(way, step))(lambda: act(way, step))
        else:
            act(way, step)

    def mlp_first(k):
        mlp_plane(k, True).wait_recv()
        each(0, lambda way: mlp_hop(way, 0, k).start(), True)

    def mlp_next(step, k):
        each(step, lambda way: mlp_came(way, step, k).wait_recv(), False)
        if step < n_dp - 1:
            each(step, lambda way: mlp_hop(way, step, k).start(), True)

    events = [functools.partial(mlp_first, k) for k in (1, 2, 3)] + [
        functools.partial(mlp_next, step, k) for step in range(1, n_dp) for k in range(4)
    ]
    events.reverse()

    def move(count):
        for _ in range(min(count, len(events))):
            events.pop()()

    own_attn.wait()
    for step in range(1, n_dp):
        each(step, lambda way: came(way, step), False)
        each(step, lambda way: attn_hop(way, step).start(), True)
        each(step, lambda way: hand_on(way, step), False)
        if step == 1:
            mlp_plane(3).start()
        if step <= 3:
            move(1)
    if n_dp == 1:
        mlp_plane(3).start()
    move(max(0, 4 - n_dp) + 2)
    for way, step in order:
        where_held(way, step, relay)
    move(1)
    for way, step in order:
        where_held(way, step, relayed)
    move(1)

    for block in range(n_dp * 4):
        wide_slots[block * owned : (block + 1) * owned, :] = slots[block].astype(f32)

    def narrow(first, size, carry):
        at = pl.ds(first, size)
        attn_full[at] = wide_slots[at].astype(bf16)
        return carry

    in_rows(width, narrow, 0)
    give(attn_full, attn_full_out)
    pick = lax.broadcasted_iota(jnp.int32, (8, 128), 0) == lax.broadcasted_iota(
        jnp.int32, (8, 128), 1
    )
    small = contract_columns(pick.astype(f32).astype(bf16), attn_full[:, 1280:1408])
    gain_rows[...] = small
    row_of = lax.broadcasted_iota(jnp.int32, (width, HD), 0)
    head_of = lax.broadcasted_iota(jnp.int32, (width, HD), 1)
    shift = owned_heads.bit_length() - 1
    chosen = row_of == (head_of >> shift) * owned + (head_of & (owned_heads - 1))
    heads = jnp.dot(
        small.astype(bf16), chosen.astype(f32).astype(bf16), preferred_element_type=f32
    )
    head_rows[...] = heads

    def normalize(first, size, carry):
        at = pl.ds(first, size)
        values = tokens[at].astype(f32)
        normed_out[at] = (values * scale_of(values) * gain_rows[0:1]).astype(bf16)
        return carry

    own_tokens.wait()
    in_rows(row_count, normalize, 0)

    def project(start, size):
        lin[:, pl.ds(start, size)] = jnp.dot(
            normed_out[...], attn_full[:, pl.ds(start, size)], preferred_element_type=f32
        )

    in_columns(3 * HD, project)
    give(normed_out, normed_out_out)
    give(lin, lin_out)

    def turn_keyval(first, size, carry):
        at = pl.ds(first, size)
        values = lin[at, 2 * HD : 3 * HD]
        keys = turned(values * scale_of(values) * head_rows[5:6], cosine[at], sine[at])
        mine = jnp.where(core == 0, keys, values).astype(bf16)
        keyval[core, pl.ds(pl.multiple_of(first + behind, 64), size)] = mine
        return carry

    in_rows(row_count, turn_keyval, 0)
    own_rows, last_rows = pl.ds(behind, row_count), pl.ds(row_count, behind)
    past_rows = pl.ds(0, behind)

    def to_core(came=False):
        block = keyval.at[1 - core if came else core, own_rows]
        return remote(block, block, keyval_send.at[0], keyval_recv.at[0], core_dev)

    def past_to_core(came=False):
        block = keyval.at[1 - core if came else core, past_rows]
        return remote(block, block, keyval_send.at[2], keyval_recv.at[2], core_dev)

    to_next = remote(
        keyval.at[core, last_rows],
        keyval.at[core, past_rows],
        keyval_send.at[1],
        keyval_recv.at[1],
        next_dev,
    )
    pl.when(ctx < 3)(to_next.start)
    to_core().start()

    def turn_query(first, size, carry):
        at = pl.ds(first, size)
        for head in range(2):
            values = lin[at, head * HD : (head + 1) * HD]
            normal = values * scale_of(values) * head_rows[4:5]
            query_out[head, at] = turned(normal, cosine[at], sine[at]).astype(bf16)
        return carry

    in_rows(row_count, turn_query, 0)
    give(query_out, query_out_out)

    @pl.when(ctx > 0)
    def _():
        to_next.wait_recv()
        past_to_core().start()
        past_to_core(True).wait_recv()

    @pl.when(ctx == 0)
    def _():
        keyval[:, 0:behind] = jnp.zeros((2, behind, HD), bf16)

    to_core(True).wait_recv()

    block_rows = 256
    reach = block_rows + behind

    def attend(first, head):
        at = pl.ds(first, block_rows)
        near = pl.ds(first, reach)
        scores = contract_columns(query_out[head, at], keyval[0, near]) * HD ** (-0.5)
        key_at = first + lax.broadcasted_iota(jnp.int32, (block_rows, reach), 1)
        query_at = first + behind + lax.broadcasted_iota(jnp.int32, (block_rows, reach), 0)
        scores = jnp.where((key_at >= lowest[at]) & (key_at <= query_at), scores, -1e30)
        row_max = jnp.max(scores, axis=1, keepdims=True)
        values = jnp.exp(scores - row_max)
        row_total = jnp.sum(values, axis=1, keepdims=True)
        probs = (values / row_total).astype(bf16)
        log_total[head, at] = row_max + jnp.log(row_total)
        out = jnp.dot(probs, keyval[1, near], preferred_element_type=f32)
        attended[at, head * HD : (head + 1) * HD] = out.astype(bf16)

    for block in range(row_count // block_rows):
        for head in range(2):
            attend(block * block_rows, head)
    give(attended, attended_out)
    give(keyval, keyval_out)
    move(2)

    def outward(start, size):
        partial[:, pl.ds(start, size)] = contract_columns(
            attended[...], attn_full[pl.ds(start, size), 3 * HD : 5 * HD]
        )

    in_columns(width, outward)

    def give_half(first, size, carry):
        at = pl.ds(pl.multiple_of((1 - core) * half + first, 64), size)
        core_send[pl.ds(first, size)] = partial[at].astype(bf16)
        return carry

    in_rows(half, give_half, 0)
    exchange = remote(core_send, core_take, keyval_send.at[3], keyval_recv.at[3], core_dev)
    exchange.start()
    move(1)
    exchange.wait_recv()

    def finish(first, size, carry):
        at = pl.ds(first, size)
        whole_at = pl.ds(pl.multiple_of(core * half + first, 64), size)
        branch = partial[whole_at] + core_take[at].astype(f32)
        branch_out[at] = branch
        middle = tokens[whole_at].astype(f32) + branch * scale_of(branch) * gain_rows[1:2]
        middle_out[at] = middle
        rows[0, 0, at] = (middle * scale_of(middle) * gain_rows[2:3]).astype(bf16)
        return carry

    in_rows(half, finish, 0)

    give(branch_out, branch_out_out)
    give(middle_out, middle_out_out)

    def remote_rows(source, target, index, device):
        return remote(source, target, rows_send.at[index], rows_recv.at[index], device)

    gather = gather_copies(remote_rows, rows, 0)
    outs = [
        pltpu.make_async_copy(rows.at[step], rows_out.at[step], rows_sem.at[step])
        for step in range(4)
    ]
    for step in range(4):
        gather_step(gather, step)
        outs[step].start()
        if step == 0:
            move(1)
    move(len(events))
    for copy in gather:
        copy.wait_send()
    for copy in outs + pending + [own_mlp]:
        copy.wait()

    exchange.wait_send()
    to_core().wait_send()
    pl.when(ctx < 3)(to_next.wait_send)
    pl.when(ctx > 0)(past_to_core().wait_send)
    for k in (1, 2, 3):
        mlp_plane(k).wait_send()
    each(0, lambda way: attn_first(way).wait_send(), True)
    each(0, lambda way: mlp_own(way).wait_send(), True)
    for step in range(n_dp - 1):
        if step:
            each(step, lambda way: attn_hop(way, step).wait_send(), True)
        for k in range(4):
            if step or k:
                each(step, lambda way: mlp_hop(way, step, k).wait_send(), True)

    def left(way, step):
        for side in (1, 2, 3):
            if step or side == 3:
                attn_plane(way, step, side).wait_send()
            else:
                attn_near(side).wait_send()

    for way, step in order:
        where_held(way, step, left)


def attend_call(n_dp, owned_heads, behind, tokens, lengths, inverse, attn_pack, mlp_pack):
    row_count, width = tokens.shape
    half = row_count // 2
    owned, attn_cols = attn_pack.shape
    blocks = n_dp * 4
    f32, bf16 = jnp.float32, jnp.bfloat16
    vmem = pl.BlockSpec(memory_space=pltpu.VMEM)
    anywhere = pl.BlockSpec(memory_space=pl.ANY)

    def array(dtype, *shape):
        return jax.ShapeDtypeStruct(shape, dtype)

    dma = pltpu.SemaphoreType.DMA
    return pl.pallas_call(
        functools.partial(attend_kernel, n_dp, owned_heads),
        out_shape=(
            array(bf16, blocks, owned, mlp_pack.shape[2]),
            array(f32, 8, width),
            array(f32, 8, HD),
            array(f32, 2, row_count, 1),
            array(f32, row_count, HD // 2),
            array(f32, row_count, HD // 2),
            array(jnp.int32, row_count, 1),
            array(bf16, width, attn_cols),
            array(bf16, row_count, width),
            array(f32, row_count, 3 * HD),
            array(bf16, 2, row_count, HD),
            array(bf16, 2, behind + row_count, HD),
            array(bf16, row_count, 2 * HD),
            array(f32, half, width),
            array(f32, half, width),
            array(bf16, 4, 2, half, width),
        ),
        in_specs=[
            anywhere,
            pl.BlockSpec(memory_space=pltpu.SMEM),
            vmem,
            anywhere,
            anywhere,
        ],
        out_specs=(anywhere,) + (vmem,) * 6 + (anywhere,) * 9,
        scratch_shapes=[
            pltpu.VMEM((blocks, owned, attn_cols), bf16),
            pltpu.VMEM((width, attn_cols), f32),
            pltpu.VMEM((2, behind + row_count, HD), bf16),
            pltpu.VMEM((row_count, width), f32),
            pltpu.VMEM((half, width), bf16),
            pltpu.VMEM((half, width), bf16),
            dma((3,)),
            dma((4,)),
            dma((4,)),
            dma((8 * n_dp,)),
            dma((8 * n_dp,)),
            dma((2 * n_dp,)),
            dma((2 * n_dp,)),
            dma((8 * n_dp,)),
            dma((8 * n_dp,)),
            dma((4,)),
            dma((4,)),
            pltpu.VMEM((4, 2, half, width), bf16),
            dma((10,)),
            dma((10,)),
            dma((4,)),
            pltpu.VMEM((width, attn_cols), bf16),
            pltpu.VMEM((row_count, width), bf16),
            pltpu.VMEM((row_count, 3 * HD), f32),
            pltpu.VMEM((2, row_count, HD), bf16),
            pltpu.VMEM((row_count, 2 * HD), bf16),
            pltpu.VMEM((half, width), f32),
            pltpu.VMEM((half, width), f32),
            dma((8,)),
            pltpu.VMEM((row_count, width), bf16),
        ],
        compiler_params=pltpu.CompilerParams(
            collective_id=1, has_side_effects=True, vmem_limit_bytes=60 * 2**20
        ),
        cost_estimate=pl.CostEstimate(
            flops=4 * 10**9, bytes_accessed=30 * 2**20, transcendentals=2 * 10**6
        ),
        name="attend",
    )(tokens, lengths, inverse, attn_pack, mlp_pack)


def mlp_kernel(
    n_dp,
    line,
    rows_in,
    middle_in,
    cotangent_in,
    gain_rows,
    weights_in,
    result_out,
    back_sum,
    gain_sum,
    weights_out,
    early,
    result,
    rows,
    grads,
    hidden,
    pair,
    weights,
    total,
    waiting,
    core_send,
    core_take,
    plane_send,
    plane_take,
    send_sem,
    recv_sem,
    load_sem,
    out_sem,
    middle,
    cotangent,
):
    half, width = middle.shape
    h = half // 2
    hid = hidden.shape[2]
    step_rows = 2 * half
    part_a, part_b = pl.ds(0, h), pl.ds(h, h)
    x_dev, y_dev, _, core_dev = plane_partners()
    core = lax.axis_index("tensor")
    gain = gain_rows.at[pl.ds(3, 1)]
    f32, bf16 = jnp.float32, jnp.bfloat16

    loads = [pltpu.make_async_copy(weights_in, weights, load_sem.at[4])] + [
        pltpu.make_async_copy(rows_in.at[step], rows.at[step], load_sem.at[step])
        for step in range(4)
    ]
    norm_loads = [
        pltpu.make_async_copy(middle_in, middle, load_sem.at[5]),
        pltpu.make_async_copy(cotangent_in, cotangent, load_sem.at[6]),
    ]
    for load in [loads[0], loads[4], loads[3], loads[2], loads[1]] + norm_loads:
        load.start()
    enter(n_dp, line > 1)

    def remote(source, target, index, device):
        return pltpu.make_async_remote_copy(
            src_ref=source,
            dst_ref=target,
            send_sem=send_sem.at[index],
            recv_sem=recv_sem.at[index],
            device_id=device,
            device_id_type=MESH,
        )

    def scatter_copies(base):
        return [
            remote(plane_send.at[0, part_a], plane_take.at[0, part_a], base, y_dev),
            remote(plane_send.at[0, part_b], plane_take.at[0, part_b], base + 1, x_dev),
            remote(plane_send.at[1, part_a], plane_take.at[1, part_a], base + 2, y_dev),
            remote(plane_send.at[1, part_b], plane_take.at[1, part_b], base + 3, x_dev),
            remote(plane_send.at[2, part_a], plane_take.at[2, part_a], base + 4, x_dev),
            remote(plane_send.at[2, part_b], plane_take.at[2, part_b], base + 5, y_dev),
        ] + [
            remote(core_send.at[step % 2], core_take.at[step], base + 6 + step, core_dev)
            for step in range(4)
        ]

    def scatter_step(copies, step, before, left, first):
        kept = (total, waiting, back_sum, back_sum)[step]
        slot = core_send.at[step % 2]
        if before is not None:
            copies[6 + before].wait_send()

        def part(rows, start, size):
            right = weights[pl.ds(start, size), first : first + left.shape[2]]
            return contract_columns(left[step, rows], right)

        def give(start, size):
            slot[:, pl.ds(start, size)] = part(pl.ds(half, half), start, size).astype(bf16)

        def keep(start, size):
            kept[:, pl.ds(start, size)] = part(pl.ds(0, half), start, size)

        in_columns(width, give)
        copies[6 + step].start()
        in_columns(width, keep)

    def scatter_rest(copies, step):
        kept = (total, waiting, back_sum, back_sum)[step]
        copies[6 + step].wait_recv()
        summed = kept[...] + core_take[step].astype(f32)
        if step < 2:
            kept[...] = summed
        else:
            plane_send[step - 2] = summed.astype(bf16)
            copies[2 * step - 4].start()
            copies[2 * step - 3].start()

    def scatter_end(copies):
        copies[2].wait_recv()
        copies[3].wait_recv()
        plane_send[2] = (waiting[...] + plane_take[1].astype(f32)).astype(bf16)
        copies[4].start()
        copies[5].start()

    def scatter_total(at):
        return total[at] + plane_take[0, at].astype(f32) + plane_take[2, at].astype(f32)

    def scatter_wait(copies):
        for index in (0, 1, 4, 5):
            copies[index].wait_recv()

    def sent(copies):
        for copy in copies:
            copy.wait_send()

    scatter = scatter_copies(0)
    loads[0].wait()
    for step in (3, 2, 1, 0):
        loads[1 + step].wait()

        def activate(start, size):
            def lin(first):
                return jnp.dot(
                    rows[step].reshape(step_rows, width),
                    weights[:, pl.ds(pl.multiple_of(first + start, 128), size)],
                    preferred_element_type=f32,
                )

            gate, up = lin(0), lin(hid)
            square = gate * gate
            chance = 0.5 + 0.5 * jnp.tanh(gate * (GELU_SCALE + GELU_SCALE * 0.044715 * square))
            gelu = gate * chance
            slope = chance + gelu * (1.0 - chance) * (
                2 * GELU_SCALE + 6 * GELU_SCALE * 0.044715 * square
            )
            hidden[step, :, pl.ds(start, size)] = (gelu * up).astype(bf16)
            pair[step, :, pl.ds(start, size)] = (slope * up).astype(bf16)
            pair[step, :, pl.ds(pl.multiple_of(hid + start, 128), size)] = gelu.astype(bf16)

        in_columns(hid, activate)
        scatter_step(scatter, step, step + 2 if step < 2 else None, hidden, 2 * hid)
        scatter_rest(scatter, step)
        if step == 1:
            scatter_end(scatter)
    scatter_wait(scatter)
    sent(scatter[:8])
    for load in norm_loads:
        load.wait()

    def norm_rows(first, size, gain_total):
        at = pl.ds(first, size)
        raw = scatter_total(at)
        scale = lax.rsqrt(jnp.mean(raw * raw, axis=1, keepdims=True) + norm_eps)
        normal = raw * scale
        result[at] = (middle[at] + normal * gain[...]).astype(bf16)
        cotangents = cotangent[pl.ds(pl.multiple_of(core * half + first, 64), size)].astype(f32)
        scaled = cotangents * gain[...]
        inner = jnp.mean(raw * scaled, axis=1, keepdims=True)
        back = scale * scaled - raw * (scale * scale * scale * inner)
        grads[0, 0, at] = back.astype(bf16)
        return gain_total + jnp.sum(cotangents * normal, axis=0, keepdims=True)

    gain_sum[...] = in_rows(half, norm_rows, jnp.zeros((1, width), f32))

    def result_rows(place):
        return result_out.at[pl.ds(pl.multiple_of(place * half, 64), half)]

    own_result = pltpu.make_async_copy(result, result_rows(core), out_sem.at[2])
    far_result = remote(result, result_rows(core), 30, core_dev)
    own_result.start()
    far_result.start()

    gather = gather_copies(remote, grads, 10)
    scatter = scatter_copies(20)
    for step in range(4):
        gather_step(gather, step)

        def unfold(start, size):
            hidden_grad = jnp.dot(
                grads[step].reshape(step_rows, width),
                weights[:, pl.ds(pl.multiple_of(2 * hid + start, 128), size)],
                preferred_element_type=f32,
            )
            hidden_grad = hidden_grad.astype(bf16)
            for first in (0, hid):
                at = pl.ds(pl.multiple_of(first + start, 128), size)
                pair[step, :, at] = pair[step, :, at] * hidden_grad

        in_columns(hid, unfold)
        if step:
            scatter_rest(scatter, step - 1)
        scatter_step(scatter, step, step - 2 if step >= 2 else None, pair, 0)
    scatter_rest(scatter, 3)
    sent(gather)

    dp, ctx, _ = places()
    last_dp = line - 1
    group = width // line
    chunk_rows = 384
    chunks = width // chunk_rows

    def weigh(first, left, right, i):
        chunk = jnp.where(2 * dp < n_dp, chunks - 1 - i, i)
        at = pl.ds(pl.multiple_of(chunk * chunk_rows, 128), chunk_rows)
        product = contract_rows(
            left[:, :, :, at].reshape(8 * half, chunk_rows),
            right[...].reshape(8 * half, right.shape[2]),
        )
        weights[at, first : first + right.shape[2]] = product.astype(bf16)

    def leave(first, count, index):
        columns = pl.ds(first, count)
        copy = pltpu.make_async_copy(
            weights.at[:, columns], weights_out.at[:, columns], out_sem.at[index]
        )
        copy.start()
        return copy

    def early_copy(way, index):
        place = last_dp - index if way == 0 else index
        first = pl.multiple_of(place * group, 8)
        device = (dp + 1, ctx, core) if way == 0 else (dp - 1, ctx, core)
        source = weights.at[pl.ds(first, group), pl.ds(2 * hid, hid)]
        item = 2 * index + way
        return remote(source, early.at[item], 31 + item, device)

    def sends_early(way):
        return dp == 0 if way == 0 else dp == last_dp

    for i in range(chunks):
        weigh(2 * hid, grads, hidden, i)
        for way, index in early_items(line):
            if i * chunk_rows < (index + 1) * group <= (i + 1) * chunk_rows:
                pl.when(sends_early(way))(early_copy(way, index).start)
    down_out = leave(2 * hid, hid, 1)
    weigh(0, rows, pair, 0)
    scatter_end(scatter)
    for i in range(1, chunks):
        weigh(0, rows, pair, i)
    gate_out = leave(0, 2 * hid, 0)
    scatter_wait(scatter)

    def finish_rows(first, size, carry):
        at = pl.ds(first, size)
        back_sum[at] = scatter_total(at)
        return carry

    in_rows(half, finish_rows, 0)
    sent(scatter[:6] + scatter[8:])
    if line > 1:
        for way, index in early_items(line):
            pl.when(sends_early(way))(early_copy(way, index).wait_send)
            pl.when(takes_early(way, dp, last_dp))(early_copy(way, index).wait_recv)
    down_out.wait()
    gate_out.wait()
    own_result.wait()
    far_result.wait_send()
    remote(result, result_rows(1 - core), 30, core_dev).wait_recv()


def early_items(line):
    return [(way, index) for index in range(min(2, line - 1)) for way in range(2)]


def takes_early(way, dp, last_dp):
    return dp == 1 if way == 0 else dp == last_dp - 1


def mlp_call(n_dp, line, rows, middle, cotangent, gain_rows, weights):
    half, width = middle.shape
    hid = weights.shape[1] // 3
    count = 8 * half
    f32, bf16 = jnp.float32, jnp.bfloat16
    vmem = pl.BlockSpec(memory_space=pltpu.VMEM)
    anywhere = pl.BlockSpec(memory_space=pl.ANY)
    return pl.pallas_call(
        functools.partial(mlp_kernel, n_dp, line),
        out_shape=(
            jax.ShapeDtypeStruct(cotangent.shape, bf16),
            jax.ShapeDtypeStruct((half, width), f32),
            jax.ShapeDtypeStruct((1, width), f32),
            jax.ShapeDtypeStruct((width, 3 * hid), bf16),
            jax.ShapeDtypeStruct((max(2, len(early_items(line))), width // line, hid), bf16),
        ),
        in_specs=[anywhere, anywhere, anywhere, vmem, anywhere],
        out_specs=(anywhere, vmem, vmem, anywhere, anywhere),
        scratch_shapes=[
            pltpu.VMEM((half, width), bf16),
            pltpu.VMEM((4, 2, half, width), bf16),
            pltpu.VMEM((4, 2, half, width), bf16),
            pltpu.VMEM((4, 2 * half, hid), bf16),
            pltpu.VMEM((4, 2 * half, 2 * hid), bf16),
            pltpu.VMEM((width, 3 * hid), bf16),
            pltpu.VMEM((half, width), f32),
            pltpu.VMEM((half, width), f32),
            pltpu.VMEM((2, half, width), bf16),
            pltpu.VMEM((4, half, width), bf16),
            pltpu.VMEM((3, half, width), bf16),
            pltpu.VMEM((3, half, width), bf16),
            pltpu.SemaphoreType.DMA((35,)),
            pltpu.SemaphoreType.DMA((35,)),
            pltpu.SemaphoreType.DMA((7,)),
            pltpu.SemaphoreType.DMA((3,)),
            pltpu.VMEM((half, width), f32),
            pltpu.VMEM(cotangent.shape, bf16),
        ],
        compiler_params=pltpu.CompilerParams(
            collective_id=0, has_side_effects=True, vmem_limit_bytes=63 * 2**20
        ),
        cost_estimate=pl.CostEstimate(
            flops=2 * count * width * hid * 9, bytes_accessed=30 * 2**20, transcendentals=count * hid
        ),
        name="feed_forward",
    )(rows, middle, cotangent, gain_rows, weights)


def norm_back(values, gains, grads):
    scale = scale_of(values)
    normal = values * scale
    scaled = grads * gains
    inner = jnp.mean(values * scaled, axis=1, keepdims=True)
    return scale * scaled - values * (scale * scale * scale * inner), grads * normal


def retreat_kernel(
    n_dp,
    line,
    owned_heads,
    back_sum,
    middle,
    branch,
    cotangent_in,
    tokens_in,
    cosine,
    sine,
    lowest,
    gain_rows,
    head_rows,
    gain_three,
    attn_full_in,
    normed_one_in,
    lin_in,
    query_in,
    keyval_in,
    attended_in,
    log_total,
    mlp_grads,
    early,
    input_whole,
    gate_reduced,
    down_reduced,
    attn_reduced,
    keyval_reduced,
    input_out,
    line_slots,
    attn_grads,
    attn_blocks,
    attn_plane_take,
    attn_sums,
    attn_slots,
    branch_low,
    attended_grad,
    query_grad,
    lin_grad,
    keyval_grad,
    keyval_send,
    keyval_take,
    past_take,
    partial,
    core_send,
    core_take,
    small_rows,
    small_take,
    line_send_sem,
    line_recv_sem,
    plane_send_sem,
    plane_recv_sem,
    attn_plane_send_sem,
    attn_plane_recv_sem,
    attn_line_send_sem,
    attn_line_recv_sem,
    core_send_sem,
    core_recv_sem,
    load_sem,
    early_sem,
    mlp_own,
    cotangent,
    tokens,
    attn_full,
    normed_one,
    lin,
    query,
    keyval,
    attended,
):
    dp, ctx, core = places()
    x_dev, y_dev, far_dev, core_dev = plane_partners()
    plane = ((dp, ctx, core), x_dev, y_dev, far_dev)
    f32, bf16 = jnp.float32, jnp.bfloat16
    row_count, width = tokens.shape
    half = row_count // 2
    owned, hid = mlp_grads.shape[1], mlp_grads.shape[2] // 3
    behind = keyval.shape[1] - row_count
    last_dp = line - 1
    here_dp = dp if line > 1 else 0
    early_count = len(early_items(line)) // 2
    sources = (
        (cotangent_in, cotangent),
        (attn_full_in, attn_full),
        (query_in, query),
        (keyval_in, keyval),
        (mlp_grads, mlp_own),
        (lin_in, lin),
        (attended_in, attended),
        (normed_one_in, normed_one),
        (tokens_in, tokens),
    )
    held = [
        pltpu.make_async_copy(source, target, load_sem.at[3 + index])
        for index, (source, target) in enumerate(sources)
    ]
    loads = [
        pltpu.make_async_copy(
            source,
            attn_grads.at[pl.ds(index * half, half), pl.ds(0, width)],
            load_sem.at[index],
        )
        for index, source in enumerate((middle, branch, back_sum))
    ]
    for load in loads + held:
        load.start()
    enter(n_dp, line > 1)

    def remote(source, target, send, recv, device):
        return pltpu.make_async_remote_copy(
            src_ref=source,
            dst_ref=target,
            send_sem=send,
            recv_sem=recv,
            device_id=device,
            device_id_type=MESH,
        )

    def goal(way, far):
        return dp + far if way == 0 else dp - far

    def has_goal(way, far):
        return dp + far <= last_dp if way == 0 else dp >= far

    def is_first(way):
        return dp == 0 if way == 0 else dp == last_dp

    def not_first(way):
        return dp > 0 if way == 0 else dp < last_dp

    def line_dev(way):
        return (dp + 1, ctx, core) if way == 0 else (dp - 1, ctx, core)

    def slot_of(way, far, k):
        return (way * last_dp + far - 1) * 4 + k

    def own_mlp(place, k):
        return mlp_own[place * 4 + plane[k][1]].astype(f32)

    def first_hop(way, far, k):
        slot = slot_of(way, far, k)
        columns = pl.ds(0, 2 * hid if last_dp - far < early_count else 3 * hid)
        return remote(
            mlp_grads.at[goal(way, far) * 4 + plane[k][1], :, columns],
            line_slots.at[slot, :, columns],
            line_send_sem.at[slot],
            line_recv_sem.at[slot],
            line_dev(way),
        )

    def next_hop(way, far, k):
        slot = slot_of(way, far, k)
        return remote(
            line_slots.at[slot_of(way, far + 1, k)],
            line_slots.at[slot],
            line_send_sem.at[slot],
            line_recv_sem.at[slot],
            line_dev(way),
        )

    def came(way, far, k):
        slot = slot_of(way, far, k)

        def wait(count):
            block = line_slots.at[slot, :, pl.ds(0, count)]
            remote(
                block, block, line_send_sem.at[slot], line_recv_sem.at[slot], line_dev(way)
            ).wait_recv()

        def wait_both():
            wait(2 * hid)
            early_load(way, last_dp - far, k).wait()

        if far == last_dp:
            wait_both()
        elif last_dp - far < early_count:
            beside_first = takes_early(way, dp, last_dp)
            pl.when(beside_first)(wait_both)
            pl.when(jnp.logical_not(beside_first))(functools.partial(wait, 3 * hid))
        else:
            wait(3 * hid)

    def early_load(way, index, k):
        return pltpu.make_async_copy(
            early.at[2 * index + way, plane[k][1]],
            line_slots.at[slot_of(way, last_dp - index, k), :, pl.ds(2 * hid, hid)],
            early_sem.at[(2 * index + way) * 4 + k],
        )

    def load_early(way):
        for index in range(early_count):
            for k in range(4):
                early_load(way, index, k).start()

    if line > 1:
        for way in range(2):
            pl.when(takes_early(way, dp, last_dp))(functools.partial(load_early, way))

    turn = (3, 1, 2, 0)

    def start_first(blocks):
        def start(way):
            for far, k in blocks:
                first_hop(way, far, k).start()

        for way in range(2):
            if line > 1:
                pl.when(is_first(way))(functools.partial(start, way))

    start_first([(far, k) for far in range(last_dp, 1, -1) for k in turn])

    def pass_on(way, far, k):
        came(way, far + 1, k)
        slot = slot_of(way, far + 1, k)
        line_slots[slot] = (line_slots[slot].astype(f32) + own_mlp(goal(way, far), k)).astype(bf16)
        next_hop(way, far, k).start()

    def mlp_step(far, k):
        for way in range(2):
            pl.when(not_first(way) & has_goal(way, far))(functools.partial(pass_on, way, far, k))

    parts = ((gate_reduced, pl.ds(0, 2 * hid)), (down_reduced, pl.ds(2 * hid, hid)))

    def to_owner(k, came=False):
        place = plane[k][1] if came else ctx
        return [
            remote(
                line_slots.at[k, :, columns],
                target.at[place],
                plane_send_sem.at[2 * k + index],
                plane_recv_sem.at[2 * k + index],
                plane[k],
            )
            for index, (target, columns) in enumerate(parts)
        ]

    own_done = [
        pltpu.make_async_copy(line_slots.at[0, :, columns], target.at[ctx], plane_send_sem.at[index])
        for index, (target, columns) in enumerate(parts)
    ]

    def mlp_last(k):
        if line > 1:
            for way in range(2):
                pl.when(not_first(way))(functools.partial(came, way, 1, k))
        total = own_mlp(here_dp, k)
        for way in range(2):
            if line > 1:
                arrived = line_slots[slot_of(way, 1, k)].astype(f32)
                total = total + jnp.where(not_first(way), arrived, 0.0)
        line_slots[k] = total.astype(bf16)
        for copy in to_owner(k) if k else own_done:
            copy.start()

    events = [
        functools.partial(mlp_step, far, k) for far in range(line - 2, 0, -1) for k in turn
    ] + [functools.partial(mlp_last, k) for k in turn]
    events.reverse()

    def move(count):
        for _ in range(min(count, len(events))):
            events.pop()()

    for load in loads + held[:1]:
        load.wait()

    def loaded(index, first, size):
        return attn_grads[pl.ds(pl.multiple_of(first + index * half, 64), size), 0:width]

    def norms(first, size, carry):
        at = pl.ds(first, size)
        part, gain_two = norm_back(loaded(0, first, size), gain_rows[2:3], loaded(2, first, size))
        whole_at = pl.ds(pl.multiple_of(core * half + first, 64), size)
        middle_grad = cotangent[whole_at].astype(f32) + part
        input_out[at] = middle_grad
        grad, gain_one = norm_back(loaded(1, first, size), gain_rows[1:2], middle_grad)
        branch_low[whole_at] = grad.astype(bf16)
        return (
            carry[0] + jnp.sum(gain_one, axis=0, keepdims=True),
            carry[1] + jnp.sum(gain_two, axis=0, keepdims=True),
        )

    nothing = jnp.zeros((1, width), f32)
    small_rows[...] = jnp.zeros_like(small_rows)
    gain_one, gain_two = in_rows(half, norms, (nothing, nothing))
    small_rows[1:2] = gain_one
    small_rows[2:3] = gain_two
    small_rows[3:4] = gain_three[...]

    def halves(came):
        rows = pl.ds(pl.multiple_of((1 - core if came else core) * half, 64), half)
        return remote(
            branch_low.at[rows], branch_low.at[rows], core_send_sem.at[0], core_recv_sem.at[0], core_dev
        )

    halves(False).start()
    halves(True).wait_recv()
    held[4].wait()
    move(1)

    def inward(start, size):
        grad = jnp.dot(
            branch_low[...],
            attn_full[:, pl.ds(pl.multiple_of(3 * HD + start, 128), size)],
            preferred_element_type=f32,
        )
        attended_grad[:, pl.ds(start, size)] = grad.astype(bf16)

    held[1].wait()
    in_columns(2 * HD, inward)
    move(1)

    block_rows = 256
    reach = block_rows + behind
    keyval_grad[...] = jnp.zeros_like(keyval_grad)
    for load in held[2:4]:
        load.wait()

    def retreat(first, head):
        at = pl.ds(first, block_rows)
        near = pl.ds(first, reach)
        columns = slice(head * HD, (head + 1) * HD)
        scores = contract_columns(query[head, at], keyval[0, near]) * HD ** (-0.5)
        key_at = first + lax.broadcasted_iota(jnp.int32, (block_rows, reach), 1)
        query_at = first + behind + lax.broadcasted_iota(jnp.int32, (block_rows, reach), 0)
        scores = jnp.where((key_at >= lowest[at]) & (key_at <= query_at), scores, -1e30)
        probs = jnp.exp(scores - log_total[head, at])
        grads = attended_grad[at, columns]
        probs_grad = contract_columns(grads, keyval[1, near])
        delta = jnp.sum(probs * probs_grad, axis=1, keepdims=True)
        score_grad = (probs * (probs_grad - delta)).astype(bf16)
        query_grad[at, columns] = (
            jnp.dot(score_grad, keyval[0, near], preferred_element_type=f32) * HD ** (-0.5)
        )
        keyval_grad[0, near] += contract_rows(score_grad, query[head, at]) * HD ** (-0.5)
        keyval_grad[1, near] += contract_rows(probs.astype(bf16), grads)

    for block in range(row_count // block_rows):
        for head in range(2):
            retreat(block * block_rows, head)
    move(2)

    keyval_send[0] = keyval_grad[1 - core].astype(bf16)
    to_core = remote(
        keyval_send.at[0], keyval_take, core_send_sem.at[1], core_recv_sem.at[1], core_dev
    )
    to_core.start()

    def query_rows(first, size, carry):
        at = pl.ds(first, size)
        total = carry
        for head in range(2):
            columns = slice(head * HD, (head + 1) * HD)
            grads = turned(query_grad[at, columns], cosine[at], -sine[at])
            grad, gain = norm_back(lin[at, columns], head_rows[4:5], grads)
            lin_grad[at, columns] = grad.astype(bf16)
            total = total + jnp.sum(gain, axis=0, keepdims=True)
        return total

    for load in held[5:]:
        load.wait()
    head_zero = in_rows(row_count, query_rows, jnp.zeros((1, HD), f32))
    move(1)
    to_core.wait_recv()
    keyval_grad[core] = keyval_grad[core] + keyval_take[...].astype(f32)
    keyval_send[1, 0:behind] = keyval_grad[core, 0:behind].astype(bf16)
    to_past = remote(
        keyval_send.at[1, pl.ds(0, behind)],
        past_take,
        core_send_sem.at[2],
        core_recv_sem.at[2],
        (dp, ctx - 1, core),
    )
    pl.when(ctx > 0)(to_past.start)

    def outward(start, size):
        attn_grads[0:width, pl.ds(pl.multiple_of(3 * HD + start, 128), size)] = contract_rows(
            branch_low[...], attended[:, pl.ds(start, size)]
        )

    in_columns(2 * HD, outward)

    @pl.when(ctx < 3)
    def _():
        to_past.wait_recv()
        late = pl.ds(row_count, behind)
        keyval_grad[core, late] = keyval_grad[core, late] + past_take[...].astype(f32)

    def keyval_rows(first, size, carry):
        at = pl.ds(first, size)
        values = keyval_grad[core, pl.ds(pl.multiple_of(first + behind, 64), size)]
        grads = turned(values, cosine[at], -sine[at])
        grad, gain = norm_back(lin[at, 2 * HD : 3 * HD], head_rows[5:6], grads)
        lin_grad[at, 2 * HD : 3 * HD] = jnp.where(core == 0, grad, values).astype(bf16)
        return carry + jnp.sum(gain, axis=0, keepdims=True)

    head_one = in_rows(row_count, keyval_rows, jnp.zeros((1, HD), f32))
    head_one = jnp.where(core == 0, head_one, 0.0)

    def weigh(start, size):
        attn_grads[0:width, pl.ds(start, size)] = contract_rows(
            normed_one[...], lin_grad[:, pl.ds(start, size)]
        )

    in_columns(3 * HD, weigh)

    attn_parts = ((0, 5 * HD), (5 * HD, 128))

    def attn_plane(k, place, part):
        index = (k - 1) * n_dp + place
        columns = pl.ds(*attn_parts[part])
        return remote(
            attn_blocks.at[place * 4 + plane[k][1], :, columns],
            attn_plane_take.at[index, :, columns],
            attn_plane_send_sem.at[2 * index + part],
            attn_plane_recv_sem.at[2 * index + part],
            plane[k],
        )

    def place_at(i):
        return jnp.where(2 * dp < n_dp, n_dp - 1 - i, i)

    def give_attn(part):
        first, count = attn_parts[part]
        for block in range(n_dp * 4):
            attn_blocks[block, :, first : first + count] = attn_grads[
                block * owned : (block + 1) * owned, first : first + count
            ].astype(bf16)
        for i in range(n_dp):
            for k in (3, 1, 2):
                attn_plane(k, place_at(i), part).start()

    give_attn(0)
    move(1)
    start_first([(1, k) for k in turn[:2]])

    def back(start, size):
        columns = pl.ds(start, size)
        product = contract_columns(lin_grad[...], attn_full[columns, 0 : 3 * HD])
        first, second = product[:half], product[half:]
        partial[:, columns] = jnp.where(core == 0, first, second)
        core_send[:, columns] = jnp.where(core == 0, second, first).astype(bf16)

    in_columns(width, back)
    exchange = remote(core_send, core_take, core_send_sem.at[3], core_recv_sem.at[3], core_dev)
    exchange.start()
    exchange.wait_recv()

    def finish(first, size, carry):
        at = pl.ds(first, size)
        whole_at = pl.ds(pl.multiple_of(core * half + first, 64), size)
        grads = partial[at] + core_take[at].astype(f32)
        part, gain = norm_back(tokens[whole_at].astype(f32), gain_rows[0:1], grads)
        input_out[at] = input_out[at] + part
        return carry + jnp.sum(gain, axis=0, keepdims=True)

    small_rows[0:1] = in_rows(half, finish, nothing)

    def input_rows(place):
        return input_whole.at[pl.ds(pl.multiple_of(place * half, 64), half)]

    own_input = pltpu.make_async_copy(input_out, input_rows(core), load_sem.at[0])
    own_input.start()

    def far_input(place):
        return remote(
            input_out, input_rows(place), core_send_sem.at[5], core_recv_sem.at[5], core_dev
        )

    far_input(core).start()

    row_of = lax.broadcasted_iota(jnp.int32, (width, HD), 0)
    head_of = lax.broadcasted_iota(jnp.int32, (width, HD), 1)
    shift = owned_heads.bit_length() - 1
    chosen = row_of == (head_of >> shift) * owned + (head_of & (owned_heads - 1))
    heads = jnp.concatenate([head_zero, head_one, jnp.zeros((6, HD), f32)], axis=0)
    spread = contract_columns(heads.astype(bf16), chosen.astype(f32).astype(bf16))
    small_rows[4:6] = spread[0:2]
    smalls = remote(
        small_rows.at[pl.ds(0, 8)], small_take, core_send_sem.at[4], core_recv_sem.at[4], core_dev
    )
    smalls.start()
    smalls.wait_recv()
    smalls.wait_send()
    small_rows[0:8] = small_rows[0:8] + small_take[...]
    attn_grads[0:width, 5 * HD : 5 * HD + 128] = small_rows[...].T

    give_attn(1)
    move(len(events) - 4)
    def attn_hop(way, far, first):
        source = attn_sums.at[goal(way, far)] if first else attn_slots.at[way * line + far + 1]
        index = way * line + far
        return remote(
            source,
            attn_slots.at[index],
            attn_line_send_sem.at[index],
            attn_line_recv_sem.at[index],
            line_dev(way),
        )

    def attn_came(way, far):
        index = way * line + far
        block = attn_slots.at[index]
        remote(
            block, block, attn_line_send_sem.at[index], attn_line_recv_sem.at[index], line_dev(way)
        ).wait_recv()

    def attn_leave(way, far):
        attn_hop(way, far, True).start()

    for i in range(n_dp):
        place = place_at(i)
        total = attn_blocks[place * 4 + ctx].astype(f32)
        for k in (1, 2, 3):
            attn_plane(k, place, 0).wait_recv()
            attn_plane(k, place, 1).wait_recv()
            total = total + attn_plane_take[(k - 1) * n_dp + place].astype(f32)
        attn_sums[place] = total.astype(bf16)
        if i < last_dp:
            for way in range(2):
                pl.when(is_first(way))(functools.partial(attn_leave, way, last_dp - i))
        if i < 2:
            start_first([(1, turn[2 + i])])

    def attn_pass(way, far):
        attn_came(way, far + 1)
        index = way * line + far + 1
        total = attn_slots[index].astype(f32) + attn_sums[goal(way, far)].astype(f32)
        attn_slots[index] = total.astype(bf16)
        attn_hop(way, far, False).start()

    for far in range(line - 2, 0, -1):
        for way in range(2):
            pl.when(not_first(way) & has_goal(way, far))(functools.partial(attn_pass, way, far))
        move(2)
    move(len(events))
    if line == 1:
        attn_reduced[...] = attn_sums[...]
    else:
        total = attn_sums[dp].astype(f32)
        for way in range(2):
            pl.when(not_first(way))(functools.partial(attn_came, way, 1))
            arrived = attn_slots[way * line + 1].astype(f32)
            total = total + jnp.where(not_first(way), arrived, 0.0)
        attn_reduced[0] = total.astype(bf16)
        columns = attn_reduced.at[0, :, pl.ds(2 * HD, HD)]
        own_keyval = pltpu.make_async_copy(columns, keyval_reduced.at[core], load_sem.at[1])
        own_keyval.start()

        def far_keyval(place):
            return remote(
                columns, keyval_reduced.at[place], core_send_sem.at[6], core_recv_sem.at[6], core_dev
            )

        far_keyval(core).start()
        far_keyval(core).wait_send()
        far_keyval(1 - core).wait_recv()
        own_keyval.wait()

    for k in (1, 2, 3):
        for copy in to_owner(k, True):
            copy.wait_recv()
        for copy in to_owner(k):
            copy.wait_send()
    for copy in own_done:
        copy.wait()
    own_input.wait()
    far_input(core).wait_send()
    far_input(1 - core).wait_recv()
    halves(False).wait_send()
    to_core.wait_send()
    pl.when(ctx > 0)(to_past.wait_send)
    exchange.wait_send()
    for place in range(n_dp):
        for k in (1, 2, 3):
            attn_plane(k, place, 0).wait_send()
            attn_plane(k, place, 1).wait_send()

    def first_left(way):
        for far in range(last_dp, 0, -1):
            attn_hop(way, far, True).wait_send()
            for k in turn:
                first_hop(way, far, k).wait_send()

    def left(way, far):
        attn_hop(way, far, False).wait_send()
        for k in turn:
            next_hop(way, far, k).wait_send()

    for way in range(2):
        if line > 1:
            pl.when(is_first(way))(functools.partial(first_left, way))
        for far in range(line - 2, 0, -1):
            pl.when(not_first(way) & has_goal(way, far))(functools.partial(left, way, far))


def retreat_call(n_dp, line, owned_heads, *arrays):
    tokens, attn_full, keyval = arrays[4], arrays[11], arrays[15]
    mlp_grads = arrays[18]
    row_count, width = tokens.shape
    half = row_count // 2
    blocks = n_dp * 4
    owned, hid = mlp_grads.shape[1], mlp_grads.shape[2] // 3
    attn_cols = attn_full.shape[1]
    reach = keyval.shape[1]
    behind = reach - row_count
    f32, bf16 = jnp.float32, jnp.bfloat16
    vmem = pl.BlockSpec(memory_space=pltpu.VMEM)
    anywhere = pl.BlockSpec(memory_space=pl.ANY)
    dma = pltpu.SemaphoreType.DMA
    return pl.pallas_call(
        functools.partial(retreat_kernel, n_dp, line, owned_heads),
        out_shape=(
            jax.ShapeDtypeStruct((row_count, width), f32),
            jax.ShapeDtypeStruct((4, owned, 2 * hid), bf16),
            jax.ShapeDtypeStruct((4, owned, hid), bf16),
            jax.ShapeDtypeStruct((n_dp if line == 1 else 1, owned, attn_cols), bf16),
            jax.ShapeDtypeStruct((2, owned, HD), bf16),
        ),
        in_specs=[
            anywhere if index < 5 or 11 <= index <= 16 or index >= 18 else vmem
            for index in range(len(arrays))
        ],
        out_specs=(anywhere, anywhere, anywhere, vmem, anywhere),
        scratch_shapes=[
            pltpu.VMEM((half, width), f32),
            pltpu.VMEM((max(8 * (line - 1), 4), owned, 3 * hid), bf16),
            pltpu.VMEM((max(width, 3 * half), attn_cols), f32),
            pltpu.VMEM((blocks, owned, attn_cols), bf16),
            pltpu.VMEM((3 * n_dp, owned, attn_cols), bf16),
            pltpu.VMEM((n_dp, owned, attn_cols), bf16),
            pltpu.VMEM((2 * line, owned, attn_cols), bf16),
            pltpu.VMEM((row_count, width), bf16),
            pltpu.VMEM((row_count, 2 * HD), bf16),
            pltpu.VMEM((row_count, 2 * HD), f32),
            pltpu.VMEM((row_count, 3 * HD), bf16),
            pltpu.VMEM((2, reach, HD), f32),
            pltpu.VMEM((2, reach, HD), bf16),
            pltpu.VMEM((reach, HD), bf16),
            pltpu.VMEM((behind, HD), bf16),
            pltpu.VMEM((half, width), f32),
            pltpu.VMEM((half, width), bf16),
            pltpu.VMEM((half, width), bf16),
            pltpu.VMEM((128, width), f32),
            pltpu.VMEM((8, width), f32),
            dma((8 * line,)),
            dma((8 * line,)),
            dma((8,)),
            dma((8,)),
            dma((6 * n_dp,)),
            dma((6 * n_dp,)),
            dma((2 * line,)),
            dma((2 * line,)),
            dma((7,)),
            dma((7,)),
            dma((12,)),
            dma((16,)),
            pltpu.VMEM(mlp_grads.shape, bf16),
        ]
        + [
            pltpu.VMEM(arrays[index].shape, arrays[index].dtype)
            for index in (3, 4, 11, 12, 13, 14, 15, 16)
        ],
        compiler_params=pltpu.CompilerParams(
            collective_id=2, has_side_effects=True, vmem_limit_bytes=63 * 2**20
        ),
        cost_estimate=pl.CostEstimate(
            flops=10**10, bytes_accessed=40 * 2**20, transcendentals=2 * 10**6
        ),
        name="retreat",
    )(*arrays)


def update_call(wide, passed, small_grads, attn_grads, keyval_grads, gate_grads, down_grads, *states):
    owned = states[0].shape[0]
    cols = states[0].shape[1]
    blocks = down_grads.shape[0]

    def whole(array):
        return pl.BlockSpec(array.shape, lambda i: (0,) * array.ndim)

    def step(state, new, gradient, rate, decay=decay_rate):
        results = adam_step(
            state[0][...], gradient.astype(jnp.float32), state[1][...], state[2][...], rate, decay
        )
        for target, result in zip(new, results):
            target[...] = result

    def kernel(first_in, second_in, small_ref, attn_ref, keyval_ref, gate_ref, down_ref, *refs):
        olds, news, first_out, second_out = refs[:21], refs[21:42], *refs[42:]
        first_out[...] = first_in[...]
        second_out[...] = second_in[...]
        step(olds[9:12], news[9:12], gate_ref[...], D ** (-0.5))
        step(olds[12:15], news[12:15], down_ref[0], FF ** (-0.5))

        @pl.when(pl.program_id(0) == 0)
        def _():
            step(olds[0:3], news[0:3], attn_ref[0, :, 0:cols], D ** (-0.5))
            keyval = jnp.concatenate([keyval_ref[0], keyval_ref[1]], axis=1)
            step(olds[3:6], news[3:6], keyval, D ** (-0.5))
            output = attn_ref[0, :, cols + HD : 2 * cols + HD]
            step(olds[6:9], news[6:9], output, (HQ * HD) ** (-0.5))
            step(olds[15:18], news[15:18], small_ref[0:4], 0.5, 0.0)
            step(olds[18:21], news[18:21], small_ref[4:6, 0 : olds[18].shape[1]], 0.5, 0.0)

    gate_block = pl.BlockSpec((owned, 2, wide), lambda i: (0, 0, i))
    down_block = pl.BlockSpec((owned, wide), lambda i: (0, i))
    state_blocks = [whole(array) for array in states[:9]] + [gate_block] * 3 + [down_block] * 3
    state_blocks += [whole(array) for array in states[15:]]
    passed_blocks = [
        pl.BlockSpec((array.shape[0] // blocks, array.shape[1]), lambda i: (i, 0))
        for array in passed
    ]
    return pl.pallas_call(
        kernel,
        grid=(blocks,),
        in_specs=[
            *passed_blocks,
            whole(small_grads),
            whole(attn_grads),
            whole(keyval_grads),
            gate_block,
            pl.BlockSpec((1, owned, wide), lambda i: (i, 0, 0)),
        ]
        + state_blocks,
        out_specs=tuple(state_blocks + passed_blocks),
        out_shape=tuple(jax.ShapeDtypeStruct(array.shape, array.dtype) for array in states + passed),
        compiler_params=pltpu.CompilerParams(vmem_limit_bytes=63 * 2**20 + 900 * 2**10),
        name="update",
    )(*passed, small_grads, attn_grads, keyval_grads, gate_grads, down_grads, *states)


def on_device(
    tokens,
    out_cotangent,
    lengths,
    norm_gains,
    gain_first,
    gain_second,
    head_gains,
    head_first,
    head_second,
    query_weight,
    query_first,
    query_second,
    keyval_weight,
    keyval_first,
    keyval_second,
    output_weight,
    output_first,
    output_second,
    gate_up,
    gate_first,
    gate_second,
    down_weight,
    down_first,
    down_second,
):
    bf16, f32 = jnp.bfloat16, jnp.float32
    row_count = tokens.shape[0]
    owned = query_weight.shape[0]
    owned_heads = head_gains.shape[0]
    n_dp, n_ctx = lax.axis_size("dp"), lax.axis_size("ctx")
    half_ff = gate_up.shape[2]
    wide = -(-half_ff // (n_ctx * 128)) * 128
    behind = WIN
    line = n_dp if n_dp <= 4 else 1
    ctx_place = lax.axis_index("ctx")
    core_first = lax.axis_index("tensor") == 0
    score_scale = HD ** (-0.5)

    head_columns = jnp.pad(head_gains, ((0, owned - owned_heads), (0, 0)))
    small = jnp.concatenate([norm_gains, head_columns], axis=1).astype(bf16)
    attn_pack = jnp.concatenate(
        [
            query_weight.astype(bf16),
            half_of(keyval_weight, 1).astype(bf16),
            output_weight.astype(bf16),
            jnp.pad(small, ((0, 0), (0, 122))),
        ],
        axis=1,
    )
    cols = query_weight.shape[1]

    def in_parts(array):
        padded = jnp.pad(array.astype(bf16), ((0, 0), (0, n_ctx * wide - half_ff)))
        return padded.reshape(owned, n_ctx, wide)

    mlp_pack = jnp.concatenate(
        [in_parts(gate_up[:, 0]), in_parts(gate_up[:, 1]), in_parts(down_weight)], axis=2
    )
    mlp_pack = jnp.moveaxis(mlp_pack, 1, 0)

    exponent = np.arange(HD // 2, dtype=np.float32) * np.float32(2.0 / HD)
    inverse = jnp.power(jnp.float32(rope_base), -jnp.asarray(exponent))[None]
    (
        mlp_full,
        gain_rows,
        head_rows,
        log_total,
        query_cosine,
        query_sine,
        lowest,
        attn_full,
        normed_one,
        lin,
        query_rot,
        keyval_all,
        attended_low,
        branch_raw,
        middle,
        group_rows,
    ) = attend_call(n_dp, owned_heads, behind, tokens, lengths, inverse, attn_pack, mlp_pack)
    result, normed_two_grad, gain_three_part, mlp_grads, early = mlp_call(
        n_dp,
        line,
        group_rows,
        middle,
        out_cotangent,
        gain_rows,
        mlp_full.reshape(n_dp * n_ctx * owned, 3 * wide),
    )


    mlp_grads = mlp_grads.reshape(n_dp, n_ctx, owned, 3 * wide)
    if line == 1:
        mlp_grads = lax.psum_scatter(mlp_grads, "dp", scatter_dimension=0, tiled=True)
    mlp_grads = mlp_grads.reshape(line * n_ctx, owned, 3 * wide)
    input_grad, gate_arrived, down_arrived, attn_reduced, keyval_both = retreat_call(
        n_dp,
        line,
        owned_heads,
        normed_two_grad,
        middle,
        branch_raw,
        out_cotangent,
        tokens,
        query_cosine,
        query_sine,
        lowest,
        gain_rows,
        head_rows,
        gain_three_part,
        attn_full,
        normed_one,
        lin,
        query_rot,
        keyval_all,
        attended_low,
        log_total,
        mlp_grads,
        early.reshape(early.shape[0], -1, owned, wide),
    )
    if line == 1:
        attn_reduced = lax.psum_scatter(attn_reduced, "dp", scatter_dimension=0, tiled=True)
        keyval_half = attn_reduced[0, :, cols : cols + HD]
        first, second = jnp.where(core_first, 0, 1), jnp.where(core_first, 1, 0)
        keyval_both = jnp.stack([keyval_half, lax.ppermute(keyval_half, "tensor", [(0, 1), (1, 0)])])
        keyval_both = jnp.stack([keyval_both[first], keyval_both[second]])
    gate_reduced = gate_arrived.reshape(n_ctx, owned, 2, wide)
    gate_reduced = gate_reduced.transpose(1, 2, 0, 3).reshape(owned, 2, n_ctx * wide)
    gate_reduced = lax.optimization_barrier(gate_reduced)
    (
        query_new,
        query_first_new,
        query_second_new,
        keyval_new,
        keyval_first_new,
        keyval_second_new,
        output_new,
        output_first_new,
        output_second_new,
        gate_new,
        gate_first_new,
        gate_second_new,
        down_new,
        down_first_new,
        down_second_new,
        *gains_updated,
        result,
        input_grad,
    ) = update_call(
        wide,
        (result, input_grad),
        attn_reduced[0, :, 2 * cols + HD :].astype(f32).T,
        attn_reduced,
        keyval_both,
        gate_reduced,
        down_arrived,
        query_weight,
        query_first,
        query_second,
        keyval_weight,
        keyval_first,
        keyval_second,
        output_weight,
        output_first,
        output_second,
        gate_up,
        gate_first,
        gate_second,
        down_weight,
        down_first,
        down_second,
        norm_gains.T,
        gain_first.T,
        gain_second.T,
        head_gains.T,
        head_first.T,
        head_second.T,
    )
    (
        gains_new,
        gain_first_new,
        gain_second_new,
        heads_new,
        head_first_new,
        head_second_new,
    ) = (new.T for new in gains_updated)
    return (
        result,
        input_grad,
        gains_new,
        gain_first_new,
        gain_second_new,
        heads_new,
        head_first_new,
        head_second_new,
        query_new,
        query_first_new,
        query_second_new,
        keyval_new,
        keyval_first_new,
        keyval_second_new,
        output_new,
        output_first_new,
        output_second_new,
        gate_new,
        gate_first_new,
        gate_second_new,
        down_new,
        down_first_new,
        down_second_new,
    )


def solution(mesh):
    placed = (
        P(("dp", "ctx"), None),
        P(("dp", "ctx"), None),
        P("dp", None),
        P(("dp", "ctx"), None),
        P(("dp", "ctx"), None),
        P(("dp", "ctx"), None),
        P(("dp", "ctx"), None),
        P(("dp", "ctx"), None),
        P(("dp", "ctx"), None),
        P(("dp", "ctx"), "tensor"),
        P(("dp", "ctx"), "tensor"),
        P(("dp", "ctx"), "tensor"),
        P(("dp", "ctx"), None),
        P(("dp", "ctx"), None),
        P(("dp", "ctx"), None),
        P(("dp", "ctx"), "tensor"),
        P(("dp", "ctx"), "tensor"),
        P(("dp", "ctx"), "tensor"),
        P(("dp", "ctx"), None, "tensor"),
        P(("dp", "ctx"), None, "tensor"),
        P(("dp", "ctx"), None, "tensor"),
        P(("dp", "ctx"), "tensor"),
        P(("dp", "ctx"), "tensor"),
        P(("dp", "ctx"), "tensor"),
    )
    return jax.shard_map(
        on_device,
        mesh=mesh,
        in_specs=placed,
        out_specs=(
            P(("dp", "ctx"), None),
            P(("dp", "ctx"), None),
            P(("dp", "ctx"), None),
            P(("dp", "ctx"), None),
            P(("dp", "ctx"), None),
            P(("dp", "ctx"), None),
            P(("dp", "ctx"), None),
            P(("dp", "ctx"), None),
            P(("dp", "ctx"), "tensor"),
            P(("dp", "ctx"), "tensor"),
            P(("dp", "ctx"), "tensor"),
            P(("dp", "ctx"), None),
            P(("dp", "ctx"), None),
            P(("dp", "ctx"), None),
            P(("dp", "ctx"), "tensor"),
            P(("dp", "ctx"), "tensor"),
            P(("dp", "ctx"), "tensor"),
            P(("dp", "ctx"), None, "tensor"),
            P(("dp", "ctx"), None, "tensor"),
            P(("dp", "ctx"), None, "tensor"),
            P(("dp", "ctx"), "tensor"),
            P(("dp", "ctx"), "tensor"),
            P(("dp", "ctx"), "tensor"),
        ),
        check_vma=False,
    )
```
